128 devices in a mesh: dp: 8 (over y, core), fsdp: 16 (over z, x).
Axes of the slice: x: 4, y: 4, z: 4, core: 2. Of those that a mesh axis runs over, the one named last changes fastest.
Arguments:
- tokens: bfloat16 [16384, 1024], P(('dp', 'fsdp')), may hold values from -20 to 20, as said below
- segment: int32 [128, 128], P(('dp', 'fsdp')), may hold values from 0 to 1, as said below
- norm_gain: float32 [1024], P(('dp', 'fsdp')), may hold values from 0.5 to 1.5
- w_query: float32 [1024, 2048], P(('dp', 'fsdp')), may hold values from -0.1875 to 0.1875
- w_key: float32 [1024, 1024], P(('dp', 'fsdp')), may hold values from -0.1875 to 0.1875
- w_value: float32 [1024, 1024], P(('dp', 'fsdp')), may hold values from -0.1875 to 0.1875
- query_gain: float32 [128], P(('dp', 'fsdp')), may hold values from 0.1 to 1.9
- key_gain: float32 [128], P(('dp', 'fsdp')), may hold values from 0.1 to 1.9
- w_out: float32 [2048, 1024], P(('dp', 'fsdp')), may hold values from -0.75 to 0.75
- mlp_gain: float32 [1024], P(('dp', 'fsdp')), may hold values from 0.5 to 1.5
- w_gate: float32 [1024, 3072], P(('dp', 'fsdp')), may hold values from -0.1875 to 0.1875
- w_up: float32 [1024, 3072], P(('dp', 'fsdp')), may hold values from -0.1875 to 0.1875
- w_down: float32 [3072, 1024], P(('dp', 'fsdp')), may hold values from -0.21875 to 0.21875
- cotangent: bfloat16 [16384, 1024], P(('dp', 'fsdp')), may hold values from -6 to 6
Outputs:
- layer_out: bfloat16 [16384, 1024], P(('dp', 'fsdp'))
- input_grad: float32 [16384, 1024], P(('dp', 'fsdp'))
- grad_norm_gain: float32 [1024], P(('dp', 'fsdp'))
- grad_w_query: float32 [1024, 2048], P(('dp', 'fsdp'))
- grad_w_key: float32 [1024, 1024], P(('dp', 'fsdp'))
- grad_w_value: float32 [1024, 1024], P(('dp', 'fsdp'))
- grad_query_gain: float32 [128], P(('dp', 'fsdp'))
- grad_key_gain: float32 [128], P(('dp', 'fsdp'))
- grad_w_out: float32 [2048, 1024], P(('dp', 'fsdp'))
- grad_mlp_gain: float32 [1024], P(('dp', 'fsdp'))
- grad_w_gate: float32 [1024, 3072], P(('dp', 'fsdp'))
- grad_w_up: float32 [1024, 3072], P(('dp', 'fsdp'))
- grad_w_down: float32 [3072, 1024], P(('dp', 'fsdp'))
The draws below stay inside these ranges and needn't reach their ends.
Inputs may be any that keep to these rules, and one draw needn't show every extreme that they name: `segment`: in each row (one device's tokens) the ids never fall; a row holds one or two sequences, each of 48 to 128 tokens, and some row holds one sequence of exactly 128. `tokens`: rows have different scales.
All inputs are finite; a program needn't handle non-finite values.
Results may differ from the reference program's by a relative error of at most 0.033.
Values may be sent and summed in bfloat16 or wider, within the bound.
A program may use at most 192 MiB of HBM per device.

```python
import math
import jax
import jax.numpy as jnp
from jax import lax

D = 1024
HQ = 16
HK = 8
HD = 128
FF = 3072
TOK_DEV = 128
MINLEN = 48
QW = 2048
KW = 1024
TOKENS = 16384


def draw_tokens(key, part):
    first_key, second_key = jax.random.split(key)
    base_values = jnp.clip(jax.random.normal(first_key, (TOKENS, D), jnp.float32), -4.0, 4.0)
    row_scale = jnp.exp(jax.random.uniform(second_key, (TOKENS, 1), jnp.float32, math.log(0.5), math.log(5.0)))
    return (base_values * row_scale).astype(jnp.bfloat16)


def draw_segment(key, part):
    row_total = TOKENS // TOK_DEV
    cut_key, whole_key = jax.random.split(jax.random.fold_in(key, 17))
    cuts = jax.random.randint(cut_key, (row_total,), MINLEN, TOK_DEV - MINLEN + 1)
    chosen = jax.random.randint(whole_key, (), 0, row_total)
    cuts = jnp.where(jnp.arange(row_total, dtype=jnp.int32) == chosen, TOK_DEV, cuts)
    columns = jnp.arange(TOK_DEV, dtype=jnp.int32)
    return (columns[None, :] >= cuts[:, None]).astype(jnp.int32)


def shard_levels(rng, extent, shards, low, largest):
    gain, own = 1.0, jax.random.fold_in(rng, 6)
    for dim, shards_of in shards:
        heights = jnp.exp(jax.random.uniform(jax.random.fold_in(own, dim), (shards_of,), jnp.float32, low / len(shards), largest / len(shards)))
        gain = gain * jnp.repeat(heights, extent[dim] // shards_of).reshape([-1 if axis == dim else 1 for axis in range(len(extent))])
    return gain


def bell_draw(own_key, extent, spread, reach, cuts=(), held_as=jnp.bfloat16):
    values = jax.random.normal(own_key, extent, jnp.float32) * spread
    if len(cuts) > 0:
        values = shard_levels(own_key, extent, cuts, -0.22, 0.18) * values
    return jnp.clip(values, min=-reach, max=reach).astype(held_as)


def setup_inputs(seed: int = 0) -> dict:
    keys = jax.random.split(jax.random.key(seed), 15)
    tokens = draw_tokens(jax.random.fold_in(keys[14], 71), 0)
    segment = draw_segment(jax.random.fold_in(keys[14], 71), 0)
    norm_gain = jnp.clip(1.0 + 0.1 * jax.random.normal(keys[2], (D,), jnp.float32), 0.5, 1.5)
    w_query = bell_draw(keys[3], (D, QW), D ** -0.5, 0.1875, ((0, 128),), jnp.float32)
    w_key = bell_draw(keys[4], (D, KW), D ** -0.5, 0.1875, ((0, 128),), jnp.float32)
    w_value = bell_draw(keys[5], (D, KW), D ** -0.5, 0.1875, ((0, 128),), jnp.float32)
    query_gain = jnp.clip(1.0 + 0.18 * jax.random.normal(keys[6], (HD,), jnp.float32), 0.1, 1.9)
    key_gain = jnp.clip(1.0 + 0.18 * jax.random.normal(keys[7], (HD,), jnp.float32), 0.1, 1.9)
    w_out = bell_draw(keys[8], (QW, D), (QW // 32) ** -0.5, 0.75, ((0, 128),), jnp.float32)
    mlp_gain = jnp.clip(1.0 + 0.1 * jax.random.normal(keys[9], (D,), jnp.float32), 0.5, 1.5)
    w_gate = bell_draw(keys[10], (D, FF), D ** -0.5, 0.1875, ((0, 128),), jnp.float32)
    w_up = bell_draw(keys[11], (D, FF), D ** -0.5, 0.1875, ((0, 128),), jnp.float32)
    w_down = bell_draw(keys[12], (FF, D), (FF // 4) ** -0.5, 0.21875, ((0, 128),), jnp.float32)
    cotangent = bell_draw(keys[13], (TOKENS, D), 1.0, 6.0, ((0, 128),))
    return dict(tokens=tokens, segment=segment, norm_gain=norm_gain, w_query=w_query, w_key=w_key, w_value=w_value, query_gain=query_gain, key_gain=key_gain, w_out=w_out, mlp_gain=mlp_gain, w_gate=w_gate, w_up=w_up, w_down=w_down, cotangent=cotangent)


EPS = 1e-06
THETA = 1000000.0
PRECISE = lax.Precision.HIGHEST

@jax.custom_vjp
def low(v):
    return lax.optimization_barrier(v.astype(jnp.bfloat16)).astype(jnp.float32)

@jax.custom_vjp
def low_back(v):
    return v

def low_keep(v):
    return (low(v), None)

def low_pass(kept, grad):
    return (grad,)

def back_keep(v):
    return (v, None)

def back_low(kept, grad):
    return (low(grad),)
low.defvjp(low_keep, low_pass)
low_back.defvjp(back_keep, back_low)

def low_both(value):
    return low_back(low(value))

def product(left, right):
    return jnp.dot(left, right, precision=PRECISE, preferred_element_type=jnp.float32)

def rotary(vector, position):
    half_dim = vector.shape[-1] // 2
    inv_freq = THETA ** (-jnp.arange(half_dim, dtype=jnp.float32) * 2.0 / vector.shape[-1])
    angles = position.astype(jnp.float32)[:, None] * inv_freq[None, :]
    cos_part = jnp.cos(angles)[:, None, :]
    sin_part = jnp.sin(angles)[:, None, :]
    first_half = vector[..., :half_dim]
    second_half = vector[..., half_dim:]
    return jnp.concatenate([first_half * cos_part - second_half * sin_part, second_half * cos_part + first_half * sin_part], axis=-1)

def layout(seg_ids):
    row_index = jnp.arange(seg_ids.shape[0], dtype=jnp.int32)
    same_seq = seg_ids[:, None] == seg_ids[None, :]
    allowed = same_seq & (row_index[None, :] <= row_index[:, None])
    position = lax.optimization_barrier(jnp.sum((same_seq & (row_index[None, :] < row_index[:, None])).astype(jnp.int32), axis=1))
    return (allowed, position)

def inverse_rms(vector):
    return lax.rsqrt(lax.optimization_barrier(jnp.mean(vector * vector, axis=-1, keepdims=True)) + EPS)

def block_layer(x_block, seg_ids, sent_weights):
    gain_in, query_w, key_w, value_w, gain_query, gain_key, out_w, gain_mid, gate_w, up_w, down_w = sent_weights
    row_count = x_block.shape[0]
    allowed, position = layout(seg_ids)
    normed = low(x_block * inverse_rms(x_block) * gain_in)
    q_raw = low_back(product(normed, query_w)).reshape(row_count, HQ, HD)
    k_raw = low_back(product(normed, key_w)).reshape(row_count, HK, HD)
    values = low_both(product(normed, value_w)).reshape(row_count, HK, HD)
    q_rot = low(rotary(q_raw * inverse_rms(q_raw) * gain_query, position))
    k_rot = low(rotary(k_raw * inverse_rms(k_raw) * gain_key, position))
    q_group = q_rot.reshape(row_count, HK, HQ // HK, HD)
    scores = low_back(jnp.einsum('qhgd,khd->hgqk', q_group, k_rot, precision=PRECISE) * HD ** (-0.5))
    masked = jnp.where(allowed[None, None], scores, -1e+30)
    exp_terms = jnp.exp(masked - lax.optimization_barrier(jnp.max(masked, axis=-1, keepdims=True)))
    prob_low = low(exp_terms / lax.optimization_barrier(jnp.sum(exp_terms, axis=-1, keepdims=True)))
    attended = low_both(jnp.einsum('hgqk,khd->qhgd', prob_low, values, precision=PRECISE).reshape(row_count, HQ * HD))
    hidden_res = x_block + low_back(product(attended, out_w))
    mid_low = low(hidden_res * inverse_rms(hidden_res) * gain_mid)
    gate_proj = low_back(product(mid_low, gate_w))
    up_proj = low_back(product(mid_low, up_w))
    mixed = low(jax.nn.silu(gate_proj) * up_proj)
    return hidden_res + product(mixed, down_w)

def reference(tokens, segment, norm_gain, w_query, w_key, w_value, query_gain, key_gain, w_out, mlp_gain, w_gate, w_up, w_down, cotangent):
    x_float = tokens.astype(jnp.float32)

    def forward(x_in, gain_in, query_w, key_w, value_w, gain_query, gain_key, out_w, gain_mid, gate_w, up_w, down_w):
        sent_weights = tuple((low(weight) for weight in (gain_in, query_w, key_w, value_w, gain_query, gain_key, out_w, gain_mid, gate_w, up_w, down_w)))

        def one_block(pair_item):
            return block_layer(pair_item[0], pair_item[1], sent_weights)
        token_blocks = x_in.reshape(segment.shape[0], TOK_DEV, D)
        result_rows = lax.map(jax.checkpoint(one_block), (token_blocks, segment))
        return result_rows.reshape(x_in.shape[0], D)
    layer_rows, pullback = jax.vjp(forward, x_float, norm_gain, w_query, w_key, w_value, query_gain, key_gain, w_out, mlp_gain, w_gate, w_up, w_down)
    gradients = pullback(cotangent.astype(jnp.float32))
    return (layer_rows.astype(jnp.bfloat16), gradients[0], gradients[1], gradients[2], gradients[3], gradients[4], gradients[5], gradients[6], gradients[7], gradients[8], gradients[9], gradients[10], gradients[11])
```

```python
import functools

import jax
import jax.numpy as jnp
from jax import lax
from jax.experimental import pallas as pl
from jax.experimental.pallas import tpu as pltpu
from jax.sharding import PartitionSpec as P

HQ = 16
HK = 8
HD = 128
EPS = 1e-06
THETA = 1000000.0

bf16 = jnp.bfloat16
f32 = jnp.float32
MESH = pl.DeviceIdType.MESH

ARRAYS = {
    "q": ("n", 8, 1024),
    "g": ("n", 8, 1536),
    "k": ("n", 8, 512),
    "v": ("n", 8, 512),
    "u": ("n", 8, 1536),
    "o": ("c", 16, 1024),
    "d": ("c", 24, 1024),
    "e": ("n", 8, 128),
}
ORDER = {
    "q": "xyz",
    "g": "xyz",
    "k": "yzx",
    "v": "yzx",
    "u": "yzx",
    "o": "zxy",
    "d": "zxy",
    "e": "zxy",
}
NAMES = tuple(ARRAYS)


def full_shape(name):
    kind, rows, cols = ARRAYS[name]
    if kind == "n":
        return (4, 2, 4, 4, 8, cols)
    return (4, 4, 4, rows // 8, 8, cols)


def coords():
    dp = lax.axis_index("dp")
    fs = lax.axis_index("fsdp")
    return {"y": dp // 2, "c": lax.rem(dp, 2), "z": fs // 4, "x": lax.rem(fs, 4)}


def device(pos, axis=None, step=0):
    pos = dict(pos)
    if axis == "c":
        pos["c"] = 1 - pos["c"]
    elif axis is not None:
        pos[axis] = lax.rem(pos[axis] + step + 4, 4)
    return (pos["y"] * 2 + pos["c"], pos["z"] * 4 + pos["x"])


def greet(pos):
    barrier = pltpu.get_barrier_semaphore()
    others = [device(pos, "c")]
    for axis in "xyz":
        others += [device(pos, axis, 1), device(pos, axis, -1)]
    for other in others:
        pl.semaphore_signal(barrier, inc=1, device_id=other, device_id_type=MESH)
    pl.semaphore_wait(barrier, len(others))


def block(ref, name, at, half=None):
    kind, rows, cols = ARRAYS[name]
    part = {axis: pl.ds(at[axis], 1) if axis in at else slice(None) for axis in "yzx"}
    if kind == "n":
        core = slice(None) if half is None else pl.ds(half, 1)
        return ref.at[part["y"], core, part["z"], part["x"]]
    if half is None:
        return ref.at[part["y"], part["z"], part["x"]]
    lanes = pl.ds(half * (cols // 2), cols // 2)
    return ref.at[part["y"], part["z"], part["x"], :, :, lanes]


def gather_kernel(*refs):
    n = len(NAMES)
    own = dict(zip(NAMES, refs[:n]))
    x_in, cot_in, seg_in = refs[n : n + 3]
    full = dict(zip(NAMES, refs[n + 3 : 2 * n + 3]))
    x_all, cot_all, seg_all = refs[2 * n + 3 : 2 * n + 6]
    send, recv, pair_send, pair_recv, local = refs[2 * n + 6 :]
    pos = coords()
    me = pos["c"]
    greet(pos)

    def remote(src, dst, sems, index, target):
        return pltpu.make_async_remote_copy(
            src_ref=src,
            dst_ref=dst,
            send_sem=sems[0].at[index],
            recv_sem=sems[1].at[index],
            device_id=target,
            device_id_type=MESH,
        )

    sibling = device(pos, "c")
    pair_sems = (pair_send, pair_recv)
    pair, kept = {}, {}
    for index, name in enumerate(NAMES):
        kind = ARRAYS[name][0]
        if kind == "n":
            mine = full[name].at[pos["y"], me, pos["z"], pos["x"]]
            kept[name] = pltpu.make_async_copy(own[name].at[me], mine, local.at[index])
            pair[name] = remote(own[name].at[1 - me], mine, pair_sems, index, sibling)
            pair[name].start()
        else:
            mine = full[name].at[pos["y"], pos["z"], pos["x"]]
            kept[name] = pltpu.make_async_copy(own[name], mine, local.at[index])
        kept[name].start()
    late = []
    for index, (src, dst) in enumerate(((x_in, x_all), (cot_in, cot_all), (seg_in, seg_all))):
        copy = remote(src, dst.at[me], pair_sems, n + index, sibling)
        copy.start()
        late.append(copy)
        copy = pltpu.make_async_copy(src, dst.at[me], local.at[n + index])
        copy.start()
        late.append(copy)
    for name in NAMES:
        kept[name].wait()
        if name in pair:
            pair[name].wait()

    sems = (send, recv)
    for phase in range(3):
        copies = {}
        for name in NAMES:
            index = NAMES.index(name)
            axis = ORDER[name][phase]
            at = {a: pos[a] for a in ORDER[name][phase:]}
            src = block(full[name], name, at)
            up = remote(src, src, sems, (index, phase, 0), device(pos, axis, 1))
            down = remote(src, src, sems, (index, phase, 1), device(pos, axis, -1))
            up.start()
            down.start()
            copies[name] = [up, down]
        for name in NAMES:
            index = NAMES.index(name)
            axis = ORDER[name][phase]
            at = {a: pos[a] for a in ORDER[name][phase:]}
            up, down = copies[name]
            up.wait_recv()
            src = block(full[name], name, {**at, axis: lax.rem(pos[axis] + 3, 4)}, 0)
            on_up = remote(src, src, sems, (index, phase, 2), device(pos, axis, 1))
            on_up.start()
            down.wait_recv()
            src = block(full[name], name, {**at, axis: lax.rem(pos[axis] + 1, 4)}, 1)
            on_down = remote(src, src, sems, (index, phase, 3), device(pos, axis, -1))
            on_down.start()
            copies[name] += [on_up, on_down]
        for name in NAMES:
            up, down, on_up, on_down = copies[name]
            on_up.wait_recv()
            on_down.wait_recv()
            for copy in copies[name]:
                copy.wait_send()
    for copy in late:
        copy.wait()


def gather(own, x, cot, seg):
    n = len(NAMES)
    shapes = [jax.ShapeDtypeStruct(full_shape(name), bf16) for name in NAMES]
    shapes += [jax.ShapeDtypeStruct((2,) + a.shape, a.dtype) for a in (x, cot, seg)]
    outs = pl.pallas_call(
        gather_kernel,
        out_shape=shapes,
        in_specs=[pl.BlockSpec(memory_space=pl.ANY)] * (n + 3),
        out_specs=[pl.BlockSpec(memory_space=pl.ANY)] * (n + 3),
        scratch_shapes=[
            pltpu.SemaphoreType.DMA((n, 3, 4)),
            pltpu.SemaphoreType.DMA((n, 3, 4)),
            pltpu.SemaphoreType.DMA((n + 3,)),
            pltpu.SemaphoreType.DMA((n + 3,)),
            pltpu.SemaphoreType.DMA((n + 3,)),
        ],
        compiler_params=pltpu.CompilerParams(collective_id=1, has_side_effects=True),
        name="gather_weights",
    )(*[own[name] for name in NAMES], x, cot, seg)
    return dict(zip(NAMES, outs[:n])), outs[n:]


def merged(name, fixed):
    shape = list(full_shape(name))
    kind = ARRAYS[name][0]
    places = {"y": 0, "z": 2, "x": 3} if kind == "n" else {"y": 0, "z": 1, "x": 2}
    for axis in fixed:
        shape[places[axis]] = 1
    return tuple(shape)


def halved(name, shape):
    kind = ARRAYS[name][0]
    shape = list(shape)
    shape[1 if kind == "n" else -1] //= 2
    return tuple(shape)


def pieces(shape):
    return shape[:-2]


def add_into(dst, sources, shape):
    lead = pieces(shape)
    count = 1
    for extent in lead:
        count *= extent

    def step(i, carry):
        index = []
        rest = i
        for extent in reversed(lead):
            index.append(lax.rem(rest, extent))
            rest = rest // extent
        index = tuple(reversed(index))
        total = sources[0][index].astype(f32)
        for source in sources[1:]:
            total = total + source[index].astype(f32)
        dst[index] = total.astype(dst.dtype)
        return carry

    lax.fori_loop(0, count, step, 0)


def sum_kernel(*refs):
    n = len(NAMES)
    part = dict(zip(NAMES, refs[:n]))
    outs = dict(zip(NAMES, refs[n : 2 * n]))
    scratch = list(refs[2 * n :])
    got, state = {}, {}
    for name in NAMES:
        for phase in range(3):
            got[name, phase] = scratch[:4]
            state[name, phase] = scratch[4]
            scratch = scratch[5:]
    send, recv, pair_send, pair_recv = scratch
    pos = coords()
    me = pos["c"]
    greet(pos)

    def remote(src, dst, sems, index, target):
        return pltpu.make_async_remote_copy(
            src_ref=src,
            dst_ref=dst,
            send_sem=sems[0].at[index],
            recv_sem=sems[1].at[index],
            device_id=target,
            device_id_type=MESH,
        )

    sems = (send, recv)
    current = dict(part)
    for phase in range(3):
        copies = {}
        for name in NAMES:
            index = NAMES.index(name)
            order = ORDER[name][::-1]
            axis = order[phase]
            up, down = device(pos, axis, 1), device(pos, axis, -1)
            ahead, behind = lax.rem(pos[axis] + 1, 4), lax.rem(pos[axis] + 3, 4)
            opposite = lax.rem(pos[axis] + 2, 4)
            cur = current[name]
            far_up, far_down, near_up, near_down = got[name, phase]
            copies[name] = [
                remote(block(cur, name, {axis: opposite}, 0), far_up, sems, (index, phase, 0), up),
                remote(block(cur, name, {axis: opposite}, 1), far_down, sems, (index, phase, 1), down),
                remote(
                    block(cur, name, {axis: ahead}, 1),
                    half_of(near_up, name, 1),
                    sems,
                    (index, phase, 2),
                    up,
                ),
                remote(
                    block(cur, name, {axis: behind}, 0),
                    half_of(near_down, name, 0),
                    sems,
                    (index, phase, 3),
                    down,
                ),
            ]
            for copy in copies[name]:
                copy.start()
        for name in NAMES:
            index = NAMES.index(name)
            order = ORDER[name][::-1]
            axis = order[phase]
            up, down = device(pos, axis, 1), device(pos, axis, -1)
            ahead, behind = lax.rem(pos[axis] + 1, 4), lax.rem(pos[axis] + 3, 4)
            cur = current[name]
            far_up, far_down, near_up, near_down = got[name, phase]
            shape = halved(name, merged(name, order[: phase + 1]))
            copies[name][0].wait_recv()
            add_into(far_up, [far_up, block(cur, name, {axis: ahead}, 0)], shape)
            copy = remote(far_up, half_of(near_up, name, 0), sems, (index, phase, 4), up)
            copy.start()
            copies[name].append(copy)
            copies[name][1].wait_recv()
            add_into(far_down, [far_down, block(cur, name, {axis: behind}, 1)], shape)
            copy = remote(far_down, half_of(near_down, name, 1), sems, (index, phase, 5), down)
            copy.start()
            copies[name].append(copy)
        for name in NAMES:
            order = ORDER[name][::-1]
            axis = order[phase]
            cur = current[name]
            near_up, near_down = got[name, phase][2:]
            for copy in copies[name][2:]:
                copy.wait_recv()
            shape = merged(name, order[: phase + 1])
            add_into(state[name, phase], [near_up, near_down, block(cur, name, {axis: pos[axis]})], shape)
            for copy in copies[name]:
                copy.wait_send()
            current[name] = state[name, phase]
    sibling = device(pos, "c")
    pairs = []
    for index, name in enumerate(NAMES):
        cur = current[name]
        if ARRAYS[name][0] == "n":
            copy = remote(
                cur.at[0, 1 - me, 0, 0], outs[name].at[me], (pair_send, pair_recv), index, sibling
            )
            copy.start()
            pairs.append(copy)
            outs[name][me] = cur[0, me, 0, 0]
        else:
            outs[name][...] = cur[0, 0, 0]
    for copy in pairs:
        copy.wait()


def half_of(ref, name, half):
    kind, rows, cols = ARRAYS[name]
    if kind == "n":
        return ref.at[:, pl.ds(half, 1)]
    return ref.at[:, :, :, :, :, pl.ds(half * (cols // 2), cols // 2)]


def reduce_all(part):
    n = len(NAMES)
    scratch = []
    for name in NAMES:
        order = ORDER[name][::-1]
        for phase in range(3):
            shape = merged(name, order[: phase + 1])
            half = halved(name, shape)
            scratch += [pltpu.VMEM(half, bf16), pltpu.VMEM(half, bf16)]
            scratch += [pltpu.VMEM(shape, bf16), pltpu.VMEM(shape, bf16)]
            scratch += [pltpu.VMEM(shape, f32 if phase == 2 else bf16)]
    shapes = []
    for name in NAMES:
        kind, rows, cols = ARRAYS[name]
        shape = (2, 8, cols) if kind == "n" else (rows // 8, 8, cols)
        shapes.append(jax.ShapeDtypeStruct(shape, f32))
    outs = pl.pallas_call(
        sum_kernel,
        out_shape=shapes,
        in_specs=[pl.BlockSpec(memory_space=pltpu.VMEM)] * n,
        out_specs=[pl.BlockSpec(memory_space=pltpu.VMEM)] * n,
        scratch_shapes=scratch
        + [
            pltpu.SemaphoreType.DMA((n, 3, 6)),
            pltpu.SemaphoreType.DMA((n, 3, 6)),
            pltpu.SemaphoreType.DMA((n,)),
            pltpu.SemaphoreType.DMA((n,)),
        ],
        compiler_params=pltpu.CompilerParams(
            collective_id=2, has_side_effects=True, vmem_limit_bytes=60 << 20
        ),
        name="sum_gradients",
    )(*[part[name] for name in NAMES])
    return dict(zip(NAMES, outs))


def contract(left, right, left_dim, right_dim):
    return lax.dot_general(
        left, right, (((left_dim,), (right_dim,)), ((), ())), preferred_element_type=f32
    )


def inverse_rms(vector):
    return lax.rsqrt(jnp.mean(vector * vector, axis=-1, keepdims=True) + EPS)


def norm_backward(grad_in, unit_vec, inverse, gain_vec):
    scaled = grad_in * gain_vec
    return inverse * (scaled - unit_vec * jnp.mean(scaled * unit_vec, axis=-1, keepdims=True))


def rotate(vector, cos_part, sin_part):
    first, second = vector[..., : HD // 2], vector[..., HD // 2 :]
    return jnp.concatenate(
        [first * cos_part - second * sin_part, second * cos_part + first * sin_part], axis=-1
    )


def unrotate(vector, cos_part, sin_part):
    return rotate(vector, cos_part, -sin_part)


def from_sibling(value):
    size = lax.axis_size("fsdp")
    total = lax.axis_size("dp") * size
    pairs = []
    for i in range(total):
        dp, fs = i // size, i % size
        pairs.append((i, (dp ^ 1) * size + fs))
    return lax.ppermute(value, ("dp", "fsdp"), pairs)


def split_columns(weight, width):
    rows, cols = weight.shape
    halves = weight.astype(bf16).reshape(rows, cols // (2 * width), 2, width)
    return halves.transpose(2, 0, 1, 3).reshape(2, rows, cols // 2)


def join_columns(halves, width):
    _, rows, cols = halves.shape
    blocks = halves.reshape(2, rows, cols // width, width)
    return blocks.transpose(1, 2, 0, 3).reshape(rows, 2 * cols)


def body(
    tokens, segment, norm_gain, w_query, w_key, w_value, query_gain, key_gain, w_out, mlp_gain,
    w_gate, w_up, w_down, cotangent,
):
    core = lax.rem(lax.axis_index("dp"), 2)
    first_row = jnp.arange(8)[:, None] == 0
    gains = jnp.concatenate(
        [
            norm_gain[:, None],
            mlp_gain[:, None],
            jnp.where(first_row, query_gain[0], 0.0),
            jnp.where(first_row, key_gain[0], 0.0),
            jnp.zeros((8, 124), f32),
        ],
        axis=1,
    ).astype(bf16)
    own = {
        "q": split_columns(w_query, 256),
        "g": split_columns(w_gate, 384),
        "k": split_columns(w_key, 128),
        "v": split_columns(w_value, 128),
        "u": split_columns(w_up, 384),
        "o": w_out.astype(bf16).reshape(2, 8, 1024),
        "d": w_down.astype(bf16).reshape(3, 8, 1024),
        "e": jnp.stack([gains, gains]),
    }
    seg_rows = jnp.broadcast_to(segment, (8, 128))
    full, (x_pair, cot_pair, seg_pair) = gather(own, tokens, cotangent, seg_rows)
    wq = full["q"].reshape(1024, 1024)
    wk = full["k"].reshape(1024, 512)
    wv = full["v"].reshape(1024, 512)
    wg = full["g"].reshape(1024, 1536)
    wu = full["u"].reshape(1024, 1536)
    wo = full["o"].reshape(1024, 1024)
    wd = full["d"].reshape(1536, 1024)
    columns = full["e"].reshape(1024, 128)[:, :4].astype(f32).T
    gain_in, gain_mid = columns[0], columns[1]
    gain_query, gain_key = columns[2].reshape(128, 8)[:, 0], columns[3].reshape(128, 8)[:, 0]

    rows = 256
    seg_ids = seg_pair[:, 0, :]
    index = jnp.arange(128, dtype=jnp.int32)
    same = seg_ids[:, :, None] == seg_ids[:, None, :]
    allowed = same & (index[None, :] <= index[:, None])[None]
    position = jnp.sum((same & (index[None, :] < index[:, None])[None]).astype(jnp.int32), axis=2)
    inv_freq = THETA ** (-jnp.arange(HD // 2, dtype=f32) * 2.0 / HD)
    angles = position.reshape(rows).astype(f32)[:, None] * inv_freq[None, :]
    cos_part = jnp.cos(angles)[:, None, :]
    sin_part = jnp.sin(angles)[:, None, :]
    scale = HD ** (-0.5)
    nq, nk, group = HQ // 2, HK // 2, HQ // HK

    x = x_pair.reshape(rows, 1024).astype(f32)
    cot = cot_pair.reshape(rows, 1024)
    inv_in = inverse_rms(x)
    unit_in = x * inv_in
    normed = (unit_in * gain_in).astype(bf16)
    q_raw = jnp.dot(normed, wq, preferred_element_type=f32).reshape(rows, nq, HD)
    k_raw = jnp.dot(normed, wk, preferred_element_type=f32).reshape(rows, nk, HD)
    values = jnp.dot(normed, wv, preferred_element_type=f32).astype(bf16).reshape(2, 128, nk, HD)
    inv_q = inverse_rms(q_raw)
    unit_q = q_raw * inv_q
    inv_k = inverse_rms(k_raw)
    unit_k = k_raw * inv_k
    q_rot = rotate(unit_q * gain_query, cos_part, sin_part).astype(bf16)
    k_rot = rotate(unit_k * gain_key, cos_part, sin_part).astype(bf16).reshape(2, 128, nk, HD)
    q_group = q_rot.reshape(2, 128, nk, group, HD)
    scores = jnp.einsum("bqhgd,bkhd->bhgqk", q_group, k_rot, preferred_element_type=f32) * scale
    masked = jnp.where(allowed[:, None, None], scores, -1e30)
    exp_terms = jnp.exp(masked - jnp.max(masked, axis=-1, keepdims=True))
    prob_full = exp_terms / jnp.sum(exp_terms, axis=-1, keepdims=True)
    prob_low = prob_full.astype(bf16)
    attended = (
        jnp.einsum("bhgqk,bkhd->bqhgd", prob_low, values, preferred_element_type=f32)
        .astype(bf16)
        .reshape(rows, nq * HD)
    )
    out_part = jnp.dot(attended, wo, preferred_element_type=f32)
    hidden = x + (out_part + from_sibling(out_part))
    inv_mid = inverse_rms(hidden)
    unit_mid = hidden * inv_mid
    mid_low = (unit_mid * gain_mid).astype(bf16)
    gate = jnp.dot(mid_low, wg, preferred_element_type=f32)
    up = jnp.dot(mid_low, wu, preferred_element_type=f32)
    sig = jax.nn.sigmoid(gate)
    act = gate * sig
    mixed = (act * up).astype(bf16)
    down_part = jnp.dot(mixed, wd, preferred_element_type=f32).reshape(2, 128, 1024)
    hidden_pair = hidden.reshape(2, 128, 1024)
    down_own = lax.dynamic_index_in_dim(down_part, core, 0, False)
    down_other = from_sibling(lax.dynamic_index_in_dim(down_part, 1 - core, 0, False))
    layer_out = (
        lax.dynamic_index_in_dim(hidden_pair, core, 0, False) + (down_own + down_other)
    ).astype(bf16)

    grad = {}
    grad["d"] = contract(mixed, cot, 0, 0)
    d_mixed = contract(cot, wd, 1, 1)
    d_gate = (d_mixed * up * sig * (1.0 + gate * (1.0 - sig))).astype(bf16)
    d_up = (d_mixed * act).astype(bf16)
    grad["g"] = contract(mid_low, d_gate, 0, 0)
    grad["u"] = contract(mid_low, d_up, 0, 0)
    mid_part = contract(d_gate, wg, 1, 1) + contract(d_up, wu, 1, 1)
    grad_mlp_gain = jnp.sum(mid_part * unit_mid, axis=0)
    d_mid = mid_part + from_sibling(mid_part)
    d_res = cot.astype(f32) + norm_backward(d_mid, unit_mid, inv_mid, gain_mid)
    d_res_low = d_res.astype(bf16)
    grad["o"] = contract(attended, d_res_low, 0, 0)
    d_attn = contract(d_res_low, wo, 1, 1).astype(bf16).reshape(2, 128, nk, group, HD)
    d_probs = jnp.einsum("bqhgd,bkhd->bhgqk", d_attn, values, preferred_element_type=f32)
    d_values = (
        jnp.einsum("bhgqk,bqhgd->bkhd", prob_low, d_attn, preferred_element_type=f32)
        .astype(bf16)
        .reshape(rows, nk * HD)
    )
    d_scores = (
        prob_full * (d_probs - jnp.sum(d_probs * prob_full, axis=-1, keepdims=True))
    ).astype(bf16)
    d_qrot = (
        jnp.einsum("bhgqk,bkhd->bqhgd", d_scores, k_rot, preferred_element_type=f32) * scale
    ).reshape(rows, nq, HD)
    d_krot = (
        jnp.einsum("bhgqk,bqhgd->bkhd", d_scores, q_group, preferred_element_type=f32) * scale
    ).reshape(rows, nk, HD)
    d_qunit = unrotate(d_qrot, cos_part, sin_part)
    d_kunit = unrotate(d_krot, cos_part, sin_part)
    grad_query_gain = jnp.sum(d_qunit * unit_q, axis=(0, 1))
    grad_key_gain = jnp.sum(d_kunit * unit_k, axis=(0, 1))
    d_qraw = norm_backward(d_qunit, unit_q, inv_q, gain_query).astype(bf16).reshape(rows, nq * HD)
    d_kraw = norm_backward(d_kunit, unit_k, inv_k, gain_key).astype(bf16).reshape(rows, nk * HD)
    grad["q"] = contract(normed, d_qraw, 0, 0)
    grad["k"] = contract(normed, d_kraw, 0, 0)
    grad["v"] = contract(normed, d_values, 0, 0)
    in_part = contract(d_qraw, wq, 1, 1) + contract(d_kraw, wk, 1, 1) + contract(d_values, wv, 1, 1)
    grad_norm_gain = jnp.sum(in_part * unit_in, axis=0)
    in_pair = in_part.reshape(2, 128, 1024)

    def mine(value):
        return lax.dynamic_index_in_dim(value.reshape(2, 128, -1), core, 0, False)

    in_other = from_sibling(lax.dynamic_index_in_dim(in_pair, 1 - core, 0, False))
    d_normed = mine(in_part) + in_other
    input_grad = mine(d_res) + norm_backward(d_normed, mine(unit_in), mine(inv_in), gain_in)

    spread = jnp.arange(8)[None, :, None] == 0
    grad["e"] = jnp.concatenate(
        [
            grad_norm_gain[:, None],
            grad_mlp_gain[:, None],
            jnp.where(spread, grad_query_gain[:, None, None], 0.0).reshape(1024, 1),
            jnp.where(spread, grad_key_gain[:, None, None], 0.0).reshape(1024, 1),
            jnp.zeros((1024, 124), f32),
        ],
        axis=1,
    )
    part = {name: grad[name].astype(bf16).reshape(full_shape(name)) for name in NAMES}
    total = reduce_all(part)
    gain_grads = total["e"][0] + total["e"][1]
    return (
        layer_out,
        input_grad,
        gain_grads[:, 0],
        join_columns(total["q"], 256),
        join_columns(total["k"], 128),
        join_columns(total["v"], 128),
        gain_grads[:1, 2],
        gain_grads[:1, 3],
        total["o"].reshape(16, 1024),
        gain_grads[:, 1],
        join_columns(total["g"], 384),
        join_columns(total["u"], 384),
        total["d"].reshape(24, 1024),
    )


def solution(mesh):
    rows = P(("dp", "fsdp"), None)
    flat = P(("dp", "fsdp"))
    return jax.shard_map(
        body,
        mesh=mesh,
        in_specs=(rows, rows, flat, rows, rows, rows, flat, flat, rows, flat, rows, rows, rows, rows),
        out_specs=(rows, rows, flat, rows, rows, rows, flat, flat, rows, flat, rows, rows, rows),
        check_vma=False,
    )
```

```python
import types

import jax
import jax.numpy as jnp
from jax import lax
from jax.experimental import pallas as pl
from jax.experimental.pallas import tpu as pltpu
from jax.sharding import PartitionSpec as P

HD = 128
EPS = 1e-06
LOG_THETA = 13.815510557964274
SCALE = HD ** (-0.5)

bf16 = jnp.bfloat16
f32 = jnp.float32
MESH = pl.DeviceIdType.MESH

ARRAYS = {
    "q": ("n", 8, 1024, 256),
    "k": ("n", 8, 512, 128),
    "v": ("n", 8, 512, 128),
    "o": ("c", 16, 1024, 0),
    "e": ("n", 8, 128, 0),
    "g": ("n", 8, 1536, 384),
    "u": ("n", 8, 1536, 384),
    "d": ("c", 24, 1024, 0),
}
ORDER = {"q": "xyz", "g": "xyz", "k": "yzx", "v": "yzx", "u": "yzx", "o": "zxy", "d": "zxy", "e": "zxy"}
NAMES = tuple(ARRAYS)
ATTN = ("q", "k", "v", "o", "e")
MLP = ("g", "u", "d")
SPLIT = tuple(name for name in NAMES if ARRAYS[name][0] == "n")


def full_shape(name):
    kind, rows, cols, _ = ARRAYS[name]
    if kind == "n":
        return (4, 2, 4, 4, 8, cols)
    return (4, 4, 4, rows // 8, 8, cols)


def coords():
    dp = lax.axis_index("dp")
    fs = lax.axis_index("fsdp")
    return {"y": dp // 2, "c": lax.rem(dp, 2), "z": fs // 4, "x": lax.rem(fs, 4)}


def device(pos, axis=None, step=0):
    pos = dict(pos)
    if axis == "c":
        pos["c"] = 1 - pos["c"]
    elif axis is not None:
        pos[axis] = lax.rem(pos[axis] + step + 4, 4)
    return (pos["y"] * 2 + pos["c"], pos["z"] * 4 + pos["x"])


def greet(pos):
    barrier = pltpu.get_barrier_semaphore()
    others = [device(pos, "c")]
    for axis in "xyz":
        others += [device(pos, axis, 1), device(pos, axis, -1)]
    for other in others:
        pl.semaphore_signal(barrier, inc=1, device_id=other, device_id_type=MESH)
    pl.semaphore_wait(barrier, len(others))


def block(ref, name, at, half=None):
    kind, _, cols, _ = ARRAYS[name]
    part = {axis: pl.ds(at[axis], 1) if axis in at else slice(None) for axis in "yzx"}
    if kind == "n":
        core = slice(None) if half is None else pl.ds(half, 1)
        return ref.at[part["y"], core, part["z"], part["x"]]
    if half is None:
        return ref.at[part["y"], part["z"], part["x"]]
    lanes = pl.ds(half * (cols // 2), cols // 2)
    return ref.at[part["y"], part["z"], part["x"], :, :, lanes]


def half_of(ref, name, half):
    kind, _, cols, _ = ARRAYS[name]
    if kind == "n":
        return ref.at[:, pl.ds(half, 1)]
    return ref.at[:, :, :, :, :, pl.ds(half * (cols // 2), cols // 2)]


def merged(name, fixed):
    shape = list(full_shape(name))
    places = {"y": 0, "z": 2, "x": 3} if ARRAYS[name][0] == "n" else {"y": 0, "z": 1, "x": 2}
    for axis in fixed:
        shape[places[axis]] = 1
    return tuple(shape)


def halved(name, shape):
    shape = list(shape)
    shape[1 if ARRAYS[name][0] == "n" else -1] //= 2
    return tuple(shape)


def add_into(dst, sources, shape):
    lead = shape[:-3]
    count = 1
    for extent in lead:
        count *= extent

    def step(i, carry):
        index, rest = [], i
        for extent in reversed(lead):
            index.append(lax.rem(rest, extent))
            rest = rest // extent
        index = tuple(reversed(index))
        total = sources[0][index].astype(f32)
        for source in sources[1:]:
            total = total + source[index].astype(f32)
        dst[index] = total.astype(dst.dtype)
        return carry

    lax.fori_loop(0, count, step, 0)


def dot(left, right):
    return jnp.dot(left, right, preferred_element_type=f32)


def dot_nt(left, right):
    return lax.dot_general(left, right, (((1,), (1,)), ((), ())), preferred_element_type=f32)


def dot_tn(left, right):
    return lax.dot_general(left, right, (((0,), (0,)), ((), ())), preferred_element_type=f32)


def inverse_rms(vector):
    return lax.rsqrt(jnp.mean(vector * vector, axis=-1, keepdims=True) + EPS)


def norm_backward(grad_in, unit_vec, inverse, gain_vec):
    scaled = grad_in * gain_vec
    return inverse * (scaled - unit_vec * jnp.mean(scaled * unit_vec, axis=-1, keepdims=True))


def lanes_at(start, size):
    return pl.ds(pl.multiple_of(start, 128), size)


def loop(count, body):
    def step(i, carry):
        body(i)
        return carry

    lax.fori_loop(0, count, step, 0)


W = {name: (full_shape(name), bf16) for name in NAMES}
STAGE = {name: ((8, ARRAYS[name][2]), bf16) for name in SPLIT}
FIN = {name: ((2, 8, ARRAYS[name][2]), f32) for name in SPLIT}
RX = {name: ((8, ARRAYS[name][2]), f32) for name in SPLIT}
FAR, NEAR = {}, {}
for _name in NAMES:
    for _phase in range(3):
        _shape = merged(_name, ORDER[_name][::-1][: _phase + 1])
        for _way in range(2):
            FAR[_name, _phase, _way] = (halved(_name, _shape), bf16)
            NEAR[_name, _phase, _way] = (_shape, bf16)
FLAT = dict(
    x=((256, 1024), bf16),
    cot=((256, 1024), bf16),
    seg=((2, 8, 128), jnp.int32),
    gain_rows=((8, 1024), f32),
    head_gains=((8, 128), f32),
    gain_sums=((8, 1024), f32),
    head_sums=((8, 128), f32),
    mask=((2, 128, 128), f32),
    cos=((256, 128), f32),
    sin=((256, 128), f32),
    normed=((256, 1024), bf16),
    q_raw=((256, 1024), f32),
    k_raw=((256, 512), f32),
    values=((256, 512), bf16),
    q_rot=((256, 1024), bf16),
    k_rot=((256, 512), bf16),
    probs=((8, 256, 128), f32),
    attended=((256, 1024), bf16),
    out_part=((256, 1024), f32),
    out_other=((256, 1024), f32),
    hidden=((256, 1024), f32),
    mid_low=((256, 1024), bf16),
    d_mixed=((256, 1536), f32),
    mixed=((256, 1536), bf16),
    d_gate=((256, 1536), bf16),
    d_up=((256, 1536), bf16),
    down_part=((256, 1024), f32),
    down_other=((128, 1024), f32),
    mid_part=((256, 1024), f32),
    mid_other=((256, 1024), f32),
    d_res=((256, 1024), f32),
    d_res_low=((256, 1024), bf16),
    d_attn=((256, 1024), bf16),
    d_q=((256, 1024), bf16),
    d_k=((256, 512), bf16),
    d_v=((256, 512), bf16),
    in_part=((256, 1024), f32),
    in_other=((128, 1024), f32),
)
GROUPS = (W, STAGE, FIN, RX, FAR, NEAR, FLAT)
X_PAIR, COT_PAIR, SEG_PAIR, OUT_PAIR, DOWN_PAIR, MID_PAIR, IN_PAIR, FIN_PAIR = range(8)


def layer_kernel(
    tokens, segment, norm_gain, w_query, w_key, w_value, query_gain, key_gain, w_out, mlp_gain, w_gate, w_up, w_down,
    cotangent, layer_out, input_grad, out_q, out_k, out_v, out_o, out_g, out_u, out_d, out_e, *refs,
):
    refs = list(refs)
    held = []
    for group in GROUPS:
        held.append({key: refs.pop(0) for key in group})
    weight, stage, fin, rx, far_of, near_of, flat = held
    r = types.SimpleNamespace(**flat)
    gather_send, gather_recv, sum_send, sum_recv, pair_send, pair_recv, local = refs
    source = dict(q=w_query, k=w_key, v=w_value, o=w_out, g=w_gate, u=w_up, d=w_down)
    result = dict(q=out_q, k=out_k, v=out_v, o=out_o, g=out_g, u=out_u, d=out_d, e=out_e)
    pos = coords()
    me = pos["c"]
    sibling = device(pos, "c")
    own_rows = pl.ds(pl.multiple_of(me * 128, 128), 128)
    other_rows = pl.ds(pl.multiple_of((1 - me) * 128, 128), 128)

    def remote(src, dst, sems, index, target):
        return pltpu.make_async_remote_copy(
            src_ref=src, dst_ref=dst, send_sem=sems[0].at[index], recv_sem=sems[1].at[index],
            device_id=target, device_id_type=MESH,
        )

    def to_sibling(index, src, dst):
        copy = remote(src, dst, (pair_send, pair_recv), index, sibling)
        copy.start()
        return copy

    gathers = {}

    def gather_start(name, phase):
        order = ORDER[name]
        axis = order[phase]
        at = {a: pos[a] for a in order[phase:]}
        index = NAMES.index(name)
        copies = {}
        for key, half, step in ((0, 0, 1), (1, 1, -1), (2, 1, 1), (3, 0, -1)):
            src = block(weight[name], name, at, half)
            copies[key] = remote(src, src, (gather_send, gather_recv), (index, phase, key), device(pos, axis, step))
            copies[key].start()
        gathers[name, phase] = copies

    def gather_forward(name, phase):
        order = ORDER[name]
        axis = order[phase]
        at = {a: pos[a] for a in order[phase:]}
        index = NAMES.index(name)
        copies = gathers[name, phase]
        for key, got, half, step in ((4, 0, 0, 1), (5, 1, 1, -1)):
            copies[got].wait_recv()
            src = block(weight[name], name, {**at, axis: lax.rem(pos[axis] + 4 - step, 4)}, half)
            copies[key] = remote(src, src, (gather_send, gather_recv), (index, phase, key), device(pos, axis, step))
            copies[key].start()

    def gather_finish(name, phase):
        for key in (2, 3, 4, 5):
            gathers[name, phase][key].wait_recv()

    sums = {}

    def sum_start(name, phase):
        order = ORDER[name][::-1]
        axis = order[phase]
        at = {a: pos[a] for a in order[:phase]}
        ahead, behind = lax.rem(pos[axis] + 1, 4), lax.rem(pos[axis] + 3, 4)
        opposite = lax.rem(pos[axis] + 2, 4)
        up, down = device(pos, axis, 1), device(pos, axis, -1)
        index, sems = NAMES.index(name), (sum_send, sum_recv)
        cur = weight[name]
        near_up, near_down = near_of[name, phase, 0], near_of[name, phase, 1]
        copies = [
            remote(block(cur, name, {**at, axis: opposite}, 0), far_of[name, phase, 0], sems, (index, phase, 0), up),
            remote(block(cur, name, {**at, axis: opposite}, 1), far_of[name, phase, 1], sems, (index, phase, 1), down),
            remote(block(cur, name, {**at, axis: ahead}, 1), half_of(near_up, name, 1), sems, (index, phase, 2), up),
            remote(block(cur, name, {**at, axis: behind}, 0), half_of(near_down, name, 0), sems, (index, phase, 3), down),
        ]
        for copy in copies:
            copy.start()
        sums[name, phase] = copies

    def sum_middle(name, phase):
        order = ORDER[name][::-1]
        axis = order[phase]
        at = {a: pos[a] for a in order[:phase]}
        index, sems = NAMES.index(name), (sum_send, sum_recv)
        shape = halved(name, merged(name, order[: phase + 1]))
        copies = sums[name, phase]
        for half, step in ((0, 1), (1, -1)):
            far, near = far_of[name, phase, half], near_of[name, phase, half]
            copies[half].wait_recv()
            add_into(far, [far, block(weight[name], name, {**at, axis: lax.rem(pos[axis] + 4 + step, 4)}, half)], shape)
            copy = remote(far, half_of(near, name, half), sems, (index, phase, 4 + half), device(pos, axis, step))
            copy.start()
            copies.append(copy)

    def sum_end(name, phase):
        order = ORDER[name][::-1]
        at = {a: pos[a] for a in order[: phase + 1]}
        copies = sums[name, phase]
        for copy in copies[2:]:
            copy.wait_recv()
        sources = [block(weight[name], name, at), near_of[name, phase, 0], near_of[name, phase, 1]]
        if phase < 2:
            add_into(sources[0], sources, merged(name, order[: phase + 1]))
            return
        for t in range(full_shape(name)[1] if name in SPLIT else full_shape(name)[3]):
            place = (0, t, 0, 0) if name in SPLIT else (0, 0, 0, t)
            total = sources[0][place].astype(f32) + sources[1][place].astype(f32) + sources[2][place].astype(f32)
            if name in SPLIT:
                fin[name][t] = total
            else:
                result[name][8 * t : 8 * t + 8, :] = total

    spot = (pos["y"], me, pos["z"], pos["x"])
    for name in NAMES:
        kind, rows, cols, width = ARRAYS[name]
        if name == "e":
            continue
        src = source[name]
        if kind == "n":
            for b in range(cols // width):
                lanes = slice(b * width, (b + 1) * width)
                mine = src[:, lanes_at((2 * b + me) * width, width)]
                weight[name][spot + (slice(None), lanes)] = mine.astype(bf16)
                stage[name][:, lanes] = src[:, lanes_at((2 * b + 1 - me) * width, width)].astype(bf16)
        else:
            for t in range(rows // 8):
                weight[name][pos["y"], pos["z"], pos["x"], t] = src[8 * t : 8 * t + 8, :].astype(bf16)
    row_id = lax.broadcasted_iota(jnp.int32, (8, 128), 0)
    lane_id = lax.broadcasted_iota(jnp.int32, (8, 128), 1)
    gains = jnp.zeros((8, 128), f32)
    for i in range(8):
        gains = jnp.where((row_id == i) & (lane_id == 0), norm_gain[i], gains)
        gains = jnp.where((row_id == i) & (lane_id == 1), mlp_gain[i], gains)
    gains = jnp.where((row_id == 0) & (lane_id == 2), query_gain[0], gains)
    gains = jnp.where((row_id == 0) & (lane_id == 3), key_gain[0], gains).astype(bf16)
    weight["e"][spot] = gains
    stage["e"][...] = gains
    r.seg[me] = jnp.broadcast_to(segment[...], (8, 128))

    greet(pos)
    pairs = {}
    for name in ATTN + MLP:
        if name in SPLIT:
            index = FIN_PAIR + SPLIT.index(name)
            pairs[name] = to_sibling(index, stage[name], weight[name].at[spot])
    kept = []
    for i, src, dst in ((X_PAIR, tokens, r.x), (COT_PAIR, cotangent, r.cot)):
        pairs[i] = to_sibling(i, src, dst.at[own_rows])
        kept.append(pltpu.make_async_copy(src, dst.at[own_rows], local.at[i]))
        kept[i].start()
    pairs[SEG_PAIR] = to_sibling(SEG_PAIR, r.seg.at[me], r.seg.at[me])

    for name in ATTN:
        if name in pairs:
            pairs[name].wait()
        gather_start(name, 0)
    for name in MLP:
        if name in pairs:
            pairs[name].wait()
        gather_start(name, 0)
    for name in ATTN:
        gather_forward(name, 0)
    for name in ATTN:
        gather_finish(name, 0)
        gather_start(name, 1)
    for name in MLP:
        gather_forward(name, 0)
    for name in ATTN:
        gather_forward(name, 1)
    for name in ATTN:
        gather_finish(name, 1)
        gather_start(name, 2)
    for name in MLP:
        gather_finish(name, 0)
        gather_start(name, 1)

    for i in (X_PAIR, COT_PAIR, SEG_PAIR):
        pairs[i].wait()
    for copy in kept:
        copy.wait()
    freq_lane = lax.rem(lax.broadcasted_iota(jnp.int32, (128, 128), 1), 64).astype(f32)
    inv_freq = jnp.exp(freq_lane * (-2.0 / HD * LOG_THETA))
    sign = jnp.where(lax.broadcasted_iota(jnp.int32, (128, 128), 1) < 64, -1.0, 1.0)
    t_id = lax.broadcasted_iota(jnp.int32, (128, 128), 0)
    u_id = lax.broadcasted_iota(jnp.int32, (128, 128), 1)
    for b in range(2):
        ids = jnp.broadcast_to(r.seg[b, 0:1, :].astype(f32), (128, 128))
        same = ids == ids.T
        position = jnp.sum(jnp.where(same & (u_id < t_id), 1.0, 0.0), axis=1, keepdims=True)
        r.mask[b] = jnp.where(same & (u_id <= t_id), 1.0, 0.0)
        angles = position * inv_freq
        r.cos[128 * b : 128 * b + 128, :] = jnp.cos(angles)
        r.sin[128 * b : 128 * b + 128, :] = jnp.sin(angles) * sign

    for name in ATTN:
        gather_forward(name, 2)
    for name in MLP:
        gather_forward(name, 1)
    for name in MLP:
        gather_finish(name, 1)
        gather_start(name, 2)
    for name in ATTN:
        gather_finish(name, 2)

    pick = jnp.where(row_id == lane_id, 1.0, 0.0).astype(bf16)
    gain_rows = dot_nt(pick, weight["e"][...].reshape(1024, 128))
    r.gain_rows[...] = gain_rows
    eighth = lax.broadcasted_iota(jnp.int32, (1024, 128), 0) == 8 * lax.broadcasted_iota(jnp.int32, (1024, 128), 1)
    eighth = jnp.where(eighth, 1.0, 0.0).astype(bf16)
    r.head_gains[...] = dot(gain_rows.astype(bf16), eighth)
    gain_in, gain_mid = r.gain_rows.at[0:1], r.gain_rows.at[1:2]
    gain_query, gain_key = r.head_gains.at[2:3], r.head_gains.at[3:4]

    def rows_of(i, size=32):
        return pl.ds(pl.multiple_of(i * size, size), size)

    def norm_in(i):
        x = r.x[rows_of(i), :].astype(f32)
        r.normed[rows_of(i), :] = (x * inverse_rms(x) * gain_in[...]).astype(bf16)

    loop(8, norm_in)
    normed = r.normed

    def project_q(i):
        lanes = lanes_at(i * 512, 512)
        r.q_raw[:, lanes] = dot(normed[...], weight["q"][..., lanes].reshape(1024, 512))

    loop(2, project_q)
    r.k_raw[...] = dot(normed[...], weight["k"][...].reshape(1024, 512))
    r.values[...] = dot(normed[...], weight["v"][...].reshape(1024, 512)).astype(bf16)

    def rotate(vector, cos_part, sin_part):
        return vector * cos_part + pltpu.roll(vector, 64, 1) * sin_part

    def turn(src, dst, gain):
        def head(h):
            lanes = lanes_at(h * 128, 128)
            raw = src[:, lanes]
            turned = rotate(raw * inverse_rms(raw) * gain[...], r.cos[...], r.sin[...])
            dst[:, lanes] = turned.astype(bf16)

        return head

    loop(8, turn(r.q_raw, r.q_rot, gain_query))
    loop(4, turn(r.k_raw, r.k_rot, gain_key))

    def both_heads(ref, rows, m):
        first = ref[rows, lanes_at(m * 256, 128)]
        second = ref[rows, lanes_at(m * 256 + 128, 128)]
        return jnp.concatenate([first, second], axis=0)

    def attend(i):
        b, m = i // 4, lax.rem(i, 4)
        rows = pl.ds(pl.multiple_of(b * 128, 128), 128)
        lanes = lanes_at(m * 128, 128)
        scores = dot_nt(both_heads(r.q_rot, rows, m), r.k_rot[rows, lanes]) * SCALE
        mask = r.mask[b]
        masked = jnp.where(jnp.concatenate([mask, mask], axis=0) > 0.0, scores, -1e30)
        terms = jnp.exp(masked - jnp.max(masked, axis=-1, keepdims=True))
        probs = terms / jnp.sum(terms, axis=-1, keepdims=True)
        r.probs[i] = probs
        got = dot(probs.astype(bf16), r.values[rows, lanes]).astype(bf16)
        r.attended[rows, lanes_at(m * 256, 128)] = got[:128]
        r.attended[rows, lanes_at(m * 256 + 128, 128)] = got[128:]

    loop(8, attend)
    attended = r.attended

    def project_out(i):
        lanes = lanes_at(i * 512, 512)
        r.out_part[:, lanes] = dot(attended[...], weight["o"][..., lanes].reshape(1024, 512))

    loop(2, project_out)
    out_copy = to_sibling(OUT_PAIR, r.out_part, r.out_other)

    for name in MLP:
        gather_forward(name, 2)
    for name in MLP:
        gather_finish(name, 2)
    for copies in gathers.values():
        for key in range(6):
            copies[key].wait_send()

    cot = r.cot

    def mixed_back(i):
        two = weight["d"][pl.ds(2 * i, 2)].reshape(768, 1024)
        r.d_mixed[:, lanes_at(i * 768, 768)] = dot_nt(cot[...], two)

    loop(2, mixed_back)
    out_copy.wait()

    def norm_mid(i):
        rows = rows_of(i)
        hidden = r.x[rows, :].astype(f32) + (r.out_part[rows, :] + r.out_other[rows, :])
        r.hidden[rows, :] = hidden
        r.mid_low[rows, :] = (hidden * inverse_rms(hidden) * gain_mid[...]).astype(bf16)

    loop(8, norm_mid)
    mid_low = r.mid_low

    def feed(i):
        lanes = lanes_at(i * 512, 512)
        gate = dot(mid_low[...], weight["g"][..., lanes].reshape(1024, 512))
        up = dot(mid_low[...], weight["u"][..., lanes].reshape(1024, 512))
        sig = jax.nn.sigmoid(gate)
        act = gate * sig
        d_mixed = r.d_mixed[:, lanes]
        r.mixed[:, lanes] = (act * up).astype(bf16)
        r.d_gate[:, lanes] = (d_mixed * up * sig * (1.0 + gate * (1.0 - sig))).astype(bf16)
        r.d_up[:, lanes] = (d_mixed * act).astype(bf16)

    loop(3, feed)
    mixed, d_gate, d_up = r.mixed, r.d_gate, r.d_up

    def project_down(i):
        lanes = lanes_at(i * 512, 512)
        r.down_part[:, lanes] = dot(mixed[...], weight["d"][..., lanes].reshape(1536, 512))

    loop(2, project_down)
    down_copy = to_sibling(DOWN_PAIR, r.down_part.at[other_rows], r.down_other)

    def grad_down(i):
        got = dot_tn(mixed[:, lanes_at(i * 384, 384)], cot[...]).astype(bf16)
        weight["d"][i] = got.reshape(4, 4, 3, 8, 1024)

    loop(4, grad_down)
    sum_start("d", 0)

    def mid_back(i):
        got = dot_nt(d_gate[...], weight["g"][pl.ds(2 * i, 2)].reshape(512, 1536))
        got += dot_nt(d_up[...], weight["u"][pl.ds(2 * i, 2)].reshape(512, 1536))
        r.mid_part[:, lanes_at(i * 512, 512)] = got

    loop(2, mid_back)
    mid_copy = to_sibling(MID_PAIR, r.mid_part, r.mid_other)

    def grad_of(name, left, right):
        cols = ARRAYS[name][2]

        def rows(i):
            got = dot_tn(left[:, lanes_at(i * 256, 256)], right[...]).astype(bf16)
            shape = (2, 4, 4, 8, cols) if name in SPLIT else (4, 4, 2, 8, cols)
            weight[name][i] = got.reshape(shape)

        loop(4, rows)

    grad_of("g", mid_low, d_gate)
    sum_start("g", 0)
    grad_of("u", mid_low, d_up)
    sum_start("u", 0)
    mid_copy.wait()

    r.gain_sums[...] = jnp.zeros((8, 1024), f32)
    r.head_sums[...] = jnp.zeros((8, 128), f32)

    def res_back(i):
        rows = rows_of(i)
        hidden = r.hidden[rows, :]
        inverse = inverse_rms(hidden)
        unit = hidden * inverse
        part = r.mid_part[rows, :]
        r.gain_sums[1:2, :] += jnp.sum(part * unit, axis=0, keepdims=True)
        d_mid = part + r.mid_other[rows, :]
        d_res = cot[rows, :].astype(f32) + norm_backward(d_mid, unit, inverse, gain_mid[...])
        r.d_res[rows, :] = d_res
        r.d_res_low[rows, :] = d_res.astype(bf16)

    loop(8, res_back)
    d_res_low = r.d_res_low
    sum_middle("d", 0)

    def attn_back(i):
        two = weight["o"][pl.ds(2 * i, 2)].reshape(512, 1024)
        r.d_attn[:, lanes_at(i * 512, 512)] = dot_nt(d_res_low[...], two).astype(bf16)

    loop(2, attn_back)
    grad_of("o", attended, d_res_low)
    sum_start("o", 0)
    sum_middle("g", 0)
    sum_middle("u", 0)

    def head_back(grad, raw, gain):
        inverse = inverse_rms(raw)
        unit = raw * inverse
        return jnp.sum(grad * unit, axis=0, keepdims=True), norm_backward(grad, unit, inverse, gain[...])

    def attend_back(i):
        b, m = i // 4, lax.rem(i, 4)
        rows = pl.ds(pl.multiple_of(b * 128, 128), 128)
        lanes = lanes_at(m * 128, 128)
        d_att = both_heads(r.d_attn, rows, m)
        query, key = both_heads(r.q_rot, rows, m), r.k_rot[rows, lanes]
        probs = r.probs[i]
        d_probs = dot_nt(d_att, r.values[rows, lanes])
        r.d_v[rows, lanes] = dot_tn(probs.astype(bf16), d_att).astype(bf16)
        d_scores = (probs * (d_probs - jnp.sum(d_probs * probs, axis=-1, keepdims=True))).astype(bf16)
        d_query = dot(d_scores, key) * SCALE
        d_key = dot_tn(d_scores, query) * SCALE
        cos_part, sin_part = r.cos[rows, :], -r.sin[rows, :]
        for j in range(2):
            spots = lanes_at(m * 256 + 128 * j, 128)
            d_unit = rotate(d_query[128 * j : 128 * j + 128], cos_part, sin_part)
            total, d_raw = head_back(d_unit, r.q_raw[rows, spots], gain_query)
            r.head_sums[2:3, :] += total
            r.d_q[rows, spots] = d_raw.astype(bf16)
        total, d_raw = head_back(rotate(d_key, cos_part, sin_part), r.k_raw[rows, lanes], gain_key)
        r.head_sums[3:4, :] += total
        r.d_k[rows, lanes] = d_raw.astype(bf16)

    loop(8, attend_back)

    def in_back(i):
        y_pair = pl.ds(2 * i, 2)
        got = dot_nt(r.d_q[...], weight["q"][y_pair].reshape(512, 1024))
        got += dot_nt(r.d_k[...], weight["k"][y_pair].reshape(512, 512))
        got += dot_nt(r.d_v[...], weight["v"][y_pair].reshape(512, 512))
        r.in_part[:, lanes_at(i * 512, 512)] = got

    loop(2, in_back)
    in_copy = to_sibling(IN_PAIR, r.in_part.at[other_rows], r.in_other)
    grad_of("q", normed, r.d_q)
    sum_start("q", 0)
    grad_of("k", normed, r.d_k)
    sum_start("k", 0)
    grad_of("v", normed, r.d_v)
    sum_start("v", 0)

    def gain_back(i):
        x = r.x[rows_of(i), :].astype(f32)
        unit = x * inverse_rms(x)
        r.gain_sums[0:1, :] += jnp.sum(r.in_part[rows_of(i), :] * unit, axis=0, keepdims=True)

    loop(8, gain_back)
    spread = dot_nt(r.head_sums[...].astype(bf16), eighth)
    grad_e = dot_tn((r.gain_sums[...] + spread).astype(bf16), pick).astype(bf16)
    weight["e"][...] = grad_e.reshape(full_shape("e"))
    sum_start("e", 0)

    for name in MLP:
        sum_end(name, 0)
        sum_start(name, 1)
    for name in ATTN:
        sum_middle(name, 0)

    down_copy.wait()

    def finish_out(i):
        rows = rows_of(i)
        mine = pl.ds(pl.multiple_of(me * 128 + i * 32, 32), 32)
        down = r.down_part[mine, :] + r.down_other[rows, :]
        layer_out[rows, :] = (r.hidden[mine, :] + down).astype(bf16)

    loop(4, finish_out)
    in_copy.wait()

    def finish_in(i):
        rows = rows_of(i)
        mine = pl.ds(pl.multiple_of(me * 128 + i * 32, 32), 32)
        d_normed = r.in_part[mine, :] + r.in_other[rows, :]
        x = r.x[mine, :].astype(f32)
        inverse = inverse_rms(x)
        input_grad[rows, :] = r.d_res[mine, :] + norm_backward(d_normed, x * inverse, inverse, gain_in[...])

    loop(4, finish_in)

    for name in MLP:
        sum_middle(name, 1)
    for name in ATTN:
        sum_end(name, 0)
        sum_start(name, 1)
    for name in MLP:
        sum_end(name, 1)
        sum_start(name, 2)
    for name in ATTN:
        sum_middle(name, 1)
    for name in MLP:
        sum_middle(name, 2)
    for name in ATTN:
        sum_end(name, 1)
        sum_start(name, 2)
    for name in MLP:
        sum_end(name, 2)
    for name in ATTN:
        sum_middle(name, 2)
    for name in ATTN:
        sum_end(name, 2)

    last = {}
    for name in SPLIT:
        last[name] = to_sibling(FIN_PAIR + len(SPLIT) + SPLIT.index(name), fin[name].at[1 - me], rx[name])
    for name in SPLIT:
        last[name].wait()
        _, _, cols, width = ARRAYS[name]
        if name == "e":
            out_e[...] = fin["e"][me] + rx["e"][...]
            continue
        for b in range(cols // width):
            lanes = slice(b * width, (b + 1) * width)
            result[name][:, lanes_at((2 * b + me) * width, width)] = fin[name][me, :, lanes]
            result[name][:, lanes_at((2 * b + 1 - me) * width, width)] = rx[name][:, lanes]
    for copies in sums.values():
        for copy in copies:
            copy.wait_send()


def body(*args):
    vmem = pl.BlockSpec(memory_space=pltpu.VMEM)
    smem = pl.BlockSpec(memory_space=pltpu.SMEM)
    hbm = pl.BlockSpec(memory_space=pl.ANY)
    n = len(NAMES)
    shapes = [(128, 1024)] * 2 + [(8, 2048), (8, 1024), (8, 1024), (16, 1024), (8, 3072), (8, 3072), (24, 1024), (8, 128)]
    scratch = [pltpu.VMEM(*entry) for group in GROUPS for entry in group.values()]
    pair_count = FIN_PAIR + 2 * len(SPLIT)
    outs = pl.pallas_call(
        layer_kernel,
        out_shape=[jax.ShapeDtypeStruct(shape, f32 if i else bf16) for i, shape in enumerate(shapes)],
        in_specs=[hbm, vmem, smem, vmem, vmem, vmem, smem, smem, vmem, smem, vmem, vmem, vmem, hbm],
        out_specs=[vmem] * len(shapes),
        scratch_shapes=scratch
        + [pltpu.SemaphoreType.DMA((n, 3, 6))] * 4
        + [pltpu.SemaphoreType.DMA((pair_count,))] * 2
        + [pltpu.SemaphoreType.DMA((2,))],
        compiler_params=pltpu.CompilerParams(
            collective_id=1, has_side_effects=True, vmem_limit_bytes=60 << 20
        ),
        name="layer",
    )(*args)
    layer_out, input_grad, grad_q, grad_k, grad_v, grad_o, grad_g, grad_u, grad_d, gains = outs
    return (
        layer_out, input_grad, gains[:, 0], grad_q, grad_k, grad_v, gains[0, 2:3], gains[0, 3:4], grad_o, gains[:, 1],
        grad_g, grad_u, grad_d,
    )


def solution(mesh):
    rows = P(("dp", "fsdp"), None)
    flat = P(("dp", "fsdp"))
    return jax.shard_map(
        body,
        mesh=mesh,
        in_specs=(rows, rows, flat, rows, rows, rows, flat, flat, rows, flat, rows, rows, rows, rows),
        out_specs=(rows, rows, flat, rows, rows, rows, flat, flat, rows, flat, rows, rows, rows),
        check_vma=False,
    )
```

```python
import types

import jax
import jax.numpy as jnp
from jax import lax
from jax.experimental import pallas as pl
from jax.experimental.pallas import tpu as pltpu
from jax.sharding import PartitionSpec as P

HD = 128
EPS = 1e-06
LOG_THETA = 13.815510557964274
SCALE = HD ** (-0.5)

bf16 = jnp.bfloat16
f32 = jnp.float32
MESH = pl.DeviceIdType.MESH

SHAPES = dict(
    q=(4, 2, 4, 4, 8, 1024),
    b=(4, 2, 4, 4, 8, 1024),
    o=(4, 4, 4, 2, 8, 1024),
    e=(4, 2, 4, 4, 1, 128),
    g=(3, 4, 2, 4, 4, 8, 512),
    u=(3, 4, 2, 4, 4, 8, 512),
    d=(3, 4, 4, 4, 8, 1024),
)
NAMES = tuple(SHAPES)
SPLIT = ("q", "b", "e", "g", "u")
ATTN = ("q", "b", "o")
MLP = ("g", "u", "d")
ORDER = dict(q="xyz", g="xyz", b="yzx", u="yzx", o="zxy", d="zxy", e="zxy")
DTYPE = {name: f32 if name == "e" else bf16 for name in NAMES}


def coords():
    dp = lax.axis_index("dp")
    fs = lax.axis_index("fsdp")
    return dict(y=dp // 2, c=lax.rem(dp, 2), z=fs // 4, x=lax.rem(fs, 4))


def device(pos, axis=None, step=0):
    pos = dict(pos)
    if axis == "c":
        pos["c"] = 1 - pos["c"]
    elif axis is not None:
        pos[axis] = lax.rem(pos[axis] + step + 4, 4)
    return (pos["y"] * 2 + pos["c"], pos["z"] * 4 + pos["x"])


def item_shape(item):
    name, third = item
    return SHAPES[name] if third is None else SHAPES[name][1:]


def lead_of(item):
    return 1 if item[0] in MLP and item[1] is None else 0


def axis_places(item):
    lead = lead_of(item)
    if item[0] in SPLIT:
        return dict(y=lead, z=lead + 2, x=lead + 3)
    return dict(y=lead, z=lead + 1, x=lead + 2)


def block(ref, item, at, half=None):
    shape = item_shape(item)
    index = [slice(None)] * len(shape)
    for axis, place in axis_places(item).items():
        if axis in at:
            start, size = at[axis] if isinstance(at[axis], tuple) else (at[axis], 1)
            index[place] = pl.ds(start, size)
    if half is not None:
        if item[0] in SPLIT:
            index[lead_of(item) + 1] = pl.ds(half, 1)
        else:
            index[-1] = pl.ds(half * (shape[-1] // 2), shape[-1] // 2)
    return ref.at[tuple(index)]


def half_of(ref, item, half):
    return block(ref, item, {}, half)


def merged(item, fixed):
    shape = list(item_shape(item))
    for axis in fixed:
        shape[axis_places(item)[axis]] = 1
    return tuple(shape)


def halved(item, shape):
    shape = list(shape)
    shape[lead_of(item) + 1 if item[0] in SPLIT else -1] //= 2
    return tuple(shape)


def add_into(dst, sources, shape):
    lead = shape[:-3]
    count = 1
    for extent in lead:
        count *= extent

    def step(i, carry):
        index, rest = [], i
        for extent in reversed(lead):
            index.append(lax.rem(rest, extent))
            rest = rest // extent
        index = tuple(reversed(index))
        total = sources[0][index].astype(f32)
        for source in sources[1:]:
            total = total + source[index].astype(f32)
        dst[index] = total.astype(dst.dtype)
        return carry

    lax.fori_loop(0, count, step, 0)


def dot(left, right):
    return jnp.dot(left, right, preferred_element_type=f32)


def dot_nt(left, right):
    return lax.dot_general(left, right, (((1,), (1,)), ((), ())), preferred_element_type=f32)


def dot_tn(left, right):
    return lax.dot_general(left, right, (((0,), (0,)), ((), ())), preferred_element_type=f32)


def inverse_rms(vector):
    return lax.rsqrt(jnp.mean(vector * vector, axis=-1, keepdims=True) + EPS)


def norm_backward(grad_in, unit_vec, inverse, gain_vec):
    scaled = grad_in * gain_vec
    return inverse * (scaled - unit_vec * jnp.mean(scaled * unit_vec, axis=-1, keepdims=True))


def lanes_at(start, size):
    return pl.ds(pl.multiple_of(start, 128), size)


def rows_at(start, size):
    return pl.ds(pl.multiple_of(start, 8), size)


def loop(count, body):
    def step(i, carry):
        body(i)
        return carry

    lax.fori_loop(0, count, step, 0)


ALL = (("q", None), ("b", None), ("o", None), ("e", None), ("g", None), ("u", None), ("d", None))
THIRDS = tuple((name, t) for t in range(3) for name in MLP)
ITEMS = ALL + THIRDS
SUMS = tuple((item, phase) for item in ALL for phase in range(3) if item[0] not in MLP or phase > 0)
SUMS += tuple((item, 0) for item in THIRDS)


def is_direct(item, phase):
    return phase == 2 or item[0] == "e" or (phase == 1 and item[0] not in MLP)


GATHERS = tuple((item, phase) for item in ALL for phase in range(3) if item[0] not in MLP or phase < 2)
GATHERS += tuple((item, 2) for item in THIRDS)
SEMS = {}
for _kind, _steps in enumerate((GATHERS, SUMS)):
    for _item, _phase in _steps:
        _direct = is_direct(_item, _phase) if _kind else _phase == 0 or _item[0] == "e"
        for _use in range(2 if _direct else 3):
            SEMS[_kind, _item, _phase, _use] = len(SEMS)
W = {name: (SHAPES[name], DTYPE[name]) for name in NAMES}
STAGE = dict(q=((8, 1024), bf16), b=((8, 1024), bf16), e=((1, 128), f32), g=((3, 8, 512), bf16), u=((3, 8, 512), bf16))
FIN = dict(q=((2, 8, 1024), f32), b=((2, 8, 1024), f32), e=((2, 1, 128), f32), g=((2, 3, 8, 512), f32), u=((2, 3, 8, 512), f32))
RX = dict(q=((8, 1024), f32), b=((8, 1024), f32), e=((1, 128), f32), g=((3, 8, 512), f32), u=((3, 8, 512), f32))
FAR, NEAR = {}, {}
for _item, _phase in SUMS:
    _shape = merged(_item, ORDER[_item[0]][::-1][: _phase + 1])
    for _way in range(2):
        NEAR[_item, _phase, _way] = (_shape, DTYPE[_item[0]])
        if not is_direct(_item, _phase):
            FAR[_item, _phase, _way] = (halved(_item, _shape), DTYPE[_item[0]])
    if is_direct(_item, _phase):
        FAR[_item, _phase, 2] = (_shape, DTYPE[_item[0]])
INS = (
    ((8, 2048), f32), ((8, 1024), f32), ((8, 1024), f32), ((16, 1024), f32), ((8, 3072), f32), ((8, 3072), f32), ((24, 1024), f32),
)
OUTS = (((128, 1024), bf16), ((128, 1024), f32)) + INS + (((8, 128), f32),)
IN_BUF = {i: entry for i, entry in enumerate(INS)}
OUT_BUF = {i: entry for i, entry in enumerate(OUTS)}
FLAT = dict(
    x=((256, 1024), bf16),
    cot=((256, 1024), bf16),
    seg=((2, 8, 128), jnp.int32),
    perm=((384, 384), bf16),
    blocks=((128, 384), f32),
    eighths=((2, 1024, 128), bf16),
    gain_rows=((8, 1024), f32),
    head_gains=((8, 128), f32),
    gain_sums=((8, 1024), f32),
    head_sums=((8, 128), f32),
    mask=((2, 128, 128), f32),
    cos=((256, 128), f32),
    sin=((256, 128), f32),
    normed=((256, 1024), bf16),
    q_raw=((256, 1024), f32),
    k_raw=((256, 512), f32),
    values=((256, 512), bf16),
    q_rot=((256, 1024), bf16),
    k_rot=((256, 512), bf16),
    probs=((8, 256, 128), f32),
    attended=((256, 1024), bf16),
    out_part=((256, 1024), f32),
    out_other=((256, 1024), f32),
    hidden=((256, 1024), f32),
    mid_low=((256, 1024), bf16),
    mixed=((256, 512), bf16),
    d_gate=((256, 512), bf16),
    d_up=((256, 512), bf16),
    down_part=((256, 1024), f32),
    down_other=((128, 1024), f32),
    mid_part=((256, 1024), f32),
    mid_other=((256, 1024), f32),
    d_res=((256, 1024), f32),
    d_res_low=((256, 1024), bf16),
    d_attn=((256, 1024), bf16),
    d_q=((256, 1024), bf16),
    d_b=((256, 1024), bf16),
    in_part=((256, 1024), f32),
    in_other=((128, 1024), f32),
)
GROUPS = (W, STAGE, FIN, RX, FAR, NEAR, IN_BUF, OUT_BUF, FLAT)
X_PAIR, COT_PAIR, SEG_PAIR, OUT_PAIR, DOWN_PAIR, MID_PAIR, IN_PAIR, STAGE_PAIR = range(8)
FIN_PAIR = STAGE_PAIR + len(SPLIT)
PAIRS = FIN_PAIR + len(SPLIT)


def layer_kernel(
    tokens, segment, norm_gain, w_query, w_key, w_value, query_gain, key_gain, w_out, mlp_gain, w_gate, w_up, w_down,
    cotangent, *refs,
):
    refs = list(refs)
    outputs = [refs.pop(0) for _ in OUTS]
    held = []
    for group in GROUPS:
        held.append({key: refs.pop(0) for key in group})
    weight, stage, fin, rx, far_of, near_of, in_buf, out_buf, flat = held
    r = types.SimpleNamespace(**flat)
    sems, pair_send, pair_recv, local_in, local_out = refs
    pos = coords()
    me = pos["c"]
    sibling = device(pos, "c")
    own_rows = pl.ds(pl.multiple_of(me * 128, 128), 128)
    other_rows = pl.ds(pl.multiple_of((1 - me) * 128, 128), 128)
    layer_out, input_grad = out_buf[0], out_buf[1]

    barrier = pltpu.get_barrier_semaphore()
    others = [sibling]
    for axis in "xyz":
        others += [device(pos, axis, step) for step in (1, -1, 2)]
    for other in others:
        pl.semaphore_signal(barrier, inc=1, device_id=other, device_id_type=MESH)
    fetches = []
    for i, src in enumerate((w_query, w_key, w_value, w_out, w_gate, w_up, w_down)):
        fetches.append(pltpu.make_async_copy(src, in_buf[i], local_in.at[i]))
    fetches.append(pltpu.make_async_copy(tokens, r.x.at[own_rows], local_in.at[7]))
    fetches.append(pltpu.make_async_copy(cotangent, r.cot.at[own_rows], local_in.at[8]))
    for copy in fetches:
        copy.start()

    def remote(src, dst, send_sem, recv_sem, target):
        return pltpu.make_async_remote_copy(
            src_ref=src, dst_ref=dst, send_sem=send_sem, recv_sem=recv_sem, device_id=target, device_id_type=MESH
        )

    def to_sibling(index, src, dst):
        copy = remote(src, dst, pair_send.at[index], pair_recv.at[index], sibling)
        copy.start()
        return copy

    def sem(kind, item, phase, use):
        return sems.at[SEMS[kind, item, phase, use]]

    def send(kind, item, phase, use, src, dst, target):
        remote(src, dst, sem(kind, item, phase, 0), sem(kind, item, phase, use), target).start()

    def wait_for(kind, item, phase, use, count):
        order = ORDER[item[0]] if kind == 0 else ORDER[item[0]][::-1]
        fixed = order[phase + 1 :] if kind == 0 else order[:phase]
        like = block(view(item), item, {**{a: pos[a] for a in fixed}, order[phase]: (0, count)})
        pltpu.make_async_copy(like, like, sem(kind, item, phase, use)).wait()

    def view(item):
        name, third = item
        return weight[name] if third is None else weight[name].at[third]

    def gather_start(item, phase, keys=(0, 1, 2, 3)):
        order = ORDER[item[0]]
        axis = order[phase]
        at = {a: pos[a] for a in order[phase:]}
        if phase == 0 or item[0] == "e":
            for step in (1, -1, 2):
                src = block(view(item), item, at)
                send(0, item, phase, 1, src, src, device(pos, axis, step))
            return
        for key, half, step in ((0, 0, 1), (1, 1, -1), (2, 1, 1), (3, 0, -1)):
            if key in keys:
                src = block(view(item), item, at, half)
                send(0, item, phase, 1 if key < 2 else 2, src, src, device(pos, axis, step))

    def gather_forward(item, phase):
        order = ORDER[item[0]]
        axis = order[phase]
        at = {a: pos[a] for a in order[phase:]}
        wait_for(0, item, phase, 1, 1)
        for half, step in ((0, 1), (1, -1)):
            src = block(view(item), item, {**at, axis: lax.rem(pos[axis] + 4 - step, 4)}, half)
            send(0, item, phase, 2, src, src, device(pos, axis, step))

    def gather_finish(item, phase):
        if phase == 0 or item[0] == "e":
            wait_for(0, item, phase, 1, 3)
        else:
            wait_for(0, item, phase, 2, 2)

    def sum_start(item, phase):
        order = ORDER[item[0]][::-1]
        axis = order[phase]
        at = {a: pos[a] for a in order[:phase]}
        ahead, behind = lax.rem(pos[axis] + 1, 4), lax.rem(pos[axis] + 3, 4)
        opposite = lax.rem(pos[axis] + 2, 4)
        up, down, across = device(pos, axis, 1), device(pos, axis, -1), device(pos, axis, 2)
        cur = view(item)
        near_up, near_down = near_of[item, phase, 0], near_of[item, phase, 1]

        def part(place, half=None):
            return block(cur, item, {**at, axis: place}, half)

        if is_direct(item, phase):
            send(1, item, phase, 1, part(opposite), far_of[item, phase, 2], across)
            send(1, item, phase, 1, part(ahead), near_up, up)
            send(1, item, phase, 1, part(behind), near_down, down)
        else:
            send(1, item, phase, 1, part(opposite, 0), far_of[item, phase, 0], up)
            send(1, item, phase, 1, part(opposite, 1), far_of[item, phase, 1], down)
            send(1, item, phase, 2, part(ahead, 1), half_of(near_up, item, 1), up)
            send(1, item, phase, 2, part(behind, 0), half_of(near_down, item, 0), down)

    def sum_middle(item, phase):
        order = ORDER[item[0]][::-1]
        axis = order[phase]
        at = {a: pos[a] for a in order[:phase]}
        shape = halved(item, merged(item, order[: phase + 1]))
        wait_for(1, item, phase, 1, 1)
        for half, step in ((0, 1), (1, -1)):
            far, near = far_of[item, phase, half], near_of[item, phase, half]
            mine = block(view(item), item, {**at, axis: lax.rem(pos[axis] + 4 + step, 4)}, half)
            add_into(far, [far, mine], shape)
            send(1, item, phase, 2, far, half_of(near, item, half), device(pos, axis, step))

    def sum_end(item, phase):
        order = ORDER[item[0]][::-1]
        at = {a: pos[a] for a in order[: phase + 1]}
        sources = [block(view(item), item, at), near_of[item, phase, 0], near_of[item, phase, 1]]
        if is_direct(item, phase):
            sources.append(far_of[item, phase, 2])
            wait_for(1, item, phase, 1, 3)
        else:
            wait_for(1, item, phase, 2, 2)
        if phase < 2:
            add_into(sources[0], sources, merged(item, order[: phase + 1]))
            return

        def total(place):
            value = sources[0][place].astype(f32)
            for source in sources[1:]:
                value = value + source[place].astype(f32)
            return value

        name = item[0]
        if name in MLP:
            for t in range(3):
                if name == "d":
                    out_buf[8][8 * t : 8 * t + 8, :] = total((t, 0, 0, 0))
                else:
                    for c in range(2):
                        fin[name][c, t] = total((t, 0, c, 0, 0))
        elif name == "o":
            for t in range(2):
                out_buf[5][8 * t : 8 * t + 8, :] = total((0, 0, 0, t))
        else:
            for c in range(2):
                fin[name][c] = total((0, c, 0, 0))

    spot = (pos["y"], me, pos["z"], pos["x"])

    def stage_columns(name, buf, start, count, width, place):
        for i in range(count):
            lanes = slice(place + i * width, place + (i + 1) * width)
            weight[name][spot + (slice(None), lanes)] = in_buf[buf][:, lanes_at((2 * i + me) * width, width)].astype(bf16)
            stage[name][:, lanes] = in_buf[buf][:, lanes_at((2 * i + 1 - me) * width, width)].astype(bf16)

    row_id = lax.broadcasted_iota(jnp.int32, (8, 128), 0)
    lane_id = lax.broadcasted_iota(jnp.int32, (8, 128), 1)
    lane_row = lax.broadcasted_iota(jnp.int32, (1, 128), 1)
    gains = jnp.zeros((1, 128), f32)
    for i in range(8):
        gains = jnp.where(lane_row == i, norm_gain[i], gains)
        gains = jnp.where(lane_row == 8 + i, mlp_gain[i], gains)
    gains = jnp.where(lane_row == 16, query_gain[0], gains)
    gains = jnp.where(lane_row == 17, key_gain[0], gains).astype(bf16).astype(f32)
    weight["e"][spot] = gains
    stage["e"][...] = gains
    r.seg[me] = jnp.broadcast_to(segment[...], (8, 128))
    for i in range(4):
        fetches[i].wait()
    stage_columns("q", 0, 0, 4, 256, 0)
    stage_columns("b", 1, 0, 4, 128, 0)
    stage_columns("b", 2, 0, 4, 128, 512)
    for t in range(2):
        weight["o"][pos["y"], pos["z"], pos["x"], t] = in_buf[3][8 * t : 8 * t + 8, :].astype(bf16)

    pl.semaphore_wait(barrier, len(others))
    pairs = {}

    def pair_start(name):
        index = STAGE_PAIR + SPLIT.index(name)
        if name in MLP:
            dst = weight[name].at[:, pos["y"], me, pos["z"], pos["x"]]
        else:
            dst = weight[name].at[spot]
        pairs[name] = to_sibling(index, stage[name], dst)

    for name in ("q", "b", "e"):
        pair_start(name)

    to_lane = lax.broadcasted_iota(jnp.int32, (384, 384), 1)
    from_lane = ((to_lane >> 3) & 15) * 24 + (to_lane >> 7) * 8 + (to_lane & 7)
    r.perm[...] = jnp.where(lax.broadcasted_iota(jnp.int32, (384, 384), 0) == from_lane, 1.0, 0.0).astype(bf16)
    for i in range(4, 7):
        fetches[i].wait()
    for i, buf in ((0, 4), (1, 5)):
        for b in range(8):
            r.blocks[64 * i + 8 * b : 64 * i + 8 * b + 8, :] = in_buf[buf][:, 384 * b : 384 * b + 384]
    r.blocks[...] = dot(r.blocks[...].astype(bf16), r.perm[...])
    for i, name in ((0, "g"), (1, "u")):
        for y in range(4):
            mine = r.blocks[rows_at(64 * i + 8 * (2 * y + me), 8), :].astype(bf16)
            theirs = r.blocks[rows_at(64 * i + 8 * (2 * y + 1 - me), 8), :].astype(bf16)
            for t in range(3):
                lanes = slice(128 * y, 128 * y + 128)
                weight[name][(t,) + spot + (slice(None), lanes)] = mine[:, 128 * t : 128 * t + 128]
                stage[name][t, :, lanes] = theirs[:, 128 * t : 128 * t + 128]
    for t in range(3):
        weight["d"][t, pos["y"], pos["z"], pos["x"]] = in_buf[6][8 * t : 8 * t + 8, :].astype(bf16)
    for name in ("g", "u"):
        pair_start(name)
    for name in ("e", "q", "b"):
        pairs[name].wait()
    for name in ("e", "q", "b", "o"):
        gather_start((name, None), 0)
    for name in ("g", "u"):
        pairs[name].wait()
    for name in MLP:
        gather_start((name, None), 0)
    fetches[7].wait()
    fetches[8].wait()
    pairs[X_PAIR] = to_sibling(X_PAIR, r.x.at[own_rows], r.x.at[own_rows])
    pairs[SEG_PAIR] = to_sibling(SEG_PAIR, r.seg.at[me], r.seg.at[me])
    pairs[COT_PAIR] = to_sibling(COT_PAIR, r.cot.at[own_rows], r.cot.at[own_rows])
    for name in ("e",) + ATTN:
        gather_finish((name, None), 0)
        gather_start((name, None), 1)
    for name in MLP:
        gather_finish((name, None), 0)
        gather_start((name, None), 1, (0, 1))

    for i in (X_PAIR, SEG_PAIR, COT_PAIR):
        pairs[i].wait()
    freq_lane = lax.rem(lax.broadcasted_iota(jnp.int32, (128, 128), 1), 64).astype(f32)
    inv_freq = jnp.exp(freq_lane * (-2.0 / HD * LOG_THETA))
    sign = jnp.where(lax.broadcasted_iota(jnp.int32, (128, 128), 1) < 64, -1.0, 1.0)
    t_id = lax.broadcasted_iota(jnp.int32, (128, 128), 0)
    u_id = lax.broadcasted_iota(jnp.int32, (128, 128), 1)

    def angles_of(b):
        ids = jnp.broadcast_to(r.seg[b, 0:1, :].astype(f32), (128, 128))
        same = ids == ids.T
        position = jnp.sum(jnp.where(same & (u_id < t_id), 1.0, 0.0), axis=1, keepdims=True)
        r.mask[b] = jnp.where(same & (u_id <= t_id), 1.0, 0.0)
        angles = position * inv_freq
        r.cos[128 * b : 128 * b + 128, :] = jnp.cos(angles)
        r.sin[128 * b : 128 * b + 128, :] = jnp.sin(angles) * sign

    angles_of(0)
    for name in ATTN:
        gather_forward((name, None), 1)
    for name in MLP:
        gather_start((name, None), 1, (2, 3))
    angles_of(1)
    gather_finish(("e", None), 1)
    gather_start(("e", None), 2)
    for name in ATTN:
        gather_finish((name, None), 1)
        gather_start((name, None), 2)
    for name in MLP:
        gather_forward((name, None), 1)

    unit_lane = lax.broadcasted_iota(jnp.int32, (1024, 128), 1)
    unit_row = lax.broadcasted_iota(jnp.int32, (1024, 128), 0) & 7
    r.eighths[0] = jnp.where(unit_lane == unit_row, 1.0, 0.0).astype(bf16)
    r.eighths[1] = jnp.where(unit_lane == unit_row + 8, 1.0, 0.0).astype(bf16)
    owner = lax.broadcasted_iota(jnp.int32, (128, 1024), 1) >> 3
    owned = owner == lax.broadcasted_iota(jnp.int32, (128, 1024), 0)
    pick = ((row_id == 2) & (lane_id == 16)) | ((row_id == 3) & (lane_id == 17))
    pick = jnp.where(pick, 1.0, 0.0).astype(bf16)
    gather_finish(("e", None), 2)
    table = weight["e"][...].reshape(128, 128).astype(bf16)
    for i in range(2):
        spread = jnp.where(owned, dot_nt(table, r.eighths[i]), 0.0)
        r.gain_rows[i : i + 1, :] = jnp.sum(spread, axis=0, keepdims=True)
    r.head_gains[...] = dot_nt(pick, table)
    gain_in, gain_mid = r.gain_rows.at[0:1], r.gain_rows.at[1:2]
    gain_query, gain_key = r.head_gains.at[2:3], r.head_gains.at[3:4]

    def rows_of(i, size=32):
        return pl.ds(pl.multiple_of(i * size, size), size)

    def norm_in(i):
        x = r.x[rows_of(i), :].astype(f32)
        r.normed[rows_of(i), :] = (x * inverse_rms(x) * gain_in[...]).astype(bf16)

    loop(8, norm_in)
    normed, cot = r.normed, r.cot
    for name in MLP:
        gather_finish((name, None), 1)
    for name in ATTN:
        gather_forward((name, None), 2)
    for name in MLP:
        gather_start((name, 0), 2)
    for name in MLP:
        gather_start((name, 1), 2, (0, 1))
    for name in ATTN:
        gather_finish((name, None), 2)

    def project_q(i):
        lanes = lanes_at(i * 512, 512)
        r.q_raw[:, lanes] = dot(normed[...], weight["q"][..., lanes].reshape(1024, 512))

    loop(2, project_q)
    r.k_raw[...] = dot(normed[...], weight["b"][..., :512].reshape(1024, 512))
    r.values[...] = dot(normed[...], weight["b"][..., 512:].reshape(1024, 512)).astype(bf16)

    def rotate(vector, cos_part, sin_part):
        return vector * cos_part + pltpu.roll(vector, 64, 1) * sin_part

    def turn(src, dst, gain):
        def head(h):
            lanes = lanes_at(h * 128, 128)
            raw = src[:, lanes]
            turned = rotate(raw * inverse_rms(raw) * gain[...], r.cos[...], r.sin[...])
            dst[:, lanes] = turned.astype(bf16)

        return head

    loop(8, turn(r.q_raw, r.q_rot, gain_query))
    loop(4, turn(r.k_raw, r.k_rot, gain_key))

    for name in MLP:
        gather_forward((name, 0), 2)
    for name in MLP:
        gather_start((name, 1), 2, (2, 3))
    for name in MLP:
        gather_start((name, 2), 2, (0, 1))

    def both_heads(ref, rows, m):
        first = ref[rows, lanes_at(m * 256, 128)]
        second = ref[rows, lanes_at(m * 256 + 128, 128)]
        return jnp.concatenate([first, second], axis=0)

    def attend(i):
        b, m = i // 4, lax.rem(i, 4)
        rows = pl.ds(pl.multiple_of(b * 128, 128), 128)
        lanes = lanes_at(m * 128, 128)
        scores = dot_nt(both_heads(r.q_rot, rows, m), r.k_rot[rows, lanes]) * SCALE
        mask = r.mask[b]
        masked = jnp.where(jnp.concatenate([mask, mask], axis=0) > 0.0, scores, -1e30)
        terms = jnp.exp(masked - jnp.max(masked, axis=-1, keepdims=True))
        probs = terms / jnp.sum(terms, axis=-1, keepdims=True)
        r.probs[i] = probs
        got = dot(probs.astype(bf16), r.values[rows, lanes]).astype(bf16)
        r.attended[rows, lanes_at(m * 256, 128)] = got[:128]
        r.attended[rows, lanes_at(m * 256 + 128, 128)] = got[128:]

    loop(8, attend)
    attended = r.attended

    def project_out(i):
        lanes = lanes_at(i * 512, 512)
        r.out_part[:, lanes] = dot(attended[...], weight["o"][..., lanes].reshape(1024, 512))

    loop(2, project_out)
    out_copy = to_sibling(OUT_PAIR, r.out_part, r.out_other)
    for name in MLP:
        gather_forward((name, 1), 2)
    for name in MLP:
        gather_start((name, 2), 2, (2, 3))
    out_copy.wait()

    def norm_mid(i):
        rows = rows_of(i)
        hidden = r.x[rows, :].astype(f32) + (r.out_part[rows, :] + r.out_other[rows, :])
        r.hidden[rows, :] = hidden
        r.mid_low[rows, :] = (hidden * inverse_rms(hidden) * gain_mid[...]).astype(bf16)

    loop(8, norm_mid)
    mid_low, mixed, d_gate, d_up = r.mid_low, r.mixed, r.d_gate, r.d_up

    def feed(t):
        gate = dot(mid_low[...], weight["g"][t].reshape(1024, 512))
        up = dot(mid_low[...], weight["u"][t].reshape(1024, 512))
        d_mixed = dot_nt(cot[...], weight["d"][t].reshape(512, 1024))
        sig = jax.nn.sigmoid(gate)
        act = gate * sig
        mixed[...] = (act * up).astype(bf16)
        d_gate[...] = (d_mixed * up * sig * (1.0 + gate * (1.0 - sig))).astype(bf16)
        d_up[...] = (d_mixed * act).astype(bf16)

        def mid_back(i):
            y_pair, lanes = pl.ds(2 * i, 2), lanes_at(i * 512, 512)
            got = dot_nt(d_gate[...], weight["g"][t, y_pair].reshape(512, 512))
            got += dot_nt(d_up[...], weight["u"][t, y_pair].reshape(512, 512))
            r.mid_part[:, lanes] = got if t == 0 else r.mid_part[:, lanes] + got

        def project_down(i):
            lanes = lanes_at(i * 512, 512)
            got = dot(mixed[...], weight["d"][t, ..., lanes].reshape(512, 512))
            r.down_part[:, lanes] = got if t == 0 else r.down_part[:, lanes] + got

        loop(2, mid_back)
        if t == 2:
            pairs[MID_PAIR] = to_sibling(MID_PAIR, r.mid_part, r.mid_other)
        loop(2, project_down)

    def grads(t):
        def grad_down(i):
            got = dot_tn(mixed[:, lanes_at(i * 256, 256)], cot[...]).astype(bf16)
            weight["d"][t, pl.ds(2 * i, 2)] = got.reshape(2, 4, 4, 8, 1024)

        def grad_gate(i):
            left = mid_low[:, lanes_at(i * 512, 512)]
            weight["g"][t, pl.ds(2 * i, 2)] = dot_tn(left, d_gate[...]).astype(bf16).reshape(2, 2, 4, 4, 8, 512)
            weight["u"][t, pl.ds(2 * i, 2)] = dot_tn(left, d_up[...]).astype(bf16).reshape(2, 2, 4, 4, 8, 512)

        loop(2, grad_down)
        loop(2, grad_gate)

    def sends_done(item, phases):
        for phase in phases:
            wait_for(0, item, phase, 0, 3)

    for name in MLP:
        gather_finish((name, 0), 2)
    feed(0)
    for name in MLP:
        gather_forward((name, 2), 2)
    for name in MLP:
        sends_done((name, None), (0, 1))
        sends_done((name, 0), (2,))
    grads(0)
    for name in MLP:
        sum_start((name, 0), 0)
    for name in MLP:
        gather_finish((name, 1), 2)
    feed(1)
    for name in MLP:
        sends_done((name, 1), (2,))
    grads(1)
    for name in MLP:
        sum_start((name, 1), 0)
    for name in MLP:
        gather_finish((name, 2), 2)
    feed(2)
    for name in MLP:
        sends_done((name, 2), (2,))
    grads(2)
    for name in MLP:
        sum_start((name, 2), 0)
    down_copy = to_sibling(DOWN_PAIR, r.down_part.at[other_rows], r.down_other)
    for name in MLP:
        sum_middle((name, 0), 0)
    pairs[MID_PAIR].wait()

    r.gain_sums[...] = jnp.zeros((8, 1024), f32)
    r.head_sums[...] = jnp.zeros((8, 128), f32)

    def res_back(i):
        rows = rows_of(i)
        hidden = r.hidden[rows, :]
        inverse = inverse_rms(hidden)
        unit = hidden * inverse
        part = r.mid_part[rows, :]
        r.gain_sums[1:2, :] += jnp.sum(part * unit, axis=0, keepdims=True)
        d_mid = part + r.mid_other[rows, :]
        d_res = cot[rows, :].astype(f32) + norm_backward(d_mid, unit, inverse, gain_mid[...])
        r.d_res[rows, :] = d_res
        r.d_res_low[rows, :] = d_res.astype(bf16)

    loop(8, res_back)
    d_res_low = r.d_res_low

    def attn_back(i):
        two = weight["o"][pl.ds(2 * i, 2)].reshape(512, 1024)
        r.d_attn[:, lanes_at(i * 512, 512)] = dot_nt(d_res_low[...], two).astype(bf16)

    loop(2, attn_back)
    for name in ATTN + ("e",):
        sends_done((name, None), (0, 1, 2))

    def grad_of(name, left, right):
        def rows(i):
            got = dot_tn(left[:, lanes_at(i * 512, 512)], right[...]).astype(bf16)
            weight[name][pl.ds(2 * i, 2)] = got.reshape((2,) + SHAPES[name][1:])

        loop(2, rows)

    grad_of("o", attended, d_res_low)
    sum_start(("o", None), 0)
    for name in MLP:
        sum_middle((name, 1), 0)

    def head_back(grad, raw, gain):
        inverse = inverse_rms(raw)
        unit = raw * inverse
        return jnp.sum(grad * unit, axis=0, keepdims=True), norm_backward(grad, unit, inverse, gain[...])

    def attend_back(i):
        b, m = i // 4, lax.rem(i, 4)
        rows = pl.ds(pl.multiple_of(b * 128, 128), 128)
        lanes = lanes_at(m * 128, 128)
        d_att = both_heads(r.d_attn, rows, m)
        query, key = both_heads(r.q_rot, rows, m), r.k_rot[rows, lanes]
        probs = r.probs[i]
        d_probs = dot_nt(d_att, r.values[rows, lanes])
        r.d_b[rows, lanes_at(512 + m * 128, 128)] = dot_tn(probs.astype(bf16), d_att).astype(bf16)
        d_scores = (probs * (d_probs - jnp.sum(d_probs * probs, axis=-1, keepdims=True))).astype(bf16)
        d_query = dot(d_scores, key) * SCALE
        d_key = dot_tn(d_scores, query) * SCALE
        cos_part, sin_part = r.cos[rows, :], -r.sin[rows, :]
        for j in range(2):
            spots = lanes_at(m * 256 + 128 * j, 128)
            d_unit = rotate(d_query[128 * j : 128 * j + 128], cos_part, sin_part)
            total, d_raw = head_back(d_unit, r.q_raw[rows, spots], gain_query)
            r.head_sums[2:3, :] += total
            r.d_q[rows, spots] = d_raw.astype(bf16)
        total, d_raw = head_back(rotate(d_key, cos_part, sin_part), r.k_raw[rows, lanes], gain_key)
        r.head_sums[3:4, :] += total
        r.d_b[rows, lanes] = d_raw.astype(bf16)

    loop(8, attend_back)
    for name in MLP:
        sum_middle((name, 2), 0)

    def in_back(i):
        y_pair = pl.ds(2 * i, 2)
        got = dot_nt(r.d_q[...], weight["q"][y_pair].reshape(512, 1024))
        got += dot_nt(r.d_b[...], weight["b"][y_pair].reshape(512, 1024))
        r.in_part[:, lanes_at(i * 512, 512)] = got

    loop(2, in_back)
    in_copy = to_sibling(IN_PAIR, r.in_part.at[other_rows], r.in_other)
    grad_of("q", normed, r.d_q)
    sum_start(("q", None), 0)
    grad_of("b", normed, r.d_b)
    sum_start(("b", None), 0)

    for t in range(3):
        for name in MLP:
            sum_end((name, t), 0)
    for name in MLP:
        sum_start((name, None), 1)

    def gain_back(i):
        x = r.x[rows_of(i), :].astype(f32)
        unit = x * inverse_rms(x)
        r.gain_sums[0:1, :] += jnp.sum(r.in_part[rows_of(i), :] * unit, axis=0, keepdims=True)

    loop(8, gain_back)
    table = dot_tn(r.head_sums[...].astype(bf16), pick)
    for i in range(2):
        table += dot(jnp.where(owned, r.gain_sums[i : i + 1, :], 0.0).astype(bf16), r.eighths[i])
    weight["e"][...] = table.reshape(SHAPES["e"])
    sum_start(("e", None), 0)
    sum_middle(("o", None), 0)

    stores = []

    def store(i):
        copy = pltpu.make_async_copy(out_buf[i], outputs[i], local_out.at[i])
        copy.start()
        stores.append(copy)

    down_copy.wait()

    def finish_out(i):
        rows = rows_of(i)
        mine = pl.ds(pl.multiple_of(me * 128 + i * 32, 32), 32)
        down = r.down_part[mine, :] + r.down_other[rows, :]
        layer_out[rows, :] = (r.hidden[mine, :] + down).astype(bf16)

    loop(4, finish_out)
    store(0)
    in_copy.wait()

    def finish_in(i):
        rows = rows_of(i)
        mine = pl.ds(pl.multiple_of(me * 128 + i * 32, 32), 32)
        d_normed = r.in_part[mine, :] + r.in_other[rows, :]
        x = r.x[mine, :].astype(f32)
        inverse = inverse_rms(x)
        input_grad[rows, :] = r.d_res[mine, :] + norm_backward(d_normed, x * inverse, inverse, gain_in[...])

    loop(4, finish_in)
    store(1)

    last = {}

    def swap(name):
        last[name] = to_sibling(FIN_PAIR + SPLIT.index(name), fin[name].at[1 - me], rx[name])

    for name in ("q", "b"):
        sum_middle((name, None), 0)
    for name in MLP:
        sum_middle((name, None), 1)
    sum_end(("e", None), 0)
    sum_start(("e", None), 1)
    sum_end(("o", None), 0)
    sum_start(("o", None), 1)
    for name in MLP:
        sum_end((name, None), 1)
        sum_start((name, None), 2)
    sum_end(("e", None), 1)
    sum_start(("e", None), 2)
    for name in ("q", "b"):
        sum_end((name, None), 0)
        sum_start((name, None), 1)
    sum_end(("o", None), 1)
    sum_start(("o", None), 2)
    for name in MLP:
        sum_end((name, None), 2)
    swap("g")
    swap("u")
    store(8)
    sum_end(("e", None), 2)
    swap("e")

    def unorder(name, i, out):
        last[name].wait()
        for y in range(4):
            lanes = slice(128 * y, 128 * y + 128)
            mine, theirs = rows_at(64 * i + 8 * (2 * y + me), 8), rows_at(64 * i + 8 * (2 * y + 1 - me), 8)
            for t in range(3):
                r.blocks[mine, 128 * t : 128 * t + 128] = fin[name][me, t, :, lanes]
                r.blocks[theirs, 128 * t : 128 * t + 128] = rx[name][t, :, lanes]

    unorder("g", 0, 6)
    unorder("u", 1, 7)
    rest = r.blocks[...]
    total = jnp.zeros((128, 384), f32)
    for _ in range(3):
        head = rest.astype(bf16)
        total += dot_nt(head, r.perm[...])
        rest = rest - head.astype(f32)
    for i, out in ((0, 6), (1, 7)):
        for b in range(8):
            out_buf[out][:, 384 * b : 384 * b + 384] = total[64 * i + 8 * b : 64 * i + 8 * b + 8, :]
        store(out)
    last["e"].wait()
    out_buf[9][...] = jnp.broadcast_to(fin["e"][me] + rx["e"][...], (8, 128))
    store(9)

    for name in ("q", "b"):
        sum_end((name, None), 1)
        sum_start((name, None), 2)
    sum_end(("o", None), 2)
    store(5)
    for name in ("q", "b"):
        sum_end((name, None), 2)
        swap(name)

    def place_columns(name, out, count, width, place):
        for i in range(count):
            lanes = slice(place + i * width, place + (i + 1) * width)
            out_buf[out][:, lanes_at((2 * i + me) * width, width)] = fin[name][me, :, lanes]
            out_buf[out][:, lanes_at((2 * i + 1 - me) * width, width)] = rx[name][:, lanes]
        store(out)

    last["q"].wait()
    place_columns("q", 2, 4, 256, 0)
    last["b"].wait()
    place_columns("b", 3, 4, 128, 0)
    place_columns("b", 4, 4, 128, 512)
    for item, phase in SUMS:
        wait_for(1, item, phase, 0, 3)
    for copy in stores:
        copy.wait()


def finish_kernel(*refs):
    n = len(OUTS)
    ins, outs, held, sems = refs[:n], refs[n : 2 * n + 3], refs[2 * n + 3 : -1], refs[-1]
    fetches = [pltpu.make_async_copy(ins[i], held[i], sems.at[0, i]) for i in range(n)]
    stores = [pltpu.make_async_copy(held[i], outs[i], sems.at[1, i]) for i in range(n - 1)]
    for copy in fetches:
        copy.start()
    for fetch, copy in zip(fetches, stores):
        fetch.wait()
        copy.start()
    fetches[-1].wait()
    row = held[-1][0:1, :]
    for ref, first, count in zip(outs[n - 1 :], (0, 8, 16, 17), (8, 8, 1, 1)):
        ref[...] = row[0, first : first + count]
    for copy in stores:
        copy.wait()


def body(*args):
    vmem = pl.BlockSpec(memory_space=pltpu.VMEM)
    smem = pl.BlockSpec(memory_space=pltpu.SMEM)
    hbm = pl.BlockSpec(memory_space=pl.ANY)
    outs = [jax.ShapeDtypeStruct(*entry) for entry in OUTS]
    parts = pl.pallas_call(
        layer_kernel,
        out_shape=outs,
        in_specs=[hbm, vmem, smem, hbm, hbm, hbm, smem, smem, hbm, smem, hbm, hbm, hbm, hbm],
        out_specs=[hbm] * len(OUTS),
        scratch_shapes=[pltpu.VMEM(*entry) for group in GROUPS for entry in group.values()]
        + [pltpu.SemaphoreType.DMA((len(SEMS),))]
        + [pltpu.SemaphoreType.DMA((PAIRS,))] * 2
        + [pltpu.SemaphoreType.DMA((9,)), pltpu.SemaphoreType.DMA((len(OUTS),))],
        compiler_params=pltpu.CompilerParams(
            collective_id=1, has_side_effects=True, vmem_limit_bytes=60 << 20
        ),
        name="layer",
    )(*args)
    flat = [jax.ShapeDtypeStruct((size,), f32) for size in (8, 8, 1, 1)]
    (
        layer_out, input_grad, grad_q, grad_k, grad_v, grad_o, grad_g, grad_u, grad_d, norm_gain, mlp_gain, query_gain, key_gain,
    ) = pl.pallas_call(
        finish_kernel,
        out_shape=outs[:-1] + flat,
        in_specs=[hbm] * len(OUTS),
        out_specs=[hbm] * (len(OUTS) - 1) + [vmem] * 4,
        scratch_shapes=[pltpu.VMEM(*entry) for entry in OUTS] + [pltpu.SemaphoreType.DMA((2, len(OUTS)))],
        name="finish",
    )(*parts)
    return (
        layer_out, input_grad, norm_gain, grad_q, grad_k, grad_v, query_gain, key_gain, grad_o, mlp_gain, grad_g, grad_u, grad_d,
    )


def solution(mesh):
    rows = P(("dp", "fsdp"), None)
    flat = P(("dp", "fsdp"))
    return jax.shard_map(
        body,
        mesh=mesh,
        in_specs=(rows, rows, flat, rows, rows, rows, flat, flat, rows, flat, rows, rows, rows, rows),
        out_specs=(rows, rows, flat, rows, rows, rows, flat, flat, rows, flat, rows, rows, rows),
        check_vma=False,
    )
```

```python
import types

import jax
import jax.numpy as jnp
from jax import lax
from jax.experimental import pallas as pl
from jax.experimental.pallas import tpu as pltpu
from jax.sharding import PartitionSpec as P

HD = 128
EPS = 1e-06
LOG_THETA = 13.815510557964274
SCALE = HD ** (-0.5)

bf16 = jnp.bfloat16
f32 = jnp.float32
MESH = pl.DeviceIdType.MESH

SHAPES = dict(
    q=(4, 2, 4, 4, 8, 1024),
    b=(4, 2, 4, 4, 8, 1024),
    o=(4, 4, 4, 2, 8, 1024),
    e=(4, 2, 4, 4, 1, 128),
    g=(3, 4, 2, 4, 4, 8, 512),
    u=(3, 4, 2, 4, 4, 8, 512),
    d=(3, 4, 4, 4, 8, 1024),
)
NAMES = tuple(SHAPES)
SPLIT = ("q", "b", "e", "g", "u")
ATTN = ("q", "b", "o")
MLP = ("g", "u", "d")
ORDER = dict(q="xyz", g="xyz", b="yzx", u="yzx", o="zxy", d="zxy", e="zxy")
DTYPE = {name: f32 if name == "e" else bf16 for name in NAMES}


def coords():
    dp = lax.axis_index("dp")
    fs = lax.axis_index("fsdp")
    return dict(y=dp // 2, c=lax.rem(dp, 2), z=fs // 4, x=lax.rem(fs, 4))


def device(pos, axis=None, step=0):
    pos = dict(pos)
    if axis == "c":
        pos["c"] = 1 - pos["c"]
    elif axis is not None:
        pos[axis] = lax.rem(pos[axis] + step + 4, 4)
    return (pos["y"] * 2 + pos["c"], pos["z"] * 4 + pos["x"])


def item_shape(item):
    name, third = item
    return SHAPES[name] if third is None else SHAPES[name][1:]


def lead_of(item):
    return 1 if item[0] in MLP and item[1] is None else 0


def axis_places(item):
    lead = lead_of(item)
    if item[0] in SPLIT:
        return dict(y=lead, z=lead + 2, x=lead + 3)
    return dict(y=lead, z=lead + 1, x=lead + 2)


def block(ref, item, at, half=None):
    shape = item_shape(item)
    index = [slice(None)] * len(shape)
    for axis, place in axis_places(item).items():
        if axis in at:
            start, size = at[axis] if isinstance(at[axis], tuple) else (at[axis], 1)
            index[place] = pl.ds(start, size)
    if half is not None:
        if item[0] in SPLIT:
            index[lead_of(item) + 1] = pl.ds(half, 1)
        else:
            index[-1] = pl.ds(half * (shape[-1] // 2), shape[-1] // 2)
    return ref.at[tuple(index)]


def half_of(ref, item, half):
    return block(ref, item, {}, half)


def merged(item, fixed):
    shape = list(item_shape(item))
    for axis in fixed:
        shape[axis_places(item)[axis]] = 1
    return tuple(shape)


def halved(item, shape):
    shape = list(shape)
    shape[lead_of(item) + 1 if item[0] in SPLIT else -1] //= 2
    return tuple(shape)


def add_into(dst, sources, shape):
    lead = shape[:-3]
    count = 1
    for extent in lead:
        count *= extent

    def step(i, carry):
        index, rest = [], i
        for extent in reversed(lead):
            index.append(lax.rem(rest, extent))
            rest = rest // extent
        index = tuple(reversed(index))
        total = sources[0][index].astype(f32)
        for source in sources[1:]:
            total = total + source[index].astype(f32)
        dst[index] = total.astype(dst.dtype)
        return carry

    lax.fori_loop(0, count, step, 0)


def dot(left, right):
    return jnp.dot(left, right, preferred_element_type=f32)


def dot_nt(left, right):
    return lax.dot_general(left, right, (((1,), (1,)), ((), ())), preferred_element_type=f32)


def dot_tn(left, right):
    return lax.dot_general(left, right, (((0,), (0,)), ((), ())), preferred_element_type=f32)


def inverse_rms(vector):
    return lax.rsqrt(jnp.mean(vector * vector, axis=-1, keepdims=True) + EPS)


def norm_backward(grad_in, unit_vec, inverse, gain_vec):
    scaled = grad_in * gain_vec
    return inverse * (scaled - unit_vec * jnp.mean(scaled * unit_vec, axis=-1, keepdims=True))


def lanes_at(start, size):
    return pl.ds(pl.multiple_of(start, 128), size)


def rows_at(start, size):
    return pl.ds(pl.multiple_of(start, 8), size)


def loop(count, body):
    def step(i, carry):
        body(i)
        return carry

    lax.fori_loop(0, count, step, 0)


ALL = (("q", None), ("b", None), ("o", None), ("e", None), ("g", None), ("u", None), ("d", None))
THIRDS = tuple((name, t) for t in range(3) for name in MLP)
ITEMS = ALL + THIRDS
SUMS = tuple((item, phase) for item in ALL for phase in range(3) if item[0] not in MLP or phase > 0)
SUMS += tuple((item, 0) for item in THIRDS)


def is_direct(item, phase):
    return phase == 2 or item[0] == "e" or (phase == 1 and item[0] not in MLP)


GATHERS = tuple((item, phase) for item in ALL for phase in range(3) if item[0] not in MLP or phase < 2)
GATHERS += tuple((item, 2) for item in THIRDS)
SEMS = {}
for _kind, _steps in enumerate((GATHERS, SUMS)):
    for _item, _phase in _steps:
        _direct = is_direct(_item, _phase) if _kind else _phase == 0 or _item[0] == "e"
        for _use in range(2 if _direct else 3):
            SEMS[_kind, _item, _phase, _use] = len(SEMS)
W = {name: (SHAPES[name], DTYPE[name]) for name in NAMES}
STAGE = dict(q=((8, 1024), bf16), b=((8, 1024), bf16), e=((1, 128), f32), g=((3, 8, 512), bf16), u=((3, 8, 512), bf16))
FIN = dict(q=((2, 8, 1024), f32), b=((2, 8, 1024), f32), e=((2, 1, 128), f32), g=((2, 3, 8, 512), f32), u=((2, 3, 8, 512), f32))
RX = dict(q=((8, 1024), f32), b=((8, 1024), f32), e=((1, 128), f32), g=((3, 8, 512), f32), u=((3, 8, 512), f32))
FAR, NEAR = {}, {}
for _item, _phase in SUMS:
    _shape = merged(_item, ORDER[_item[0]][::-1][: _phase + 1])
    for _way in range(2):
        NEAR[_item, _phase, _way] = (_shape, DTYPE[_item[0]])
        if not is_direct(_item, _phase):
            FAR[_item, _phase, _way] = (halved(_item, _shape), DTYPE[_item[0]])
    if is_direct(_item, _phase):
        FAR[_item, _phase, 2] = (_shape, DTYPE[_item[0]])
INS = (
    ((8, 2048), f32), ((8, 1024), f32), ((8, 1024), f32), ((16, 1024), f32), ((8, 3072), f32), ((8, 3072), f32), ((24, 1024), f32),
)
OUTS = (((128, 1024), bf16), ((128, 1024), f32)) + INS + (((8, 128), f32),)
IN_BUF = {i: entry for i, entry in enumerate(INS)}
OUT_BUF = {i: entry for i, entry in enumerate(OUTS)}
FLAT = dict(
    x=((256, 1024), bf16),
    cot=((256, 1024), bf16),
    seg=((2, 8, 128), jnp.int32),
    perm=((384, 384), bf16),
    blocks=((128, 384), f32),
    eighths=((2, 1024, 128), bf16),
    gain_rows=((8, 1024), f32),
    head_gains=((8, 128), f32),
    gain_sums=((8, 1024), f32),
    head_sums=((8, 128), f32),
    mask=((2, 128, 128), f32),
    cos=((256, 128), f32),
    sin=((256, 128), f32),
    normed=((256, 1024), bf16),
    q_raw=((256, 1024), f32),
    k_raw=((256, 512), f32),
    values=((256, 512), bf16),
    q_rot=((256, 1024), bf16),
    k_rot=((256, 512), bf16),
    probs=((8, 256, 128), f32),
    attended=((256, 1024), bf16),
    out_part=((256, 1024), f32),
    out_other=((256, 1024), f32),
    hidden=((256, 1024), f32),
    mid_low=((256, 1024), bf16),
    mixed=((256, 512), bf16),
    d_gate=((256, 512), bf16),
    d_up=((256, 512), bf16),
    down_part=((256, 1024), f32),
    down_other=((128, 1024), f32),
    mid_part=((256, 1024), f32),
    mid_other=((256, 1024), f32),
    d_res=((256, 1024), f32),
    d_res_low=((256, 1024), bf16),
    d_attn=((256, 1024), bf16),
    d_q=((256, 1024), bf16),
    d_b=((256, 1024), bf16),
    in_part=((256, 1024), f32),
    in_other=((128, 1024), f32),
)
GROUPS = (W, STAGE, FIN, RX, FAR, NEAR, IN_BUF, OUT_BUF, FLAT)
X_PAIR, COT_PAIR, SEG_PAIR, OUT_PAIR, DOWN_PAIR, MID_PAIR, IN_PAIR, STAGE_PAIR = range(8)
FIN_PAIR = STAGE_PAIR + len(SPLIT)
PAIRS = FIN_PAIR + len(SPLIT)


def layer_kernel(
    tokens, segment, norm_gain, w_query, w_key, w_value, query_gain, key_gain, w_out, mlp_gain, w_gate, w_up, w_down,
    cotangent, *refs,
):
    refs = list(refs)
    outputs = [refs.pop(0) for _ in OUTS]
    held = []
    for group in GROUPS:
        held.append({key: refs.pop(0) for key in group})
    weight, stage, fin, rx, far_of, near_of, in_buf, out_buf, flat = held
    r = types.SimpleNamespace(**flat)
    sems, pair_send, pair_recv, local_in, local_out = refs
    pos = coords()
    me = pos["c"]
    sibling = device(pos, "c")
    own_rows = pl.ds(pl.multiple_of(me * 128, 128), 128)
    other_rows = pl.ds(pl.multiple_of((1 - me) * 128, 128), 128)
    layer_out, input_grad = out_buf[0], out_buf[1]

    barrier = pltpu.get_barrier_semaphore()
    others = [sibling]
    for axis in "xyz":
        others += [device(pos, axis, step) for step in (1, -1, 2)]
    for other in others:
        pl.semaphore_signal(barrier, inc=1, device_id=other, device_id_type=MESH)
    fetches = []
    for i, src in enumerate((w_query, w_key, w_value, w_out, w_gate, w_up, w_down)):
        fetches.append(pltpu.make_async_copy(src, in_buf[i], local_in.at[i]))
    fetches.append(pltpu.make_async_copy(tokens, r.x.at[own_rows], local_in.at[7]))
    fetches.append(pltpu.make_async_copy(cotangent, r.cot.at[own_rows], local_in.at[8]))
    for copy in fetches:
        copy.start()

    def remote(src, dst, send_sem, recv_sem, target):
        return pltpu.make_async_remote_copy(
            src_ref=src, dst_ref=dst, send_sem=send_sem, recv_sem=recv_sem, device_id=target, device_id_type=MESH
        )

    def to_sibling(index, src, dst):
        copy = remote(src, dst, pair_send.at[index], pair_recv.at[index], sibling)
        copy.start()
        return copy

    def sem(kind, item, phase, use):
        return sems.at[SEMS[kind, item, phase, use]]

    def send(kind, item, phase, use, src, dst, target):
        remote(src, dst, sem(kind, item, phase, 0), sem(kind, item, phase, use), target).start()

    def wait_for(kind, item, phase, use, count):
        order = ORDER[item[0]] if kind == 0 else ORDER[item[0]][::-1]
        fixed = order[phase + 1 :] if kind == 0 else order[:phase]
        like = block(view(item), item, {**{a: pos[a] for a in fixed}, order[phase]: (0, count)})
        pltpu.make_async_copy(like, like, sem(kind, item, phase, use)).wait()

    def view(item):
        name, third = item
        return weight[name] if third is None else weight[name].at[third]

    def gather_start(item, phase, keys=(0, 1, 2, 3)):
        order = ORDER[item[0]]
        axis = order[phase]
        at = {a: pos[a] for a in order[phase:]}
        if phase == 0 or item[0] == "e":
            for step in (1, -1, 2):
                src = block(view(item), item, at)
                send(0, item, phase, 1, src, src, device(pos, axis, step))
            return
        for key, half, step in ((0, 0, 1), (1, 1, -1), (2, 1, 1), (3, 0, -1)):
            if key in keys:
                src = block(view(item), item, at, half)
                send(0, item, phase, 1 if key < 2 else 2, src, src, device(pos, axis, step))

    def gather_forward(item, phase):
        order = ORDER[item[0]]
        axis = order[phase]
        at = {a: pos[a] for a in order[phase:]}
        wait_for(0, item, phase, 1, 1)
        for half, step in ((0, 1), (1, -1)):
            src = block(view(item), item, {**at, axis: lax.rem(pos[axis] + 4 - step, 4)}, half)
            send(0, item, phase, 2, src, src, device(pos, axis, step))

    def gather_finish(item, phase):
        if phase == 0 or item[0] == "e":
            wait_for(0, item, phase, 1, 3)
        else:
            wait_for(0, item, phase, 2, 2)

    def sum_start(item, phase):
        order = ORDER[item[0]][::-1]
        axis = order[phase]
        at = {a: pos[a] for a in order[:phase]}
        ahead, behind = lax.rem(pos[axis] + 1, 4), lax.rem(pos[axis] + 3, 4)
        opposite = lax.rem(pos[axis] + 2, 4)
        up, down, across = device(pos, axis, 1), device(pos, axis, -1), device(pos, axis, 2)
        cur = view(item)
        near_up, near_down = near_of[item, phase, 0], near_of[item, phase, 1]

        def part(place, half=None):
            return block(cur, item, {**at, axis: place}, half)

        if is_direct(item, phase):
            send(1, item, phase, 1, part(opposite), far_of[item, phase, 2], across)
            send(1, item, phase, 1, part(ahead), near_up, up)
            send(1, item, phase, 1, part(behind), near_down, down)
        else:
            send(1, item, phase, 1, part(opposite, 0), far_of[item, phase, 0], up)
            send(1, item, phase, 1, part(opposite, 1), far_of[item, phase, 1], down)
            send(1, item, phase, 2, part(ahead, 1), half_of(near_up, item, 1), up)
            send(1, item, phase, 2, part(behind, 0), half_of(near_down, item, 0), down)

    def sum_middle(item, phase):
        order = ORDER[item[0]][::-1]
        axis = order[phase]
        at = {a: pos[a] for a in order[:phase]}
        shape = halved(item, merged(item, order[: phase + 1]))
        wait_for(1, item, phase, 1, 1)
        for half, step in ((0, 1), (1, -1)):
            far, near = far_of[item, phase, half], near_of[item, phase, half]
            mine = block(view(item), item, {**at, axis: lax.rem(pos[axis] + 4 + step, 4)}, half)
            add_into(far, [far, mine], shape)
            send(1, item, phase, 2, far, half_of(near, item, half), device(pos, axis, step))

    def sum_end(item, phase):
        order = ORDER[item[0]][::-1]
        at = {a: pos[a] for a in order[: phase + 1]}
        sources = [block(view(item), item, at), near_of[item, phase, 0], near_of[item, phase, 1]]
        if is_direct(item, phase):
            sources.append(far_of[item, phase, 2])
            wait_for(1, item, phase, 1, 3)
        else:
            wait_for(1, item, phase, 2, 2)
        if phase < 2:
            add_into(sources[0], sources, merged(item, order[: phase + 1]))
            return

        def total(place):
            value = sources[0][place].astype(f32)
            for source in sources[1:]:
                value = value + source[place].astype(f32)
            return value

        name = item[0]
        if name in MLP:
            for t in range(3):
                if name == "d":
                    out_buf[8][8 * t : 8 * t + 8, :] = total((t, 0, 0, 0))
                else:
                    for c in range(2):
                        fin[name][c, t] = total((t, 0, c, 0, 0))
        elif name == "o":
            for t in range(2):
                out_buf[5][8 * t : 8 * t + 8, :] = total((0, 0, 0, t))
        else:
            for c in range(2):
                fin[name][c] = total((0, c, 0, 0))

    spot = (pos["y"], me, pos["z"], pos["x"])

    def stage_columns(name, buf, start, count, width, place):
        for i in range(count):
            lanes = slice(place + i * width, place + (i + 1) * width)
            weight[name][spot + (slice(None), lanes)] = in_buf[buf][:, lanes_at((2 * i + me) * width, width)].astype(bf16)
            stage[name][:, lanes] = in_buf[buf][:, lanes_at((2 * i + 1 - me) * width, width)].astype(bf16)

    row_id = lax.broadcasted_iota(jnp.int32, (8, 128), 0)
    lane_id = lax.broadcasted_iota(jnp.int32, (8, 128), 1)
    lane_row = lax.broadcasted_iota(jnp.int32, (1, 128), 1)
    gains = jnp.zeros((1, 128), f32)
    for i in range(8):
        gains = jnp.where(lane_row == i, norm_gain[i], gains)
        gains = jnp.where(lane_row == 8 + i, mlp_gain[i], gains)
    gains = jnp.where(lane_row == 16, query_gain[0], gains)
    gains = jnp.where(lane_row == 17, key_gain[0], gains).astype(bf16).astype(f32)
    weight["e"][spot] = gains
    stage["e"][...] = gains
    r.seg[me] = jnp.broadcast_to(segment[...], (8, 128))
    for i in range(4):
        fetches[i].wait()
    stage_columns("q", 0, 0, 4, 256, 0)
    stage_columns("b", 1, 0, 4, 128, 0)
    stage_columns("b", 2, 0, 4, 128, 512)
    for t in range(2):
        weight["o"][pos["y"], pos["z"], pos["x"], t] = in_buf[3][8 * t : 8 * t + 8, :].astype(bf16)

    pl.semaphore_wait(barrier, len(others))
    pairs = {}

    def pair_start(name):
        index = STAGE_PAIR + SPLIT.index(name)
        if name in MLP:
            dst = weight[name].at[:, pos["y"], me, pos["z"], pos["x"]]
        else:
            dst = weight[name].at[spot]
        pairs[name] = to_sibling(index, stage[name], dst)

    for name in ("q", "b", "e"):
        pair_start(name)

    to_lane = lax.broadcasted_iota(jnp.int32, (384, 384), 1)
    from_lane = ((to_lane >> 3) & 15) * 24 + (to_lane >> 7) * 8 + (to_lane & 7)
    r.perm[...] = jnp.where(lax.broadcasted_iota(jnp.int32, (384, 384), 0) == from_lane, 1.0, 0.0).astype(bf16)
    for i in range(4, 7):
        fetches[i].wait()
    for i, buf in ((0, 4), (1, 5)):
        for b in range(8):
            r.blocks[64 * i + 8 * b : 64 * i + 8 * b + 8, :] = in_buf[buf][:, 384 * b : 384 * b + 384]
    r.blocks[...] = dot(r.blocks[...].astype(bf16), r.perm[...])
    for i, name in ((0, "g"), (1, "u")):
        for y in range(4):
            mine = r.blocks[rows_at(64 * i + 8 * (2 * y + me), 8), :].astype(bf16)
            theirs = r.blocks[rows_at(64 * i + 8 * (2 * y + 1 - me), 8), :].astype(bf16)
            for t in range(3):
                lanes = slice(128 * y, 128 * y + 128)
                weight[name][(t,) + spot + (slice(None), lanes)] = mine[:, 128 * t : 128 * t + 128]
                stage[name][t, :, lanes] = theirs[:, 128 * t : 128 * t + 128]
    for t in range(3):
        weight["d"][t, pos["y"], pos["z"], pos["x"]] = in_buf[6][8 * t : 8 * t + 8, :].astype(bf16)
    for name in ("g", "u"):
        pair_start(name)
    for name in ("e", "q", "b"):
        pairs[name].wait()
    for name in ("e", "q", "b", "o"):
        gather_start((name, None), 0)
    for name in ("g", "u"):
        pairs[name].wait()
    for name in MLP:
        gather_start((name, None), 0)
    fetches[7].wait()
    fetches[8].wait()
    pairs[X_PAIR] = to_sibling(X_PAIR, r.x.at[own_rows], r.x.at[own_rows])
    pairs[SEG_PAIR] = to_sibling(SEG_PAIR, r.seg.at[me], r.seg.at[me])
    pairs[COT_PAIR] = to_sibling(COT_PAIR, r.cot.at[own_rows], r.cot.at[own_rows])
    for name in ("e",) + ATTN:
        gather_finish((name, None), 0)
        gather_start((name, None), 1)
    for name in MLP:
        gather_finish((name, None), 0)
        gather_start((name, None), 1, (0, 1))

    for i in (X_PAIR, SEG_PAIR, COT_PAIR):
        pairs[i].wait()
    freq_lane = lax.rem(lax.broadcasted_iota(jnp.int32, (128, 128), 1), 64).astype(f32)
    inv_freq = jnp.exp(freq_lane * (-2.0 / HD * LOG_THETA))
    sign = jnp.where(lax.broadcasted_iota(jnp.int32, (128, 128), 1) < 64, -1.0, 1.0)
    t_id = lax.broadcasted_iota(jnp.int32, (128, 128), 0)
    u_id = lax.broadcasted_iota(jnp.int32, (128, 128), 1)

    def angles_of(b):
        ids = jnp.broadcast_to(r.seg[b, 0:1, :].astype(f32), (128, 128))
        same = ids == ids.T
        position = jnp.sum(jnp.where(same & (u_id < t_id), 1.0, 0.0), axis=1, keepdims=True)
        r.mask[b] = jnp.where(same & (u_id <= t_id), 1.0, 0.0)
        angles = position * inv_freq
        r.cos[128 * b : 128 * b + 128, :] = jnp.cos(angles)
        r.sin[128 * b : 128 * b + 128, :] = jnp.sin(angles) * sign

    angles_of(0)
    for name in ATTN:
        gather_forward((name, None), 1)
    for name in MLP:
        gather_start((name, None), 1, (2, 3))
    angles_of(1)
    gather_finish(("e", None), 1)
    gather_start(("e", None), 2)
    for name in ATTN:
        gather_finish((name, None), 1)
        gather_start((name, None), 2)
    for name in MLP:
        gather_forward((name, None), 1)

    unit_lane = lax.broadcasted_iota(jnp.int32, (1024, 128), 1)
    unit_row = lax.broadcasted_iota(jnp.int32, (1024, 128), 0) & 7
    r.eighths[0] = jnp.where(unit_lane == unit_row, 1.0, 0.0).astype(bf16)
    r.eighths[1] = jnp.where(unit_lane == unit_row + 8, 1.0, 0.0).astype(bf16)
    owner = lax.broadcasted_iota(jnp.int32, (128, 1024), 1) >> 3
    owned = owner == lax.broadcasted_iota(jnp.int32, (128, 1024), 0)
    pick = ((row_id == 2) & (lane_id == 16)) | ((row_id == 3) & (lane_id == 17))
    pick = jnp.where(pick, 1.0, 0.0).astype(bf16)
    gather_finish(("e", None), 2)
    table = weight["e"][...].reshape(128, 128).astype(bf16)
    for i in range(2):
        spread = jnp.where(owned, dot_nt(table, r.eighths[i]), 0.0)
        r.gain_rows[i : i + 1, :] = jnp.sum(spread, axis=0, keepdims=True)
    r.head_gains[...] = dot_nt(pick, table)
    gain_in, gain_mid = r.gain_rows.at[0:1], r.gain_rows.at[1:2]
    gain_query, gain_key = r.head_gains.at[2:3], r.head_gains.at[3:4]

    def rows_of(i, size=32):
        return pl.ds(pl.multiple_of(i * size, size), size)

    def norm_in(i):
        x = r.x[rows_of(i), :].astype(f32)
        r.normed[rows_of(i), :] = (x * inverse_rms(x) * gain_in[...]).astype(bf16)

    loop(8, norm_in)
    normed, cot = r.normed, r.cot
    for name in ATTN:
        gather_forward((name, None), 2)
    for name in MLP:
        gather_finish((name, None), 1)
    for name in MLP:
        gather_start((name, 0), 2)
    for name in MLP:
        gather_start((name, 1), 2, (0, 1))
    for name in ATTN:
        gather_finish((name, None), 2)

    def project_q(i):
        lanes = lanes_at(i * 512, 512)
        r.q_raw[:, lanes] = dot(normed[...], weight["q"][..., lanes].reshape(1024, 512))

    loop(2, project_q)
    r.k_raw[...] = dot(normed[...], weight["b"][..., :512].reshape(1024, 512))
    r.values[...] = dot(normed[...], weight["b"][..., 512:].reshape(1024, 512)).astype(bf16)

    def rotate(vector, cos_part, sin_part):
        return vector * cos_part + pltpu.roll(vector, 64, 1) * sin_part

    def turn(src, dst, gain):
        def head(h):
            lanes = lanes_at(h * 128, 128)
            raw = src[:, lanes]
            turned = rotate(raw * inverse_rms(raw) * gain[...], r.cos[...], r.sin[...])
            dst[:, lanes] = turned.astype(bf16)

        return head

    loop(8, turn(r.q_raw, r.q_rot, gain_query))
    loop(4, turn(r.k_raw, r.k_rot, gain_key))

    for name in MLP:
        gather_forward((name, 0), 2)
    for name in MLP:
        gather_start((name, 1), 2, (2, 3))
    for name in MLP:
        gather_start((name, 2), 2, (0, 1))

    def both_heads(ref, rows, m):
        first = ref[rows, lanes_at(m * 256, 128)]
        second = ref[rows, lanes_at(m * 256 + 128, 128)]
        return jnp.concatenate([first, second], axis=0)

    def attend(i):
        b, m = i // 4, lax.rem(i, 4)
        rows = pl.ds(pl.multiple_of(b * 128, 128), 128)
        lanes = lanes_at(m * 128, 128)
        scores = dot_nt(both_heads(r.q_rot, rows, m), r.k_rot[rows, lanes]) * SCALE
        mask = r.mask[b]
        masked = jnp.where(jnp.concatenate([mask, mask], axis=0) > 0.0, scores, -1e30)
        terms = jnp.exp(masked - jnp.max(masked, axis=-1, keepdims=True))
        probs = terms / jnp.sum(terms, axis=-1, keepdims=True)
        r.probs[i] = probs
        got = dot(probs.astype(bf16), r.values[rows, lanes]).astype(bf16)
        r.attended[rows, lanes_at(m * 256, 128)] = got[:128]
        r.attended[rows, lanes_at(m * 256 + 128, 128)] = got[128:]

    loop(8, attend)
    attended = r.attended

    def project_out(i):
        lanes = lanes_at(i * 512, 512)
        r.out_part[:, lanes] = dot(attended[...], weight["o"][..., lanes].reshape(1024, 512))

    loop(2, project_out)
    out_copy = to_sibling(OUT_PAIR, r.out_part, r.out_other)
    for name in MLP:
        gather_forward((name, 1), 2)
    for name in MLP:
        gather_start((name, 2), 2, (2, 3))
    out_copy.wait()

    def norm_mid(i):
        rows = rows_of(i)
        hidden = r.x[rows, :].astype(f32) + (r.out_part[rows, :] + r.out_other[rows, :])
        r.hidden[rows, :] = hidden
        r.mid_low[rows, :] = (hidden * inverse_rms(hidden) * gain_mid[...]).astype(bf16)

    loop(8, norm_mid)
    mid_low, mixed, d_gate, d_up = r.mid_low, r.mixed, r.d_gate, r.d_up

    def feed(t):
        gate = dot(mid_low[...], weight["g"][t].reshape(1024, 512))
        up = dot(mid_low[...], weight["u"][t].reshape(1024, 512))
        d_mixed = dot_nt(cot[...], weight["d"][t].reshape(512, 1024))
        sig = jax.nn.sigmoid(gate)
        act = gate * sig
        mixed[...] = (act * up).astype(bf16)
        d_gate[...] = (d_mixed * up * sig * (1.0 + gate * (1.0 - sig))).astype(bf16)
        d_up[...] = (d_mixed * act).astype(bf16)

        def mid_back(i):
            y_pair, lanes = pl.ds(2 * i, 2), lanes_at(i * 512, 512)
            got = dot_nt(d_gate[...], weight["g"][t, y_pair].reshape(512, 512))
            got += dot_nt(d_up[...], weight["u"][t, y_pair].reshape(512, 512))
            r.mid_part[:, lanes] = got if t == 0 else r.mid_part[:, lanes] + got

        def project_down(i):
            lanes = lanes_at(i * 512, 512)
            got = dot(mixed[...], weight["d"][t, ..., lanes].reshape(512, 512))
            r.down_part[:, lanes] = got if t == 0 else r.down_part[:, lanes] + got

        loop(2, mid_back)
        if t == 2:
            pairs[MID_PAIR] = to_sibling(MID_PAIR, r.mid_part, r.mid_other)
        loop(2, project_down)

    def grads(t):
        def grad_down(i):
            got = dot_tn(mixed[:, lanes_at(i * 256, 256)], cot[...]).astype(bf16)
            weight["d"][t, pl.ds(2 * i, 2)] = got.reshape(2, 4, 4, 8, 1024)

        def grad_gate(i):
            left = mid_low[:, lanes_at(i * 512, 512)]
            weight["g"][t, pl.ds(2 * i, 2)] = dot_tn(left, d_gate[...]).astype(bf16).reshape(2, 2, 4, 4, 8, 512)
            weight["u"][t, pl.ds(2 * i, 2)] = dot_tn(left, d_up[...]).astype(bf16).reshape(2, 2, 4, 4, 8, 512)

        loop(2, grad_down)
        loop(2, grad_gate)

    def sends_done(item, phases):
        for phase in phases:
            wait_for(0, item, phase, 0, 3)

    for name in MLP:
        gather_finish((name, 0), 2)
    feed(0)
    for name in MLP:
        gather_forward((name, 2), 2)
    for name in MLP:
        sends_done((name, None), (0, 1))
        sends_done((name, 0), (2,))
    grads(0)
    for name in MLP:
        sum_start((name, 0), 0)
    for name in MLP:
        gather_finish((name, 1), 2)
    feed(1)
    for name in MLP:
        sends_done((name, 1), (2,))
    grads(1)
    for name in MLP:
        sum_start((name, 1), 0)
    for name in MLP:
        gather_finish((name, 2), 2)
    feed(2)
    for name in MLP:
        sends_done((name, 2), (2,))
    grads(2)
    for name in MLP:
        sum_start((name, 2), 0)
    down_copy = to_sibling(DOWN_PAIR, r.down_part.at[other_rows], r.down_other)
    for name in MLP:
        sum_middle((name, 0), 0)
    pairs[MID_PAIR].wait()

    r.gain_sums[...] = jnp.zeros((8, 1024), f32)
    r.head_sums[...] = jnp.zeros((8, 128), f32)

    def res_back(i):
        rows = rows_of(i)
        hidden = r.hidden[rows, :]
        inverse = inverse_rms(hidden)
        unit = hidden * inverse
        part = r.mid_part[rows, :]
        r.gain_sums[1:2, :] += jnp.sum(part * unit, axis=0, keepdims=True)
        d_mid = part + r.mid_other[rows, :]
        d_res = cot[rows, :].astype(f32) + norm_backward(d_mid, unit, inverse, gain_mid[...])
        r.d_res[rows, :] = d_res
        r.d_res_low[rows, :] = d_res.astype(bf16)

    loop(8, res_back)
    d_res_low = r.d_res_low

    def attn_back(i):
        two = weight["o"][pl.ds(2 * i, 2)].reshape(512, 1024)
        r.d_attn[:, lanes_at(i * 512, 512)] = dot_nt(d_res_low[...], two).astype(bf16)

    loop(2, attn_back)
    for name in ATTN + ("e",):
        sends_done((name, None), (0, 1, 2))

    def grad_of(name, left, right):
        def rows(i):
            got = dot_tn(left[:, lanes_at(i * 512, 512)], right[...]).astype(bf16)
            weight[name][pl.ds(2 * i, 2)] = got.reshape((2,) + SHAPES[name][1:])

        loop(2, rows)

    grad_of("o", attended, d_res_low)
    for name in MLP:
        sum_middle((name, 1), 0)

    def head_back(grad, raw, gain):
        inverse = inverse_rms(raw)
        unit = raw * inverse
        return jnp.sum(grad * unit, axis=0, keepdims=True), norm_backward(grad, unit, inverse, gain[...])

    def attend_back(i):
        b, m = i // 4, lax.rem(i, 4)
        rows = pl.ds(pl.multiple_of(b * 128, 128), 128)
        lanes = lanes_at(m * 128, 128)
        d_att = both_heads(r.d_attn, rows, m)
        query, key = both_heads(r.q_rot, rows, m), r.k_rot[rows, lanes]
        probs = r.probs[i]
        d_probs = dot_nt(d_att, r.values[rows, lanes])
        r.d_b[rows, lanes_at(512 + m * 128, 128)] = dot_tn(probs.astype(bf16), d_att).astype(bf16)
        d_scores = (probs * (d_probs - jnp.sum(d_probs * probs, axis=-1, keepdims=True))).astype(bf16)
        d_query = dot(d_scores, key) * SCALE
        d_key = dot_tn(d_scores, query) * SCALE
        cos_part, sin_part = r.cos[rows, :], -r.sin[rows, :]
        for j in range(2):
            spots = lanes_at(m * 256 + 128 * j, 128)
            d_unit = rotate(d_query[128 * j : 128 * j + 128], cos_part, sin_part)
            total, d_raw = head_back(d_unit, r.q_raw[rows, spots], gain_query)
            r.head_sums[2:3, :] += total
            r.d_q[rows, spots] = d_raw.astype(bf16)
        total, d_raw = head_back(rotate(d_key, cos_part, sin_part), r.k_raw[rows, lanes], gain_key)
        r.head_sums[3:4, :] += total
        r.d_b[rows, lanes] = d_raw.astype(bf16)

    loop(8, attend_back)
    for name in MLP:
        sum_middle((name, 2), 0)
    sum_start(("o", None), 0)

    def in_back(i):
        y_pair = pl.ds(2 * i, 2)
        got = dot_nt(r.d_q[...], weight["q"][y_pair].reshape(512, 1024))
        got += dot_nt(r.d_b[...], weight["b"][y_pair].reshape(512, 1024))
        r.in_part[:, lanes_at(i * 512, 512)] = got

    loop(2, in_back)
    in_copy = to_sibling(IN_PAIR, r.in_part.at[other_rows], r.in_other)
    grad_of("q", normed, r.d_q)
    sum_start(("q", None), 0)
    grad_of("b", normed, r.d_b)
    sum_start(("b", None), 0)

    def gain_back(i):
        x = r.x[rows_of(i), :].astype(f32)
        unit = x * inverse_rms(x)
        r.gain_sums[0:1, :] += jnp.sum(r.in_part[rows_of(i), :] * unit, axis=0, keepdims=True)

    loop(8, gain_back)
    table = dot_tn(r.head_sums[...].astype(bf16), pick)
    for i in range(2):
        table += dot(jnp.where(owned, r.gain_sums[i : i + 1, :], 0.0).astype(bf16), r.eighths[i])
    weight["e"][...] = table.reshape(SHAPES["e"])
    sum_start(("e", None), 0)

    stores = []

    def store(i):
        copy = pltpu.make_async_copy(out_buf[i], outputs[i], local_out.at[i])
        copy.start()
        stores.append(copy)

    down_copy.wait()

    def finish_out(i):
        rows = rows_of(i)
        mine = pl.ds(pl.multiple_of(me * 128 + i * 32, 32), 32)
        down = r.down_part[mine, :] + r.down_other[rows, :]
        layer_out[rows, :] = (r.hidden[mine, :] + down).astype(bf16)

    loop(4, finish_out)
    store(0)
    for t in range(3):
        for name in MLP:
            sum_end((name, t), 0)
    in_copy.wait()

    def finish_in(i):
        rows = rows_of(i)
        mine = pl.ds(pl.multiple_of(me * 128 + i * 32, 32), 32)
        d_normed = r.in_part[mine, :] + r.in_other[rows, :]
        x = r.x[mine, :].astype(f32)
        inverse = inverse_rms(x)
        input_grad[rows, :] = r.d_res[mine, :] + norm_backward(d_normed, x * inverse, inverse, gain_in[...])

    loop(4, finish_in)
    store(1)

    last = {}

    def swap(name):
        last[name] = to_sibling(FIN_PAIR + SPLIT.index(name), fin[name].at[1 - me], rx[name])

    for name in ATTN:
        sum_middle((name, None), 0)
    for name in MLP:
        sum_start((name, None), 1)
    sum_end(("e", None), 0)
    sum_start(("e", None), 1)
    for name in ATTN:
        sum_end((name, None), 0)
        sum_start((name, None), 1)
    for name in MLP:
        sum_middle((name, None), 1)
    sum_end(("e", None), 1)
    sum_start(("e", None), 2)
    for name in ATTN:
        sum_end((name, None), 1)
        sum_start((name, None), 2)
    for name in MLP:
        sum_end((name, None), 1)
        sum_start((name, None), 2)
    sum_end(("e", None), 2)
    swap("e")
    for name in ATTN:
        sum_end((name, None), 2)
        if name != "o":
            swap(name)
    store(5)
    for name in MLP:
        sum_end((name, None), 2)
        if name != "d":
            swap(name)
    store(8)

    def unorder(name, i, out):
        last[name].wait()
        for y in range(4):
            lanes = slice(128 * y, 128 * y + 128)
            mine, theirs = rows_at(64 * i + 8 * (2 * y + me), 8), rows_at(64 * i + 8 * (2 * y + 1 - me), 8)
            for t in range(3):
                r.blocks[mine, 128 * t : 128 * t + 128] = fin[name][me, t, :, lanes]
                r.blocks[theirs, 128 * t : 128 * t + 128] = rx[name][t, :, lanes]

    def place_columns(name, out, count, width, place):
        for i in range(count):
            lanes = slice(place + i * width, place + (i + 1) * width)
            out_buf[out][:, lanes_at((2 * i + me) * width, width)] = fin[name][me, :, lanes]
            out_buf[out][:, lanes_at((2 * i + 1 - me) * width, width)] = rx[name][:, lanes]
        store(out)

    last["q"].wait()
    place_columns("q", 2, 4, 256, 0)
    last["b"].wait()
    place_columns("b", 3, 4, 128, 0)
    place_columns("b", 4, 4, 128, 512)
    unorder("g", 0, 6)
    unorder("u", 1, 7)
    rest = r.blocks[...]
    total = jnp.zeros((128, 384), f32)
    for _ in range(3):
        head = rest.astype(bf16)
        total += dot_nt(head, r.perm[...])
        rest = rest - head.astype(f32)
    for i, out in ((0, 6), (1, 7)):
        for b in range(8):
            out_buf[out][:, 384 * b : 384 * b + 384] = total[64 * i + 8 * b : 64 * i + 8 * b + 8, :]
        store(out)
    last["e"].wait()
    out_buf[9][...] = jnp.broadcast_to(fin["e"][me] + rx["e"][...], (8, 128))
    store(9)

    for item, phase in SUMS:
        wait_for(1, item, phase, 0, 3)
    for copy in stores:
        copy.wait()


def finish_kernel(*refs):
    n = len(OUTS)
    ins, outs, held, sems = refs[:n], refs[n : 2 * n + 3], refs[2 * n + 3 : -1], refs[-1]
    fetches = [pltpu.make_async_copy(ins[i], held[i], sems.at[0, i]) for i in range(n)]
    stores = [pltpu.make_async_copy(held[i], outs[i], sems.at[1, i]) for i in range(n - 1)]
    for copy in fetches:
        copy.start()
    for fetch, copy in zip(fetches, stores):
        fetch.wait()
        copy.start()
    fetches[-1].wait()
    row = held[-1][0:1, :]
    for ref, first, count in zip(outs[n - 1 :], (0, 8, 16, 17), (8, 8, 1, 1)):
        ref[...] = row[0, first : first + count]
    for copy in stores:
        copy.wait()


def body(*args):
    vmem = pl.BlockSpec(memory_space=pltpu.VMEM)
    smem = pl.BlockSpec(memory_space=pltpu.SMEM)
    hbm = pl.BlockSpec(memory_space=pl.ANY)
    outs = [jax.ShapeDtypeStruct(*entry) for entry in OUTS]
    parts = pl.pallas_call(
        layer_kernel,
        out_shape=outs,
        in_specs=[hbm, vmem, smem, hbm, hbm, hbm, smem, smem, hbm, smem, hbm, hbm, hbm, hbm],
        out_specs=[hbm] * len(OUTS),
        scratch_shapes=[pltpu.VMEM(*entry) for group in GROUPS for entry in group.values()]
        + [pltpu.SemaphoreType.DMA((len(SEMS),))]
        + [pltpu.SemaphoreType.DMA((PAIRS,))] * 2
        + [pltpu.SemaphoreType.DMA((9,)), pltpu.SemaphoreType.DMA((len(OUTS),))],
        compiler_params=pltpu.CompilerParams(
            collective_id=1, has_side_effects=True, vmem_limit_bytes=60 << 20
        ),
        name="layer",
    )(*args)
    flat = [jax.ShapeDtypeStruct((size,), f32) for size in (8, 8, 1, 1)]
    (
        layer_out, input_grad, grad_q, grad_k, grad_v, grad_o, grad_g, grad_u, grad_d, norm_gain, mlp_gain, query_gain, key_gain,
    ) = pl.pallas_call(
        finish_kernel,
        out_shape=outs[:-1] + flat,
        in_specs=[hbm] * len(OUTS),
        out_specs=[hbm] * (len(OUTS) - 1) + [vmem] * 4,
        scratch_shapes=[pltpu.VMEM(*entry) for entry in OUTS] + [pltpu.SemaphoreType.DMA((2, len(OUTS)))],
        name="finish",
    )(*parts)
    return (
        layer_out, input_grad, norm_gain, grad_q, grad_k, grad_v, query_gain, key_gain, grad_o, mlp_gain, grad_g, grad_u, grad_d,
    )


def solution(mesh):
    rows = P(("dp", "fsdp"), None)
    flat = P(("dp", "fsdp"))
    return jax.shard_map(
        body,
        mesh=mesh,
        in_specs=(rows, rows, flat, rows, rows, rows, flat, flat, rows, flat, rows, rows, rows, rows),
        out_specs=(rows, rows, flat, rows, rows, rows, flat, flat, rows, flat, rows, rows, rows),
        check_vma=False,
    )
```

```python
import types

import jax
import jax.numpy as jnp
from jax import lax
from jax.experimental import pallas as pl
from jax.experimental.pallas import tpu as pltpu
from jax.sharding import PartitionSpec as P

HD = 128
EPS = 1e-06
LOG_THETA = 13.815510557964274
SCALE = HD ** (-0.5)

bf16 = jnp.bfloat16
f32 = jnp.float32
MESH = pl.DeviceIdType.MESH

SHAPES = dict(
    q=(4, 2, 4, 4, 8, 1024),
    b=(4, 2, 4, 4, 8, 1024),
    o=(4, 4, 4, 2, 8, 1024),
    e=(4, 2, 4, 4, 1, 128),
    g=(3, 4, 2, 4, 4, 8, 512),
    u=(3, 4, 2, 4, 4, 8, 512),
    d=(3, 4, 4, 4, 8, 1024),
)
NAMES = tuple(SHAPES)
SPLIT = ("q", "b", "e", "g", "u")
CROSS = ("q", "b", "g", "u")
ATTN = ("q", "b", "o")
MLP = ("g", "u", "d")
ORDER = dict(q="xyz", g="xyz", b="yzx", u="yzx", o="zxy", d="zxy", e="zxy")
DTYPE = {name: f32 if name == "e" else bf16 for name in NAMES}


def coords():
    dp = lax.axis_index("dp")
    fs = lax.axis_index("fsdp")
    return dict(y=dp // 2, c=lax.rem(dp, 2), z=fs // 4, x=lax.rem(fs, 4))


def device(pos, axis=None, step=0):
    pos = dict(pos)
    if axis == "c":
        pos["c"] = 1 - pos["c"]
    elif axis is not None:
        pos[axis] = lax.rem(pos[axis] + step + 4, 4)
    return (pos["y"] * 2 + pos["c"], pos["z"] * 4 + pos["x"])


def item_shape(item):
    name, third = item
    return SHAPES[name] if third is None else SHAPES[name][1:]


def lead_of(item):
    return 1 if item[0] in MLP and item[1] is None else 0


def axis_places(item):
    lead = lead_of(item)
    if item[0] in SPLIT:
        return dict(y=lead, z=lead + 2, x=lead + 3)
    return dict(y=lead, z=lead + 1, x=lead + 2)


def block(ref, item, at, half=None):
    shape = item_shape(item)
    index = [slice(None)] * len(shape)
    for axis, place in axis_places(item).items():
        if axis in at:
            start, size = at[axis] if isinstance(at[axis], tuple) else (at[axis], 1)
            index[place] = pl.ds(start, size)
    if half is not None:
        if item[0] in SPLIT:
            index[lead_of(item) + 1] = pl.ds(half, 1)
        else:
            index[-1] = pl.ds(half * (shape[-1] // 2), shape[-1] // 2)
    return ref.at[tuple(index)]


def half_of(ref, item, half):
    return block(ref, item, {}, half)


def merged(item, fixed):
    shape = list(item_shape(item))
    for axis in fixed:
        shape[axis_places(item)[axis]] = 1
    return tuple(shape)


def halved(item, shape):
    shape = list(shape)
    shape[lead_of(item) + 1 if item[0] in SPLIT else -1] //= 2
    return tuple(shape)


def add_into(dst, sources, shape):
    lead = shape[:-3]
    count = 1
    for extent in lead:
        count *= extent

    def step(i, carry):
        index, rest = [], i
        for extent in reversed(lead):
            index.append(lax.rem(rest, extent))
            rest = rest // extent
        index = tuple(reversed(index))
        total = sources[0][index].astype(f32)
        for source in sources[1:]:
            total = total + source[index].astype(f32)
        dst[index] = total.astype(dst.dtype)
        return carry

    lax.fori_loop(0, count, step, 0)


def dot(left, right):
    return jnp.dot(left, right, preferred_element_type=f32)


def dot_nt(left, right):
    return lax.dot_general(left, right, (((1,), (1,)), ((), ())), preferred_element_type=f32)


def dot_tn(left, right):
    return lax.dot_general(left, right, (((0,), (0,)), ((), ())), preferred_element_type=f32)


def inverse_rms(vector):
    return lax.rsqrt(jnp.mean(vector * vector, axis=-1, keepdims=True) + EPS)


def norm_backward(grad_in, unit_vec, inverse, gain_vec):
    scaled = grad_in * gain_vec
    return inverse * (scaled - unit_vec * jnp.mean(scaled * unit_vec, axis=-1, keepdims=True))


def lanes_at(start, size):
    return pl.ds(pl.multiple_of(start, 128), size)


def rows_at(start, size):
    return pl.ds(pl.multiple_of(start, 8), size)


def loop(count, body):
    def step(i, carry):
        body(i)
        return carry

    lax.fori_loop(0, count, step, 0)


ALL = (("q", None), ("b", None), ("o", None), ("e", None), ("g", None), ("u", None), ("d", None))
THIRDS = tuple((name, t) for t in range(3) for name in MLP)
ITEMS = ALL + THIRDS
SUMS = tuple((item, phase) for item in ALL for phase in range(3) if item[0] not in MLP or phase > 0)
SUMS += tuple((item, 0) for item in THIRDS)


def is_direct(item, phase):
    return phase == 2 or item[0] == "e"


GATHERS = tuple((item, phase) for item in ALL for phase in range(3) if item[0] not in MLP or phase < 2)
GATHERS += tuple((item, 2) for item in THIRDS)
SEMS = {}
for _kind, _steps in enumerate((GATHERS, SUMS)):
    for _item, _phase in _steps:
        _direct = is_direct(_item, _phase) if _kind else _phase == 0 or _item[0] == "e"
        for _use in range(2 if _direct else 3):
            SEMS[_kind, _item, _phase, _use] = len(SEMS)
W = {name: (SHAPES[name], DTYPE[name]) for name in NAMES}
ROWS = {name: halved((name, None), merged((name, None), ORDER[name])) for name in CROSS}
STAGE = {name: (ROWS[name], bf16) for name in CROSS}
RX = {name: (ROWS[name], bf16) for name in CROSS}
STAGE["e"] = RX["e"] = ((1, 128), f32)
FIN = dict(e=((2, 1, 128), f32))
FAR, NEAR = {}, {}
for _item, _phase in SUMS:
    _shape = merged(_item, ORDER[_item[0]][::-1][: _phase + 1])
    for _way in range(2):
        NEAR[_item, _phase, _way] = (_shape, DTYPE[_item[0]])
        if not is_direct(_item, _phase):
            FAR[_item, _phase, _way] = (halved(_item, _shape), DTYPE[_item[0]])
    if is_direct(_item, _phase):
        FAR[_item, _phase, 2] = (_shape, DTYPE[_item[0]])
INS = (
    ((8, 2048), f32), ((8, 1024), f32), ((8, 1024), f32), ((16, 1024), f32), ((8, 3072), f32), ((8, 3072), f32), ((24, 1024), f32),
)
OUTS = (((128, 1024), bf16), ((128, 1024), f32)) + INS + tuple(((size,), f32) for size in (8, 8, 1, 1))
IN_BUF = {i: entry for i, entry in enumerate(INS)}
FLAT = dict(
    x=((256, 1024), bf16),
    cot=((256, 1024), bf16),
    seg=((2, 8, 128), jnp.int32),
    seg_in=((1, 128), jnp.int32),
    perm=((384, 384), bf16),
    blocks=((128, 384), f32),
    eighths=((2, 1024, 128), bf16),
    gain_rows=((8, 1024), f32),
    head_gains=((8, 128), f32),
    gain_sums=((8, 1024), f32),
    head_sums=((8, 128), f32),
    mask=((2, 128, 128), f32),
    cos=((256, 128), f32),
    sin=((256, 128), f32),
    normed=((256, 1024), bf16),
    q_raw=((256, 1024), f32),
    k_raw=((256, 512), f32),
    values=((256, 512), bf16),
    q_rot=((256, 1024), bf16),
    k_rot=((256, 512), bf16),
    probs=((8, 256, 128), f32),
    attended=((256, 1024), bf16),
    out_part=((256, 1024), f32),
    out_other=((256, 1024), f32),
    hidden=((256, 1024), f32),
    mid_low=((256, 1024), bf16),
    mixed=((256, 512), bf16),
    d_gate=((256, 512), bf16),
    d_up=((256, 512), bf16),
    down_part=((256, 1024), f32),
    down_other=((128, 1024), f32),
    mid_part=((256, 1024), f32),
    mid_other=((256, 1024), f32),
    d_res=((256, 1024), f32),
    d_res_low=((256, 1024), bf16),
    d_attn=((256, 1024), bf16),
    d_q=((256, 1024), bf16),
    d_b=((256, 1024), bf16),
    in_part=((256, 1024), f32),
    in_other=((128, 1024), f32),
)
GROUPS = (W, STAGE, FIN, RX, FAR, NEAR, IN_BUF, FLAT)
X_PAIR, COT_PAIR, SEG_PAIR, OUT_PAIR, DOWN_PAIR, MID_PAIR, IN_PAIR, STAGE_PAIR = range(8)
FIN_PAIR = STAGE_PAIR + len(SPLIT)
PAIRS = FIN_PAIR + len(SPLIT)


def layer_kernel(
    tokens, segment, norm_gain, w_query, w_key, w_value, query_gain, key_gain, w_out, mlp_gain, w_gate, w_up, w_down,
    cotangent, *refs,
):
    refs = list(refs)
    out_buf = [refs.pop(0) for _ in OUTS]
    held = []
    for group in GROUPS:
        held.append({key: refs.pop(0) for key in group})
    weight, stage, fin, rx, far_of, near_of, in_buf, flat = held
    r = types.SimpleNamespace(**flat)
    gains_in, (sems, pair_send, pair_recv, local_in) = refs[:4], refs[4:]
    pos = coords()
    me = pos["c"]
    sibling = device(pos, "c")
    flipped = dict(pos, c=1 - me)
    own_rows = pl.ds(pl.multiple_of(me * 128, 128), 128)
    other_rows = pl.ds(pl.multiple_of((1 - me) * 128, 128), 128)
    layer_out, input_grad = out_buf[0], out_buf[1]

    barrier = pltpu.get_barrier_semaphore()
    others = [sibling]
    for axis in "xyz":
        others += [device(pos, axis, step) for step in (1, -1, 2)]
    for axis in "xy":
        others += [device(flipped, axis, step) for step in (1, -1, 2)]
    for other in others:
        pl.semaphore_signal(barrier, inc=1, device_id=other, device_id_type=MESH)
    fetches = []
    for i, src in enumerate((w_query, w_key, w_value, w_out, w_gate, w_up, w_down)):
        fetches.append(pltpu.make_async_copy(src, in_buf[i], local_in.at[i]))
    fetches.append(pltpu.make_async_copy(tokens, r.x.at[own_rows], local_in.at[7]))
    fetches.append(pltpu.make_async_copy(cotangent, r.cot.at[own_rows], local_in.at[8]))
    small = ((norm_gain, gains_in[0]), (mlp_gain, gains_in[1]), (query_gain, gains_in[2]), (key_gain, gains_in[3]), (segment, r.seg_in))
    for i, (src, dst) in enumerate(small):
        fetches.append(pltpu.make_async_copy(src, dst, local_in.at[9 + i]))
    for copy in fetches[9:] + fetches[:9]:
        copy.start()
    norm_gain, mlp_gain, query_gain, key_gain = gains_in

    def remote(src, dst, send_sem, recv_sem, target):
        return pltpu.make_async_remote_copy(
            src_ref=src, dst_ref=dst, send_sem=send_sem, recv_sem=recv_sem, device_id=target, device_id_type=MESH
        )

    def to_sibling(index, src, dst):
        copy = remote(src, dst, pair_send.at[index], pair_recv.at[index], sibling)
        copy.start()
        return copy

    def sem(kind, item, phase, use):
        return sems.at[SEMS[kind, item, phase, use]]

    def send(kind, item, phase, use, src, dst, target):
        remote(src, dst, sem(kind, item, phase, 0), sem(kind, item, phase, use), target).start()

    def wait_for(kind, item, phase, use, count):
        order = ORDER[item[0]] if kind == 0 else ORDER[item[0]][::-1]
        fixed = order[phase + 1 :] if kind == 0 else order[:phase]
        like = block(view(item), item, {**{a: pos[a] for a in fixed}, order[phase]: (0, count)})
        pltpu.make_async_copy(like, like, sem(kind, item, phase, use)).wait()

    def view(item):
        name, third = item
        return weight[name] if third is None else weight[name].at[third]

    pairs = {}

    def gather_start(item, phase, keys=(0, 1, 2, 3)):
        order = ORDER[item[0]]
        axis = order[phase]
        at = {a: pos[a] for a in order[phase:]}
        if phase == 0 and item[0] in CROSS:
            mine = block(view(item), item, at, me)
            for step in (1, -1, 2):
                send(0, item, phase, 1, mine, mine, device(pos, axis, step))
                send(0, item, phase, 1, stage[item[0]], mine, device(flipped, axis, step))
            return
        if phase == 0 or item[0] == "e":
            for step in (1, -1, 2):
                src = block(view(item), item, at)
                send(0, item, phase, 1, src, src, device(pos, axis, step))
            return
        for key, half, step in ((0, 0, 1), (1, 1, -1), (2, 1, 1), (3, 0, -1)):
            if key in keys:
                src = block(view(item), item, at, half)
                send(0, item, phase, 1 if key < 2 else 2, src, src, device(pos, axis, step))

    def gather_forward(item, phase):
        order = ORDER[item[0]]
        axis = order[phase]
        at = {a: pos[a] for a in order[phase:]}
        wait_for(0, item, phase, 1, 1)
        for half, step in ((0, 1), (1, -1)):
            src = block(view(item), item, {**at, axis: lax.rem(pos[axis] + 4 - step, 4)}, half)
            send(0, item, phase, 2, src, src, device(pos, axis, step))

    def gather_finish(item, phase):
        if phase == 0 or item[0] == "e":
            wait_for(0, item, phase, 1, 3)
        else:
            wait_for(0, item, phase, 2, 2)

    def sum_start(item, phase):
        order = ORDER[item[0]][::-1]
        axis = order[phase]
        at = {a: pos[a] for a in order[:phase]}
        ahead, behind = lax.rem(pos[axis] + 1, 4), lax.rem(pos[axis] + 3, 4)
        opposite = lax.rem(pos[axis] + 2, 4)
        up, down, across = device(pos, axis, 1), device(pos, axis, -1), device(pos, axis, 2)
        cur = view(item)
        near_up, near_down = near_of[item, phase, 0], near_of[item, phase, 1]

        def part(place, half=None):
            return block(cur, item, {**at, axis: place}, half)

        if phase == 2 and item[0] in CROSS:
            ways = ((opposite, far_of[item, phase, 2], 2), (ahead, near_up, 1), (behind, near_down, -1))
            for place, dst, step in ways:
                slot = half_of(dst, item, me)
                send(1, item, phase, 1, part(place, me), slot, device(pos, axis, step))
                send(1, item, phase, 1, part(place, 1 - me), slot, device(flipped, axis, step))
            index = FIN_PAIR + SPLIT.index(item[0])
            pairs[index] = to_sibling(index, block(cur, item, pos, 1 - me), rx[item[0]])
        elif is_direct(item, phase):
            send(1, item, phase, 1, part(opposite), far_of[item, phase, 2], across)
            send(1, item, phase, 1, part(ahead), near_up, up)
            send(1, item, phase, 1, part(behind), near_down, down)
        else:
            send(1, item, phase, 1, part(opposite, 0), far_of[item, phase, 0], up)
            send(1, item, phase, 1, part(opposite, 1), far_of[item, phase, 1], down)
            send(1, item, phase, 2, part(ahead, 1), half_of(near_up, item, 1), up)
            send(1, item, phase, 2, part(behind, 0), half_of(near_down, item, 0), down)

    def sum_middle(item, phase):
        order = ORDER[item[0]][::-1]
        axis = order[phase]
        at = {a: pos[a] for a in order[:phase]}
        shape = halved(item, merged(item, order[: phase + 1]))
        wait_for(1, item, phase, 1, 1)
        for half, step in ((0, 1), (1, -1)):
            far, near = far_of[item, phase, half], near_of[item, phase, half]
            mine = block(view(item), item, {**at, axis: lax.rem(pos[axis] + 4 + step, 4)}, half)
            add_into(far, [far, mine], shape)
            send(1, item, phase, 2, far, half_of(near, item, half), device(pos, axis, step))

    def sum_end(item, phase):
        order = ORDER[item[0]][::-1]
        at = {a: pos[a] for a in order[: phase + 1]}
        sources = [block(view(item), item, at), near_of[item, phase, 0], near_of[item, phase, 1]]
        if is_direct(item, phase):
            sources.append(far_of[item, phase, 2])
            wait_for(1, item, phase, 1, 3)
        else:
            wait_for(1, item, phase, 2, 2)
        if phase < 2:
            add_into(sources[0], sources, merged(item, order[: phase + 1]))
            return

        name = item[0]

        def total(place, first=None):
            value = (sources[0] if first is None else first)[place].astype(f32)
            for source in sources[1:]:
                value = value + source[place].astype(f32)
            return value

        def both(t):
            lead = () if t is None else (t,)
            mine = total(lead + (0, me, 0, 0))
            theirs = rx[name][lead + (0, 0, 0, 0)].astype(f32)
            for source in sources[1:]:
                theirs = theirs + source[lead + (0, 1 - me, 0, 0)].astype(f32)
            return mine, theirs

        if name in CROSS:
            pairs[FIN_PAIR + SPLIT.index(name)].wait()
        if name == "d":
            for t in range(3):
                out_buf[8][8 * t : 8 * t + 8, :] = total((t, 0, 0, 0))
        elif name == "o":
            for t in range(2):
                out_buf[5][8 * t : 8 * t + 8, :] = total((0, 0, 0, t))
        elif name == "e":
            for c in range(2):
                fin["e"][c] = total((0, c, 0, 0))
        elif name in MLP:
            start = 0 if name == "g" else 64
            for t in range(3):
                columns = slice(128 * t, 128 * t + 128)
                for core, value in zip((me, 1 - me), both(t)):
                    for y in range(4):
                        r.blocks[rows_at(start + 8 * (2 * y + core), 8), columns] = value[:, 128 * y : 128 * y + 128]
        else:
            layouts = ((2, 4, 256, 0),) if name == "q" else ((3, 4, 128, 0), (4, 4, 128, 512))
            for core, value in zip((me, 1 - me), both(None)):
                for out, count, width, place in layouts:
                    for i in range(count):
                        lanes = slice(place + i * width, place + (i + 1) * width)
                        out_buf[out][:, lanes_at((2 * i + core) * width, width)] = value[:, lanes]

    spot = (pos["y"], me, pos["z"], pos["x"])

    def stage_columns(name, buf, start, count, width, place):
        for i in range(count):
            lanes = slice(place + i * width, place + (i + 1) * width)
            weight[name][spot + (slice(None), lanes)] = in_buf[buf][:, lanes_at((2 * i + me) * width, width)].astype(bf16)
            theirs = in_buf[buf][:, lanes_at((2 * i + 1 - me) * width, width)].astype(bf16)
            stage[name][0, 0, 0, 0, :, lanes] = theirs

    row_id = lax.broadcasted_iota(jnp.int32, (8, 128), 0)
    lane_id = lax.broadcasted_iota(jnp.int32, (8, 128), 1)
    lane_row = lax.broadcasted_iota(jnp.int32, (1, 128), 1)
    for copy in fetches[9:]:
        copy.wait()
    gains = jnp.zeros((1, 128), f32)
    for i in range(8):
        gains = jnp.where(lane_row == i, norm_gain[i], gains)
        gains = jnp.where(lane_row == 8 + i, mlp_gain[i], gains)
    gains = jnp.where(lane_row == 16, query_gain[0], gains)
    gains = jnp.where(lane_row == 17, key_gain[0], gains).astype(bf16).astype(f32)
    weight["e"][spot] = gains
    stage["e"][...] = gains
    r.seg[me] = jnp.broadcast_to(r.seg_in[...], (8, 128))
    for i in range(4):
        fetches[i].wait()
    stage_columns("q", 0, 0, 4, 256, 0)
    stage_columns("b", 1, 0, 4, 128, 0)
    stage_columns("b", 2, 0, 4, 128, 512)
    for t in range(2):
        weight["o"][pos["y"], pos["z"], pos["x"], t] = in_buf[3][8 * t : 8 * t + 8, :].astype(bf16)

    pl.semaphore_wait(barrier, len(others))

    def pair_start(name):
        index = STAGE_PAIR + SPLIT.index(name)
        dst = weight["e"].at[spot] if name == "e" else block(weight[name], (name, None), pos, me)
        pairs[name] = to_sibling(index, stage[name], dst)

    pair_start("e")
    for name in ATTN:
        gather_start((name, None), 0)
    for name in ("q", "b"):
        pair_start(name)

    to_lane = lax.broadcasted_iota(jnp.int32, (384, 384), 1)
    from_lane = ((to_lane >> 3) & 15) * 24 + (to_lane >> 7) * 8 + (to_lane & 7)
    r.perm[...] = jnp.where(lax.broadcasted_iota(jnp.int32, (384, 384), 0) == from_lane, 1.0, 0.0).astype(bf16)
    for i in range(4, 7):
        fetches[i].wait()
    for i, buf in ((0, 4), (1, 5)):
        for b in range(8):
            r.blocks[64 * i + 8 * b : 64 * i + 8 * b + 8, :] = in_buf[buf][:, 384 * b : 384 * b + 384]
    r.blocks[...] = dot(r.blocks[...].astype(bf16), r.perm[...])
    for i, name in ((0, "g"), (1, "u")):
        for y in range(4):
            mine = r.blocks[rows_at(64 * i + 8 * (2 * y + me), 8), :].astype(bf16)
            theirs = r.blocks[rows_at(64 * i + 8 * (2 * y + 1 - me), 8), :].astype(bf16)
            for t in range(3):
                lanes = slice(128 * y, 128 * y + 128)
                weight[name][(t,) + spot + (slice(None), lanes)] = mine[:, 128 * t : 128 * t + 128]
                stage[name][t, 0, 0, 0, 0, :, lanes] = theirs[:, 128 * t : 128 * t + 128]
    for t in range(3):
        weight["d"][t, pos["y"], pos["z"], pos["x"]] = in_buf[6][8 * t : 8 * t + 8, :].astype(bf16)
    pairs["e"].wait()
    gather_start(("e", None), 0)
    for name in MLP:
        gather_start((name, None), 0)
    for name in ("g", "u"):
        pair_start(name)
    fetches[7].wait()
    fetches[8].wait()
    pairs[X_PAIR] = to_sibling(X_PAIR, r.x.at[own_rows], r.x.at[own_rows])
    pairs[SEG_PAIR] = to_sibling(SEG_PAIR, r.seg.at[me], r.seg.at[me])
    pairs[COT_PAIR] = to_sibling(COT_PAIR, r.cot.at[own_rows], r.cot.at[own_rows])
    for name in ("e",) + ATTN:
        if name in CROSS:
            pairs[name].wait()
        gather_finish((name, None), 0)
        gather_start((name, None), 1)
    for name in MLP:
        if name in CROSS:
            pairs[name].wait()
        gather_finish((name, None), 0)
        gather_start((name, None), 1, (0, 1))

    for i in (X_PAIR, SEG_PAIR, COT_PAIR):
        pairs[i].wait()
    freq_lane = lax.rem(lax.broadcasted_iota(jnp.int32, (128, 128), 1), 64).astype(f32)
    inv_freq = jnp.exp(freq_lane * (-2.0 / HD * LOG_THETA))
    sign = jnp.where(lax.broadcasted_iota(jnp.int32, (128, 128), 1) < 64, -1.0, 1.0)
    t_id = lax.broadcasted_iota(jnp.int32, (128, 128), 0)
    u_id = lax.broadcasted_iota(jnp.int32, (128, 128), 1)

    def angles_of(b):
        ids = jnp.broadcast_to(r.seg[b, 0:1, :].astype(f32), (128, 128))
        same = ids == ids.T
        position = jnp.sum(jnp.where(same & (u_id < t_id), 1.0, 0.0), axis=1, keepdims=True)
        r.mask[b] = jnp.where(same & (u_id <= t_id), 1.0, 0.0)
        angles = position * inv_freq
        r.cos[128 * b : 128 * b + 128, :] = jnp.cos(angles)
        r.sin[128 * b : 128 * b + 128, :] = jnp.sin(angles) * sign

    angles_of(0)
    for name in ATTN:
        gather_forward((name, None), 1)
    for name in MLP:
        gather_start((name, None), 1, (2, 3))
    angles_of(1)
    gather_finish(("e", None), 1)
    gather_start(("e", None), 2)
    for name in ATTN:
        gather_finish((name, None), 1)
        gather_start((name, None), 2)
    for name in MLP:
        gather_forward((name, None), 1)

    unit_lane = lax.broadcasted_iota(jnp.int32, (1024, 128), 1)
    unit_row = lax.broadcasted_iota(jnp.int32, (1024, 128), 0) & 7
    r.eighths[0] = jnp.where(unit_lane == unit_row, 1.0, 0.0).astype(bf16)
    r.eighths[1] = jnp.where(unit_lane == unit_row + 8, 1.0, 0.0).astype(bf16)
    owner = lax.broadcasted_iota(jnp.int32, (128, 1024), 1) >> 3
    owned = owner == lax.broadcasted_iota(jnp.int32, (128, 1024), 0)
    pick = ((row_id == 2) & (lane_id == 16)) | ((row_id == 3) & (lane_id == 17))
    pick = jnp.where(pick, 1.0, 0.0).astype(bf16)
    gather_finish(("e", None), 2)
    table = weight["e"][...].reshape(128, 128).astype(bf16)
    for i in range(2):
        spread = jnp.where(owned, dot_nt(table, r.eighths[i]), 0.0)
        r.gain_rows[i : i + 1, :] = jnp.sum(spread, axis=0, keepdims=True)
    r.head_gains[...] = dot_nt(pick, table)
    gain_in, gain_mid = r.gain_rows.at[0:1], r.gain_rows.at[1:2]
    gain_query, gain_key = r.head_gains.at[2:3], r.head_gains.at[3:4]

    def rows_of(i, size=32):
        return pl.ds(pl.multiple_of(i * size, size), size)

    def norm_in(i):
        x = r.x[rows_of(i), :].astype(f32)
        r.normed[rows_of(i), :] = (x * inverse_rms(x) * gain_in[...]).astype(bf16)

    loop(8, norm_in)
    normed, cot = r.normed, r.cot
    for name in ATTN:
        gather_forward((name, None), 2)
    for name in MLP:
        gather_finish((name, None), 1)
    for name in MLP:
        gather_start((name, 0), 2)
    for name in MLP:
        gather_start((name, 1), 2, (0, 1))
    for name in ATTN:
        gather_finish((name, None), 2)

    def project_q(i):
        lanes = lanes_at(i * 512, 512)
        r.q_raw[:, lanes] = dot(normed[...], weight["q"][..., lanes].reshape(1024, 512))

    loop(2, project_q)
    r.k_raw[...] = dot(normed[...], weight["b"][..., :512].reshape(1024, 512))
    r.values[...] = dot(normed[...], weight["b"][..., 512:].reshape(1024, 512)).astype(bf16)

    def rotate(vector, cos_part, sin_part):
        return vector * cos_part + pltpu.roll(vector, 64, 1) * sin_part

    def turn(src, dst, gain):
        def head(h):
            lanes = lanes_at(h * 128, 128)
            raw = src[:, lanes]
            turned = rotate(raw * inverse_rms(raw) * gain[...], r.cos[...], r.sin[...])
            dst[:, lanes] = turned.astype(bf16)

        return head

    loop(8, turn(r.q_raw, r.q_rot, gain_query))
    loop(4, turn(r.k_raw, r.k_rot, gain_key))

    for name in MLP:
        gather_forward((name, 0), 2)
    for name in MLP:
        gather_start((name, 1), 2, (2, 3))
    for name in MLP:
        gather_start((name, 2), 2, (0, 1))

    def both_heads(ref, rows, m):
        first = ref[rows, lanes_at(m * 256, 128)]
        second = ref[rows, lanes_at(m * 256 + 128, 128)]
        return jnp.concatenate([first, second], axis=0)

    def attend(i):
        b, m = i // 4, lax.rem(i, 4)
        rows = pl.ds(pl.multiple_of(b * 128, 128), 128)
        lanes = lanes_at(m * 128, 128)
        scores = dot_nt(both_heads(r.q_rot, rows, m), r.k_rot[rows, lanes]) * SCALE
        mask = r.mask[b]
        masked = jnp.where(jnp.concatenate([mask, mask], axis=0) > 0.0, scores, -1e30)
        terms = jnp.exp(masked - jnp.max(masked, axis=-1, keepdims=True))
        probs = terms / jnp.sum(terms, axis=-1, keepdims=True)
        r.probs[i] = probs
        got = dot(probs.astype(bf16), r.values[rows, lanes]).astype(bf16)
        r.attended[rows, lanes_at(m * 256, 128)] = got[:128]
        r.attended[rows, lanes_at(m * 256 + 128, 128)] = got[128:]

    loop(8, attend)
    attended = r.attended

    def project_out(i):
        lanes = lanes_at(i * 512, 512)
        r.out_part[:, lanes] = dot(attended[...], weight["o"][..., lanes].reshape(1024, 512))

    loop(2, project_out)
    out_copy = to_sibling(OUT_PAIR, r.out_part, r.out_other)
    for name in MLP:
        gather_forward((name, 1), 2)
    for name in MLP:
        gather_start((name, 2), 2, (2, 3))
    out_copy.wait()

    def norm_mid(i):
        rows = rows_of(i)
        hidden = r.x[rows, :].astype(f32) + (r.out_part[rows, :] + r.out_other[rows, :])
        r.hidden[rows, :] = hidden
        r.mid_low[rows, :] = (hidden * inverse_rms(hidden) * gain_mid[...]).astype(bf16)

    loop(8, norm_mid)
    mid_low, mixed, d_gate, d_up = r.mid_low, r.mixed, r.d_gate, r.d_up

    def feed(t):
        gate = dot(mid_low[...], weight["g"][t].reshape(1024, 512))
        up = dot(mid_low[...], weight["u"][t].reshape(1024, 512))
        d_mixed = dot_nt(cot[...], weight["d"][t].reshape(512, 1024))
        sig = jax.nn.sigmoid(gate)
        act = gate * sig
        mixed[...] = (act * up).astype(bf16)
        d_gate[...] = (d_mixed * up * sig * (1.0 + gate * (1.0 - sig))).astype(bf16)
        d_up[...] = (d_mixed * act).astype(bf16)

        def mid_back(i):
            y_pair, lanes = pl.ds(2 * i, 2), lanes_at(i * 512, 512)
            got = dot_nt(d_gate[...], weight["g"][t, y_pair].reshape(512, 512))
            got += dot_nt(d_up[...], weight["u"][t, y_pair].reshape(512, 512))
            r.mid_part[:, lanes] = got if t == 0 else r.mid_part[:, lanes] + got

        def project_down(i):
            lanes = lanes_at(i * 512, 512)
            got = dot(mixed[...], weight["d"][t, ..., lanes].reshape(512, 512))
            r.down_part[:, lanes] = got if t == 0 else r.down_part[:, lanes] + got

        loop(2, mid_back)
        if t == 2:
            pairs[MID_PAIR] = to_sibling(MID_PAIR, r.mid_part, r.mid_other)
        loop(2, project_down)

    def grads(t):
        def grad_down(i):
            got = dot_tn(mixed[:, lanes_at(i * 256, 256)], cot[...]).astype(bf16)
            weight["d"][t, pl.ds(2 * i, 2)] = got.reshape(2, 4, 4, 8, 1024)

        def grad_gate(i):
            left = mid_low[:, lanes_at(i * 512, 512)]
            weight["g"][t, pl.ds(2 * i, 2)] = dot_tn(left, d_gate[...]).astype(bf16).reshape(2, 2, 4, 4, 8, 512)
            weight["u"][t, pl.ds(2 * i, 2)] = dot_tn(left, d_up[...]).astype(bf16).reshape(2, 2, 4, 4, 8, 512)

        loop(2, grad_down)
        loop(2, grad_gate)

    def sends_done(item, phases):
        for phase in phases:
            wait_for(0, item, phase, 0, 3)

    for name in MLP:
        gather_finish((name, 0), 2)
    feed(0)
    for name in MLP:
        gather_forward((name, 2), 2)
    for name in MLP:
        sends_done((name, None), (0, 1))
        sends_done((name, 0), (2,))
    grads(0)
    for name in MLP:
        sum_start((name, 0), 0)
    for name in MLP:
        gather_finish((name, 1), 2)
    feed(1)
    for name in MLP:
        sends_done((name, 1), (2,))
    grads(1)
    for name in MLP:
        sum_start((name, 1), 0)
    for name in MLP:
        gather_finish((name, 2), 2)
    feed(2)
    for name in MLP:
        sends_done((name, 2), (2,))
    grads(2)
    for name in MLP:
        sum_start((name, 2), 0)
    down_copy = to_sibling(DOWN_PAIR, r.down_part.at[other_rows], r.down_other)
    for name in MLP:
        sum_middle((name, 0), 0)
    pairs[MID_PAIR].wait()

    r.gain_sums[...] = jnp.zeros((8, 1024), f32)
    r.head_sums[...] = jnp.zeros((8, 128), f32)

    def res_back(i):
        rows = rows_of(i)
        hidden = r.hidden[rows, :]
        inverse = inverse_rms(hidden)
        unit = hidden * inverse
        part = r.mid_part[rows, :]
        r.gain_sums[1:2, :] += jnp.sum(part * unit, axis=0, keepdims=True)
        d_mid = part + r.mid_other[rows, :]
        d_res = cot[rows, :].astype(f32) + norm_backward(d_mid, unit, inverse, gain_mid[...])
        r.d_res[rows, :] = d_res
        r.d_res_low[rows, :] = d_res.astype(bf16)

    loop(8, res_back)
    d_res_low = r.d_res_low

    def attn_back(i):
        two = weight["o"][pl.ds(2 * i, 2)].reshape(512, 1024)
        r.d_attn[:, lanes_at(i * 512, 512)] = dot_nt(d_res_low[...], two).astype(bf16)

    loop(2, attn_back)
    for name in ATTN + ("e",):
        sends_done((name, None), (0, 1, 2))

    def grad_of(name, left, right):
        def rows(i):
            got = dot_tn(left[:, lanes_at(i * 512, 512)], right[...]).astype(bf16)
            weight[name][pl.ds(2 * i, 2)] = got.reshape((2,) + SHAPES[name][1:])

        loop(2, rows)

    grad_of("o", attended, d_res_low)
    for name in MLP:
        sum_middle((name, 1), 0)

    def head_back(grad, raw, gain):
        inverse = inverse_rms(raw)
        unit = raw * inverse
        return jnp.sum(grad * unit, axis=0, keepdims=True), norm_backward(grad, unit, inverse, gain[...])

    def attend_back(i):
        b, m = i // 4, lax.rem(i, 4)
        rows = pl.ds(pl.multiple_of(b * 128, 128), 128)
        lanes = lanes_at(m * 128, 128)
        d_att = both_heads(r.d_attn, rows, m)
        query, key = both_heads(r.q_rot, rows, m), r.k_rot[rows, lanes]
        probs = r.probs[i]
        d_probs = dot_nt(d_att, r.values[rows, lanes])
        r.d_b[rows, lanes_at(512 + m * 128, 128)] = dot_tn(probs.astype(bf16), d_att).astype(bf16)
        d_scores = (probs * (d_probs - jnp.sum(d_probs * probs, axis=-1, keepdims=True))).astype(bf16)
        d_query = dot(d_scores, key) * SCALE
        d_key = dot_tn(d_scores, query) * SCALE
        cos_part, sin_part = r.cos[rows, :], -r.sin[rows, :]
        for j in range(2):
            spots = lanes_at(m * 256 + 128 * j, 128)
            d_unit = rotate(d_query[128 * j : 128 * j + 128], cos_part, sin_part)
            total, d_raw = head_back(d_unit, r.q_raw[rows, spots], gain_query)
            r.head_sums[2:3, :] += total
            r.d_q[rows, spots] = d_raw.astype(bf16)
        total, d_raw = head_back(rotate(d_key, cos_part, sin_part), r.k_raw[rows, lanes], gain_key)
        r.head_sums[3:4, :] += total
        r.d_b[rows, lanes] = d_raw.astype(bf16)

    loop(8, attend_back)
    for name in MLP:
        sum_middle((name, 2), 0)
    sum_start(("o", None), 0)

    def in_back(i):
        y_pair = pl.ds(2 * i, 2)
        got = dot_nt(r.d_q[...], weight["q"][y_pair].reshape(512, 1024))
        got += dot_nt(r.d_b[...], weight["b"][y_pair].reshape(512, 1024))
        r.in_part[:, lanes_at(i * 512, 512)] = got

    loop(2, in_back)
    in_copy = to_sibling(IN_PAIR, r.in_part.at[other_rows], r.in_other)
    grad_of("q", normed, r.d_q)
    sum_start(("q", None), 0)
    grad_of("b", normed, r.d_b)
    sum_start(("b", None), 0)

    def gain_back(i):
        x = r.x[rows_of(i), :].astype(f32)
        unit = x * inverse_rms(x)
        r.gain_sums[0:1, :] += jnp.sum(r.in_part[rows_of(i), :] * unit, axis=0, keepdims=True)

    loop(8, gain_back)
    table = dot_tn(r.head_sums[...].astype(bf16), pick)
    for i in range(2):
        table += dot(jnp.where(owned, r.gain_sums[i : i + 1, :], 0.0).astype(bf16), r.eighths[i])
    weight["e"][...] = table.reshape(SHAPES["e"])
    sum_start(("e", None), 0)

    down_copy.wait()

    def finish_out(i):
        rows = rows_of(i)
        mine = pl.ds(pl.multiple_of(me * 128 + i * 32, 32), 32)
        down = r.down_part[mine, :] + r.down_other[rows, :]
        layer_out[rows, :] = (r.hidden[mine, :] + down).astype(bf16)

    loop(4, finish_out)
    for t in range(3):
        for name in MLP:
            sum_end((name, t), 0)
    in_copy.wait()

    def finish_in(i):
        rows = rows_of(i)
        mine = pl.ds(pl.multiple_of(me * 128 + i * 32, 32), 32)
        d_normed = r.in_part[mine, :] + r.in_other[rows, :]
        x = r.x[mine, :].astype(f32)
        inverse = inverse_rms(x)
        input_grad[rows, :] = r.d_res[mine, :] + norm_backward(d_normed, x * inverse, inverse, gain_in[...])

    loop(4, finish_in)

    for name in ATTN:
        sum_middle((name, None), 0)
    for name in MLP:
        sum_start((name, None), 1)
    sum_end(("e", None), 0)
    sum_start(("e", None), 1)
    for name in ATTN:
        sum_end((name, None), 0)
        sum_start((name, None), 1)
    for name in MLP:
        sum_middle((name, None), 1)
    sum_end(("e", None), 1)
    sum_start(("e", None), 2)
    for name in ATTN:
        sum_middle((name, None), 1)
    for name in MLP:
        sum_end((name, None), 1)
        sum_start((name, None), 2)
    for name in ATTN:
        sum_end((name, None), 1)
        sum_start((name, None), 2)
    sum_end(("e", None), 2)
    swap = to_sibling(FIN_PAIR + SPLIT.index("e"), fin["e"].at[1 - me], rx["e"])
    for name in MLP:
        sum_end((name, None), 2)
    rest = r.blocks[...]
    total = jnp.zeros((128, 384), f32)
    for _ in range(3):
        head = rest.astype(bf16)
        total += dot_nt(head, r.perm[...])
        rest = rest - head.astype(f32)
    for i, out in ((0, 6), (1, 7)):
        for b in range(8):
            out_buf[out][:, 384 * b : 384 * b + 384] = total[64 * i + 8 * b : 64 * i + 8 * b + 8, :]
    swap.wait()
    row = fin["e"][me] + rx["e"][...]
    for ref, first, count in zip(out_buf[9:], (0, 8, 16, 17), (8, 8, 1, 1)):
        ref[...] = row[0, first : first + count]
    for name in ATTN:
        sum_end((name, None), 2)
    for item, phase in SUMS:
        wait_for(1, item, phase, 0, 3)


def finish_kernel(*refs):
    n = len(OUTS)
    ins, outs, sems = refs[:n], refs[n : 2 * n], refs[-1]
    copies = [pltpu.make_async_copy(ins[i], outs[i], sems.at[i]) for i in range(n)]
    for copy in copies:
        copy.start()
    for copy in copies:
        copy.wait()


def body(*args):
    hbm = pl.BlockSpec(memory_space=pl.ANY)
    vmem = pl.BlockSpec(memory_space=pltpu.VMEM)
    parts = pl.pallas_call(
        layer_kernel,
        out_shape=[pltpu.VMEM(*entry) for entry in OUTS],
        in_specs=[hbm] * 14,
        out_specs=[vmem] * len(OUTS),
        scratch_shapes=[pltpu.VMEM(*entry) for group in GROUPS for entry in group.values()]
        + [pltpu.SMEM((size,), f32) for size in (8, 8, 1, 1)]
        + [pltpu.SemaphoreType.DMA((len(SEMS),))]
        + [pltpu.SemaphoreType.DMA((PAIRS,))] * 2
        + [pltpu.SemaphoreType.DMA((14,))],
        compiler_params=pltpu.CompilerParams(
            collective_id=1, has_side_effects=True, vmem_limit_bytes=57 << 20
        ),
        name="layer",
    )(*args)
    parts = [pltpu.with_memory_space_constraint(part, pltpu.VMEM) for part in parts]
    (
        layer_out, input_grad, grad_q, grad_k, grad_v, grad_o, grad_g, grad_u, grad_d, norm_gain, mlp_gain, query_gain, key_gain,
    ) = pl.pallas_call(
        finish_kernel,
        out_shape=[jax.ShapeDtypeStruct(*entry) for entry in OUTS],
        in_specs=[vmem] * len(OUTS),
        out_specs=[hbm] * len(OUTS),
        scratch_shapes=[pltpu.SemaphoreType.DMA((len(OUTS),))],
        name="finish",
    )(*parts)
    return (
        layer_out, input_grad, norm_gain, grad_q, grad_k, grad_v, query_gain, key_gain, grad_o, mlp_gain, grad_g, grad_u, grad_d,
    )


def solution(mesh):
    rows = P(("dp", "fsdp"), None)
    flat = P(("dp", "fsdp"))
    return jax.shard_map(
        body,
        mesh=mesh,
        in_specs=(rows, rows, flat, rows, rows, rows, flat, flat, rows, flat, rows, rows, rows, rows),
        out_specs=(rows, rows, flat, rows, rows, rows, flat, flat, rows, flat, rows, rows, rows),
        check_vma=False,
    )
```

```python
import types

import jax
import jax.numpy as jnp
from jax import lax
from jax.experimental import pallas as pl
from jax.experimental.pallas import tpu as pltpu
from jax.sharding import PartitionSpec as P

HD = 128
EPS = 1e-06
LOG_THETA = 13.815510557964274
SCALE = HD ** (-0.5)

bf16 = jnp.bfloat16
f32 = jnp.float32
MESH = pl.DeviceIdType.MESH

SHAPES = dict(
    q=(4, 2, 4, 4, 8, 1024),
    b=(4, 2, 4, 4, 8, 1024),
    o=(4, 4, 4, 2, 8, 1024),
    e=(4, 2, 4, 4, 1, 128),
    g=(3, 4, 2, 4, 4, 8, 512),
    u=(3, 4, 2, 4, 4, 8, 512),
    d=(3, 4, 4, 4, 8, 1024),
)
NAMES = tuple(SHAPES)
SPLIT = ("q", "b", "e", "g", "u")
CROSS = ("q", "b", "g", "u")
ATTN = ("q", "b", "o")
MLP = ("g", "u", "d")
ORDER = dict(q="xyz", g="xyz", b="yzx", u="yzx", o="zxy", d="zxy", e="zxy")
DTYPE = {name: f32 if name == "e" else bf16 for name in NAMES}


def coords():
    dp = lax.axis_index("dp")
    fs = lax.axis_index("fsdp")
    return dict(y=dp // 2, c=lax.rem(dp, 2), z=fs // 4, x=lax.rem(fs, 4))


def device(pos, axis=None, step=0):
    pos = dict(pos)
    if axis == "c":
        pos["c"] = 1 - pos["c"]
    elif axis is not None:
        pos[axis] = lax.rem(pos[axis] + step + 4, 4)
    return (pos["y"] * 2 + pos["c"], pos["z"] * 4 + pos["x"])


def item_shape(item):
    name, third = item
    return SHAPES[name] if third is None else SHAPES[name][1:]


def lead_of(item):
    return 1 if item[0] in MLP and item[1] is None else 0


def axis_places(item):
    lead = lead_of(item)
    if item[0] in SPLIT:
        return dict(y=lead, z=lead + 2, x=lead + 3)
    return dict(y=lead, z=lead + 1, x=lead + 2)


def block(ref, item, at, half=None):
    shape = item_shape(item)
    index = [slice(None)] * len(shape)
    for axis, place in axis_places(item).items():
        if axis in at:
            start, size = at[axis] if isinstance(at[axis], tuple) else (at[axis], 1)
            index[place] = pl.ds(start, size)
    if half is not None:
        if item[0] in SPLIT:
            index[lead_of(item) + 1] = pl.ds(half, 1)
        else:
            index[-1] = pl.ds(half * (shape[-1] // 2), shape[-1] // 2)
    return ref.at[tuple(index)]


def half_of(ref, item, half):
    return block(ref, item, {}, half)


def merged(item, fixed):
    shape = list(item_shape(item))
    for axis in fixed:
        shape[axis_places(item)[axis]] = 1
    return tuple(shape)


def halved(item, shape):
    shape = list(shape)
    shape[lead_of(item) + 1 if item[0] in SPLIT else -1] //= 2
    return tuple(shape)


def add_into(dst, sources, shape):
    lead = shape[:-3]
    count = 1
    for extent in lead:
        count *= extent

    def step(i, carry):
        index, rest = [], i
        for extent in reversed(lead):
            index.append(lax.rem(rest, extent))
            rest = rest // extent
        index = tuple(reversed(index))
        total = sources[0][index].astype(f32)
        for source in sources[1:]:
            total = total + source[index].astype(f32)
        dst[index] = total.astype(dst.dtype)
        return carry

    lax.fori_loop(0, count, step, 0)


def dot(left, right):
    return jnp.dot(left, right, preferred_element_type=f32)


def dot_nt(left, right):
    return lax.dot_general(left, right, (((1,), (1,)), ((), ())), preferred_element_type=f32)


def dot_tn(left, right):
    return lax.dot_general(left, right, (((0,), (0,)), ((), ())), preferred_element_type=f32)


def inverse_rms(vector):
    return lax.rsqrt(jnp.mean(vector * vector, axis=-1, keepdims=True) + EPS)


def norm_backward(grad_in, unit_vec, inverse, gain_vec):
    scaled = grad_in * gain_vec
    return inverse * (scaled - unit_vec * jnp.mean(scaled * unit_vec, axis=-1, keepdims=True))


def lanes_at(start, size):
    return pl.ds(pl.multiple_of(start, 128), size)


def rows_at(start, size):
    return pl.ds(pl.multiple_of(start, 8), size)


def loop(count, body):
    def step(i, carry):
        body(i)
        return carry

    lax.fori_loop(0, count, step, 0)


ALL = (("q", None), ("b", None), ("o", None), ("e", None), ("g", None), ("u", None), ("d", None))
THIRDS = tuple((name, t) for t in range(3) for name in MLP)
ITEMS = ALL + THIRDS
SUMS = tuple((item, phase) for item in ALL for phase in range(3) if item[0] not in MLP or phase > 0)
SUMS += tuple((item, 0) for item in THIRDS)


def is_direct(item, phase):
    return phase == 2 or item[0] == "e"


GATHERS = tuple((item, phase) for item in ALL for phase in range(3) if item[0] not in MLP or phase < 2)
GATHERS += tuple((item, 2) for item in THIRDS)
SEMS = {}
for _kind, _steps in enumerate((GATHERS, SUMS)):
    for _item, _phase in _steps:
        if _item[0] in ("u", "d"):
            continue
        _direct = is_direct(_item, _phase) if _kind else _phase == 0 or _item[0] == "e"
        for _use in range(2 if _direct else 3):
            SEMS[_kind, _item, _phase, _use] = len(SEMS)
W = {name: (SHAPES[name], DTYPE[name]) for name in NAMES}
ROWS = {name: halved((name, None), merged((name, None), ORDER[name])) for name in CROSS}
STAGE = {name: (ROWS[name], bf16) for name in CROSS}
RX = {name: (ROWS[name], bf16) for name in CROSS}
STAGE["e"] = RX["e"] = ((1, 128), f32)
FIN = dict(e=((2, 1, 128), f32))
FAR, NEAR = {}, {}
for _item, _phase in SUMS:
    _shape = merged(_item, ORDER[_item[0]][::-1][: _phase + 1])
    for _way in range(2):
        NEAR[_item, _phase, _way] = (_shape, DTYPE[_item[0]])
        if not is_direct(_item, _phase):
            FAR[_item, _phase, _way] = (halved(_item, _shape), DTYPE[_item[0]])
    if is_direct(_item, _phase):
        FAR[_item, _phase, 2] = (_shape, DTYPE[_item[0]])
INS = (
    ((8, 2048), f32), ((8, 1024), f32), ((8, 1024), f32), ((16, 1024), f32), ((8, 3072), f32), ((8, 3072), f32), ((24, 1024), f32),
)
OUTS = (((128, 1024), bf16), ((128, 1024), f32)) + INS + tuple(((size,), f32) for size in (8, 8, 1, 1))
IN_BUF = {i: entry for i, entry in enumerate(INS)}
FLAT = dict(
    x=((256, 1024), bf16),
    cot=((256, 1024), bf16),
    seg=((2, 8, 128), jnp.int32),
    seg_in=((1, 128), jnp.int32),
    perm=((384, 384), bf16),
    blocks=((128, 384), f32),
    eighths=((2, 1024, 128), bf16),
    gain_rows=((8, 1024), f32),
    head_gains=((8, 128), f32),
    gain_sums=((8, 1024), f32),
    head_sums=((8, 128), f32),
    mask=((2, 128, 128), f32),
    cos=((256, 128), f32),
    sin=((256, 128), f32),
    normed=((256, 1024), bf16),
    q_raw=((256, 1024), f32),
    k_raw=((256, 512), f32),
    values=((256, 512), bf16),
    q_rot=((256, 1024), bf16),
    k_rot=((256, 512), bf16),
    probs=((8, 256, 128), f32),
    attended=((256, 1024), bf16),
    out_part=((256, 1024), f32),
    out_other=((256, 1024), f32),
    hidden=((256, 1024), f32),
    mid_low=((256, 1024), bf16),
    mixed=((256, 512), bf16),
    d_gate=((256, 512), bf16),
    d_up=((256, 512), bf16),
    down_part=((256, 1024), f32),
    down_other=((128, 1024), f32),
    mid_part=((256, 1024), f32),
    mid_other=((256, 1024), f32),
    d_res=((256, 1024), f32),
    d_res_low=((256, 1024), bf16),
    d_attn=((256, 1024), bf16),
    d_q=((256, 1024), bf16),
    d_b=((256, 1024), bf16),
    in_part=((256, 1024), f32),
    in_other=((128, 1024), f32),
)
GROUPS = (W, STAGE, FIN, RX, FAR, NEAR, IN_BUF, FLAT)
X_PAIR, COT_PAIR, SEG_PAIR, OUT_PAIR, DOWN_PAIR, MID_PAIR, IN_PAIR, STAGE_PAIR = range(8)
FIN_PAIR = STAGE_PAIR + len(SPLIT)
PAIRS = FIN_PAIR + len(SPLIT)


def layer_kernel(
    tokens, segment, norm_gain, w_query, w_key, w_value, query_gain, key_gain, w_out, mlp_gain, w_gate, w_up, w_down,
    cotangent, *refs,
):
    refs = list(refs)
    out_buf = [refs.pop(0) for _ in OUTS]
    held = []
    for group in GROUPS:
        held.append({key: refs.pop(0) for key in group})
    weight, stage, fin, rx, far_of, near_of, in_buf, flat = held
    r = types.SimpleNamespace(**flat)
    gains_in, (sems, pair_send, pair_recv, local_in) = refs[:4], refs[4:]
    pos = coords()
    me = pos["c"]
    sibling = device(pos, "c")
    flipped = dict(pos, c=1 - me)
    own_rows = pl.ds(pl.multiple_of(me * 128, 128), 128)
    other_rows = pl.ds(pl.multiple_of((1 - me) * 128, 128), 128)
    layer_out, input_grad = out_buf[0], out_buf[1]

    barrier = pltpu.get_barrier_semaphore()
    others = [sibling]
    for axis in "xyz":
        others += [device(pos, axis, step) for step in (1, -1, 2)]
    for axis in "xy":
        others += [device(flipped, axis, step) for step in (1, -1, 2)]
    for other in others:
        pl.semaphore_signal(barrier, inc=1, device_id=other, device_id_type=MESH)
    fetches = []
    for i, src in enumerate((w_query, w_key, w_value, w_out, w_gate, w_up, w_down)):
        fetches.append(pltpu.make_async_copy(src, in_buf[i], local_in.at[i]))
    fetches.append(pltpu.make_async_copy(tokens, r.x.at[own_rows], local_in.at[7]))
    fetches.append(pltpu.make_async_copy(cotangent, r.cot.at[own_rows], local_in.at[8]))
    small = ((norm_gain, gains_in[0]), (mlp_gain, gains_in[1]), (query_gain, gains_in[2]), (key_gain, gains_in[3]), (segment, r.seg_in))
    for i, (src, dst) in enumerate(small):
        fetches.append(pltpu.make_async_copy(src, dst, local_in.at[9 + i]))
    for copy in fetches[9:] + fetches[:9]:
        copy.start()
    norm_gain, mlp_gain, query_gain, key_gain = gains_in

    def remote(src, dst, send_sem, recv_sem, target):
        return pltpu.make_async_remote_copy(
            src_ref=src, dst_ref=dst, send_sem=send_sem, recv_sem=recv_sem, device_id=target, device_id_type=MESH
        )

    def to_sibling(index, src, dst):
        copy = remote(src, dst, pair_send.at[index], pair_recv.at[index], sibling)
        copy.start()
        return copy

    def sem(kind, item, phase, use):
        name, third = item
        return sems.at[SEMS[kind, ("g" if name in MLP else name, third), phase, use]]

    def send(kind, item, phase, use, src, dst, target):
        remote(src, dst, sem(kind, item, phase, 0), sem(kind, item, phase, use), target).start()

    def wait_for(kind, item, phase, use, count):
        name, third = item
        if name in ("u", "d"):
            return
        order = ORDER[name] if kind == 0 else ORDER[name][::-1]
        fixed = order[phase + 1 :] if kind == 0 else order[:phase]
        at = {a: pos[a] for a in fixed}
        if name == "g" and third is None:
            at[fixed[0]] = (0, 3)
        like = block(weight[name], (name, None), {**at, order[phase]: (0, count)})
        pltpu.make_async_copy(like, like, sem(kind, item, phase, use)).wait()

    def view(item):
        name, third = item
        return weight[name] if third is None else weight[name].at[third]

    pairs = {}

    def gather_start(item, phase, keys=(0, 1, 2, 3)):
        order = ORDER[item[0]]
        axis = order[phase]
        at = {a: pos[a] for a in order[phase:]}
        if phase == 0 and item[0] in CROSS:
            mine = block(view(item), item, at, me)
            for step in (1, -1, 2):
                send(0, item, phase, 1, mine, mine, device(pos, axis, step))
                send(0, item, phase, 1, stage[item[0]], mine, device(flipped, axis, step))
            return
        if phase == 0 or item[0] == "e":
            for step in (1, -1, 2):
                src = block(view(item), item, at)
                send(0, item, phase, 1, src, src, device(pos, axis, step))
            return
        for key, half, step in ((0, 0, 1), (1, 1, -1), (2, 1, 1), (3, 0, -1)):
            if key in keys:
                src = block(view(item), item, at, half)
                send(0, item, phase, 1 if key < 2 else 2, src, src, device(pos, axis, step))

    def gather_forward(item, phase):
        order = ORDER[item[0]]
        axis = order[phase]
        at = {a: pos[a] for a in order[phase:]}
        wait_for(0, item, phase, 1, 1)
        for half, step in ((0, 1), (1, -1)):
            src = block(view(item), item, {**at, axis: lax.rem(pos[axis] + 4 - step, 4)}, half)
            send(0, item, phase, 2, src, src, device(pos, axis, step))

    def gather_finish(item, phase):
        if phase == 0 or item[0] == "e":
            wait_for(0, item, phase, 1, 3)
        else:
            wait_for(0, item, phase, 2, 2)

    def sum_start(item, phase):
        order = ORDER[item[0]][::-1]
        axis = order[phase]
        at = {a: pos[a] for a in order[:phase]}
        ahead, behind = lax.rem(pos[axis] + 1, 4), lax.rem(pos[axis] + 3, 4)
        opposite = lax.rem(pos[axis] + 2, 4)
        up, down, across = device(pos, axis, 1), device(pos, axis, -1), device(pos, axis, 2)
        cur = view(item)
        near_up, near_down = near_of[item, phase, 0], near_of[item, phase, 1]

        def part(place, half=None):
            return block(cur, item, {**at, axis: place}, half)

        if phase == 2 and item[0] in CROSS:
            ways = ((opposite, far_of[item, phase, 2], 2), (ahead, near_up, 1), (behind, near_down, -1))
            for place, dst, step in ways:
                slot = half_of(dst, item, me)
                send(1, item, phase, 1, part(place, me), slot, device(pos, axis, step))
                send(1, item, phase, 1, part(place, 1 - me), slot, device(flipped, axis, step))
            index = FIN_PAIR + SPLIT.index(item[0])
            pairs[index] = to_sibling(index, block(cur, item, pos, 1 - me), rx[item[0]])
        elif is_direct(item, phase):
            send(1, item, phase, 1, part(opposite), far_of[item, phase, 2], across)
            send(1, item, phase, 1, part(ahead), near_up, up)
            send(1, item, phase, 1, part(behind), near_down, down)
        else:
            send(1, item, phase, 1, part(opposite, 0), far_of[item, phase, 0], up)
            send(1, item, phase, 1, part(opposite, 1), far_of[item, phase, 1], down)
            send(1, item, phase, 2, part(ahead, 1), half_of(near_up, item, 1), up)
            send(1, item, phase, 2, part(behind, 0), half_of(near_down, item, 0), down)

    def sum_middle(item, phase):
        order = ORDER[item[0]][::-1]
        axis = order[phase]
        at = {a: pos[a] for a in order[:phase]}
        shape = halved(item, merged(item, order[: phase + 1]))
        wait_for(1, item, phase, 1, 1)
        for half, step in ((0, 1), (1, -1)):
            far, near = far_of[item, phase, half], near_of[item, phase, half]
            mine = block(view(item), item, {**at, axis: lax.rem(pos[axis] + 4 + step, 4)}, half)
            add_into(far, [far, mine], shape)
            send(1, item, phase, 2, far, half_of(near, item, half), device(pos, axis, step))

    def sum_end(item, phase):
        order = ORDER[item[0]][::-1]
        at = {a: pos[a] for a in order[: phase + 1]}
        sources = [block(view(item), item, at), near_of[item, phase, 0], near_of[item, phase, 1]]
        if is_direct(item, phase):
            sources.append(far_of[item, phase, 2])
            wait_for(1, item, phase, 1, 3)
        else:
            wait_for(1, item, phase, 2, 2)
        if phase < 2:
            add_into(sources[0], sources, merged(item, order[: phase + 1]))
            return

        name = item[0]

        def total(place, first=None):
            value = (sources[0] if first is None else first)[place].astype(f32)
            for source in sources[1:]:
                value = value + source[place].astype(f32)
            return value

        def both(t):
            lead = () if t is None else (t,)
            mine = total(lead + (0, me, 0, 0))
            theirs = rx[name][lead + (0, 0, 0, 0)].astype(f32)
            for source in sources[1:]:
                theirs = theirs + source[lead + (0, 1 - me, 0, 0)].astype(f32)
            return mine, theirs

        if name in CROSS:
            pairs[FIN_PAIR + SPLIT.index(name)].wait()
        if name == "d":
            for t in range(3):
                out_buf[8][8 * t : 8 * t + 8, :] = total((t, 0, 0, 0))
        elif name == "o":
            for t in range(2):
                out_buf[5][8 * t : 8 * t + 8, :] = total((0, 0, 0, t))
        elif name == "e":
            for c in range(2):
                fin["e"][c] = total((0, c, 0, 0))
        elif name in MLP:
            start = 0 if name == "g" else 64
            for t in range(3):
                columns = slice(128 * t, 128 * t + 128)
                for core, value in zip((me, 1 - me), both(t)):
                    for y in range(4):
                        r.blocks[rows_at(start + 8 * (2 * y + core), 8), columns] = value[:, 128 * y : 128 * y + 128]
        else:
            layouts = ((2, 4, 256, 0),) if name == "q" else ((3, 4, 128, 0), (4, 4, 128, 512))
            for core, value in zip((me, 1 - me), both(None)):
                for out, count, width, place in layouts:
                    for i in range(count):
                        lanes = slice(place + i * width, place + (i + 1) * width)
                        out_buf[out][:, lanes_at((2 * i + core) * width, width)] = value[:, lanes]

    spot = (pos["y"], me, pos["z"], pos["x"])

    def stage_columns(name, buf, start, count, width, place):
        for i in range(count):
            lanes = slice(place + i * width, place + (i + 1) * width)
            weight[name][spot + (slice(None), lanes)] = in_buf[buf][:, lanes_at((2 * i + me) * width, width)].astype(bf16)
            theirs = in_buf[buf][:, lanes_at((2 * i + 1 - me) * width, width)].astype(bf16)
            stage[name][0, 0, 0, 0, :, lanes] = theirs

    row_id = lax.broadcasted_iota(jnp.int32, (8, 128), 0)
    lane_id = lax.broadcasted_iota(jnp.int32, (8, 128), 1)
    lane_row = lax.broadcasted_iota(jnp.int32, (1, 128), 1)
    for copy in fetches[9:]:
        copy.wait()
    gains = jnp.zeros((1, 128), f32)
    for i in range(8):
        gains = jnp.where(lane_row == i, norm_gain[i], gains)
        gains = jnp.where(lane_row == 8 + i, mlp_gain[i], gains)
    gains = jnp.where(lane_row == 16, query_gain[0], gains)
    gains = jnp.where(lane_row == 17, key_gain[0], gains).astype(bf16).astype(f32)
    weight["e"][spot] = gains
    stage["e"][...] = gains
    r.seg[me] = jnp.broadcast_to(r.seg_in[...], (8, 128))
    for i in range(4):
        fetches[i].wait()
    stage_columns("q", 0, 0, 4, 256, 0)
    stage_columns("b", 1, 0, 4, 128, 0)
    stage_columns("b", 2, 0, 4, 128, 512)
    for t in range(2):
        weight["o"][pos["y"], pos["z"], pos["x"], t] = in_buf[3][8 * t : 8 * t + 8, :].astype(bf16)

    pl.semaphore_wait(barrier, len(others))

    def pair_start(name):
        index = STAGE_PAIR + SPLIT.index(name)
        dst = weight["e"].at[spot] if name == "e" else block(weight[name], (name, None), pos, me)
        pairs[name] = to_sibling(index, stage[name], dst)

    pair_start("e")
    for name in ATTN:
        gather_start((name, None), 0)
    for name in ("q", "b"):
        pair_start(name)

    to_lane = lax.broadcasted_iota(jnp.int32, (384, 384), 1)
    from_lane = ((to_lane >> 3) & 15) * 24 + (to_lane >> 7) * 8 + (to_lane & 7)
    r.perm[...] = jnp.where(lax.broadcasted_iota(jnp.int32, (384, 384), 0) == from_lane, 1.0, 0.0).astype(bf16)
    for i in range(4, 7):
        fetches[i].wait()
    for i, buf in ((0, 4), (1, 5)):
        for b in range(8):
            r.blocks[64 * i + 8 * b : 64 * i + 8 * b + 8, :] = in_buf[buf][:, 384 * b : 384 * b + 384]
    r.blocks[...] = dot(r.blocks[...].astype(bf16), r.perm[...])
    for i, name in ((0, "g"), (1, "u")):
        for y in range(4):
            mine = r.blocks[rows_at(64 * i + 8 * (2 * y + me), 8), :].astype(bf16)
            theirs = r.blocks[rows_at(64 * i + 8 * (2 * y + 1 - me), 8), :].astype(bf16)
            for t in range(3):
                lanes = slice(128 * y, 128 * y + 128)
                weight[name][(t,) + spot + (slice(None), lanes)] = mine[:, 128 * t : 128 * t + 128]
                stage[name][t, 0, 0, 0, 0, :, lanes] = theirs[:, 128 * t : 128 * t + 128]
    for t in range(3):
        weight["d"][t, pos["y"], pos["z"], pos["x"]] = in_buf[6][8 * t : 8 * t + 8, :].astype(bf16)
    pairs["e"].wait()
    gather_start(("e", None), 0)
    for name in MLP:
        gather_start((name, None), 0)
    for name in ("g", "u"):
        pair_start(name)
    fetches[7].wait()
    fetches[8].wait()
    pairs[X_PAIR] = to_sibling(X_PAIR, r.x.at[own_rows], r.x.at[own_rows])
    pairs[SEG_PAIR] = to_sibling(SEG_PAIR, r.seg.at[me], r.seg.at[me])
    pairs[COT_PAIR] = to_sibling(COT_PAIR, r.cot.at[own_rows], r.cot.at[own_rows])
    for name in ("e",) + ATTN:
        if name in CROSS:
            pairs[name].wait()
        gather_finish((name, None), 0)
        gather_start((name, None), 1)
    for name in MLP:
        if name in CROSS:
            pairs[name].wait()
        gather_finish((name, None), 0)
        gather_start((name, None), 1, (0, 1))

    for i in (X_PAIR, SEG_PAIR, COT_PAIR):
        pairs[i].wait()
    freq_lane = lax.rem(lax.broadcasted_iota(jnp.int32, (128, 128), 1), 64).astype(f32)
    inv_freq = jnp.exp(freq_lane * (-2.0 / HD * LOG_THETA))
    sign = jnp.where(lax.broadcasted_iota(jnp.int32, (128, 128), 1) < 64, -1.0, 1.0)
    t_id = lax.broadcasted_iota(jnp.int32, (128, 128), 0)
    u_id = lax.broadcasted_iota(jnp.int32, (128, 128), 1)

    def angles_of(b):
        ids = jnp.broadcast_to(r.seg[b, 0:1, :].astype(f32), (128, 128))
        same = ids == ids.T
        position = jnp.sum(jnp.where(same & (u_id < t_id), 1.0, 0.0), axis=1, keepdims=True)
        r.mask[b] = jnp.where(same & (u_id <= t_id), 1.0, 0.0)
        angles = position * inv_freq
        r.cos[128 * b : 128 * b + 128, :] = jnp.cos(angles)
        r.sin[128 * b : 128 * b + 128, :] = jnp.sin(angles) * sign

    angles_of(0)
    for name in ATTN:
        gather_forward((name, None), 1)
    for name in MLP:
        gather_start((name, None), 1, (2, 3))
    angles_of(1)
    gather_finish(("e", None), 1)
    gather_start(("e", None), 2)
    for name in ATTN:
        gather_finish((name, None), 1)
        gather_start((name, None), 2)
    for name in MLP:
        gather_forward((name, None), 1)

    unit_lane = lax.broadcasted_iota(jnp.int32, (1024, 128), 1)
    unit_row = lax.broadcasted_iota(jnp.int32, (1024, 128), 0) & 7
    r.eighths[0] = jnp.where(unit_lane == unit_row, 1.0, 0.0).astype(bf16)
    r.eighths[1] = jnp.where(unit_lane == unit_row + 8, 1.0, 0.0).astype(bf16)
    owner = lax.broadcasted_iota(jnp.int32, (128, 1024), 1) >> 3
    owned = owner == lax.broadcasted_iota(jnp.int32, (128, 1024), 0)
    pick = ((row_id == 2) & (lane_id == 16)) | ((row_id == 3) & (lane_id == 17))
    pick = jnp.where(pick, 1.0, 0.0).astype(bf16)
    gather_finish(("e", None), 2)
    table = weight["e"][...].reshape(128, 128).astype(bf16)
    for i in range(2):
        spread = jnp.where(owned, dot_nt(table, r.eighths[i]), 0.0)
        r.gain_rows[i : i + 1, :] = jnp.sum(spread, axis=0, keepdims=True)
    r.head_gains[...] = dot_nt(pick, table)
    gain_in, gain_mid = r.gain_rows.at[0:1], r.gain_rows.at[1:2]
    gain_query, gain_key = r.head_gains.at[2:3], r.head_gains.at[3:4]

    def rows_of(i, size=32):
        return pl.ds(pl.multiple_of(i * size, size), size)

    def norm_in(i):
        x = r.x[rows_of(i), :].astype(f32)
        r.normed[rows_of(i), :] = (x * inverse_rms(x) * gain_in[...]).astype(bf16)

    loop(8, norm_in)
    normed, cot = r.normed, r.cot
    for name in ATTN:
        gather_forward((name, None), 2)
    for name in MLP:
        gather_finish((name, None), 1)
    for name in MLP:
        gather_start((name, 0), 2)
    for name in MLP:
        gather_start((name, 1), 2, (0, 1))
    for name in ATTN:
        gather_finish((name, None), 2)

    def project_q(i):
        lanes = lanes_at(i * 512, 512)
        r.q_raw[:, lanes] = dot(normed[...], weight["q"][..., lanes].reshape(1024, 512))

    loop(2, project_q)
    r.k_raw[...] = dot(normed[...], weight["b"][..., :512].reshape(1024, 512))
    r.values[...] = dot(normed[...], weight["b"][..., 512:].reshape(1024, 512)).astype(bf16)

    def rotate(vector, cos_part, sin_part):
        return vector * cos_part + pltpu.roll(vector, 64, 1) * sin_part

    def turn(src, dst, gain):
        def head(h):
            lanes = lanes_at(h * 128, 128)
            raw = src[:, lanes]
            turned = rotate(raw * inverse_rms(raw) * gain[...], r.cos[...], r.sin[...])
            dst[:, lanes] = turned.astype(bf16)

        return head

    loop(8, turn(r.q_raw, r.q_rot, gain_query))
    loop(4, turn(r.k_raw, r.k_rot, gain_key))

    for name in MLP:
        gather_forward((name, 0), 2)
    for name in MLP:
        gather_start((name, 1), 2, (2, 3))
    for name in MLP:
        gather_start((name, 2), 2, (0, 1))

    def both_heads(ref, rows, m):
        first = ref[rows, lanes_at(m * 256, 128)]
        second = ref[rows, lanes_at(m * 256 + 128, 128)]
        return jnp.concatenate([first, second], axis=0)

    def attend(i):
        b, m = i // 4, lax.rem(i, 4)
        rows = pl.ds(pl.multiple_of(b * 128, 128), 128)
        lanes = lanes_at(m * 128, 128)
        scores = dot_nt(both_heads(r.q_rot, rows, m), r.k_rot[rows, lanes]) * SCALE
        mask = r.mask[b]
        masked = jnp.where(jnp.concatenate([mask, mask], axis=0) > 0.0, scores, -1e30)
        terms = jnp.exp(masked - jnp.max(masked, axis=-1, keepdims=True))
        probs = terms / jnp.sum(terms, axis=-1, keepdims=True)
        r.probs[i] = probs
        got = dot(probs.astype(bf16), r.values[rows, lanes]).astype(bf16)
        r.attended[rows, lanes_at(m * 256, 128)] = got[:128]
        r.attended[rows, lanes_at(m * 256 + 128, 128)] = got[128:]

    loop(8, attend)
    attended = r.attended

    def project_out(i):
        lanes = lanes_at(i * 512, 512)
        r.out_part[:, lanes] = dot(attended[...], weight["o"][..., lanes].reshape(1024, 512))

    loop(2, project_out)
    out_copy = to_sibling(OUT_PAIR, r.out_part, r.out_other)
    for name in MLP:
        gather_forward((name, 1), 2)
    for name in MLP:
        gather_start((name, 2), 2, (2, 3))
    out_copy.wait()

    def norm_mid(i):
        rows = rows_of(i)
        hidden = r.x[rows, :].astype(f32) + (r.out_part[rows, :] + r.out_other[rows, :])
        r.hidden[rows, :] = hidden
        r.mid_low[rows, :] = (hidden * inverse_rms(hidden) * gain_mid[...]).astype(bf16)

    loop(8, norm_mid)
    mid_low, mixed, d_gate, d_up = r.mid_low, r.mixed, r.d_gate, r.d_up

    def feed(t):
        gate = dot(mid_low[...], weight["g"][t].reshape(1024, 512))
        up = dot(mid_low[...], weight["u"][t].reshape(1024, 512))
        d_mixed = dot_nt(cot[...], weight["d"][t].reshape(512, 1024))
        sig = jax.nn.sigmoid(gate)
        act = gate * sig
        mixed[...] = (act * up).astype(bf16)
        d_gate[...] = (d_mixed * up * sig * (1.0 + gate * (1.0 - sig))).astype(bf16)
        d_up[...] = (d_mixed * act).astype(bf16)

        def mid_back(i):
            y_pair, lanes = pl.ds(2 * i, 2), lanes_at(i * 512, 512)
            got = dot_nt(d_gate[...], weight["g"][t, y_pair].reshape(512, 512))
            got += dot_nt(d_up[...], weight["u"][t, y_pair].reshape(512, 512))
            r.mid_part[:, lanes] = got if t == 0 else r.mid_part[:, lanes] + got

        def project_down(i):
            lanes = lanes_at(i * 512, 512)
            got = dot(mixed[...], weight["d"][t, ..., lanes].reshape(512, 512))
            r.down_part[:, lanes] = got if t == 0 else r.down_part[:, lanes] + got

        loop(2, mid_back)
        if t == 2:
            pairs[MID_PAIR] = to_sibling(MID_PAIR, r.mid_part, r.mid_other)
        loop(2, project_down)

    def grads(t):
        def grad_down(i):
            got = dot_tn(mixed[:, lanes_at(i * 256, 256)], cot[...]).astype(bf16)
            weight["d"][t, pl.ds(2 * i, 2)] = got.reshape(2, 4, 4, 8, 1024)

        def grad_gate(i):
            left = mid_low[:, lanes_at(i * 512, 512)]
            weight["g"][t, pl.ds(2 * i, 2)] = dot_tn(left, d_gate[...]).astype(bf16).reshape(2, 2, 4, 4, 8, 512)
            weight["u"][t, pl.ds(2 * i, 2)] = dot_tn(left, d_up[...]).astype(bf16).reshape(2, 2, 4, 4, 8, 512)

        loop(2, grad_down)
        loop(2, grad_gate)

    def sends_done(item, phases):
        for phase in phases:
            wait_for(0, item, phase, 0, 3)

    for name in MLP:
        gather_finish((name, 0), 2)
    feed(0)
    for name in MLP:
        gather_forward((name, 2), 2)
    for name in MLP:
        sends_done((name, None), (0, 1))
        sends_done((name, 0), (2,))
    grads(0)
    for name in MLP:
        sum_start((name, 0), 0)
    for name in MLP:
        gather_finish((name, 1), 2)
    feed(1)
    for name in MLP:
        sends_done((name, 1), (2,))
    grads(1)
    for name in MLP:
        sum_start((name, 1), 0)
    for name in MLP:
        gather_finish((name, 2), 2)
    feed(2)
    for name in MLP:
        sends_done((name, 2), (2,))
    grads(2)
    for name in MLP:
        sum_start((name, 2), 0)
    down_copy = to_sibling(DOWN_PAIR, r.down_part.at[other_rows], r.down_other)
    for name in MLP:
        sum_middle((name, 0), 0)
    pairs[MID_PAIR].wait()

    r.gain_sums[...] = jnp.zeros((8, 1024), f32)
    r.head_sums[...] = jnp.zeros((8, 128), f32)

    def res_back(i):
        rows = rows_of(i)
        hidden = r.hidden[rows, :]
        inverse = inverse_rms(hidden)
        unit = hidden * inverse
        part = r.mid_part[rows, :]
        r.gain_sums[1:2, :] += jnp.sum(part * unit, axis=0, keepdims=True)
        d_mid = part + r.mid_other[rows, :]
        d_res = cot[rows, :].astype(f32) + norm_backward(d_mid, unit, inverse, gain_mid[...])
        r.d_res[rows, :] = d_res
        r.d_res_low[rows, :] = d_res.astype(bf16)

    loop(8, res_back)
    d_res_low = r.d_res_low

    def attn_back(i):
        two = weight["o"][pl.ds(2 * i, 2)].reshape(512, 1024)
        r.d_attn[:, lanes_at(i * 512, 512)] = dot_nt(d_res_low[...], two).astype(bf16)

    loop(2, attn_back)
    for name in ATTN + ("e",):
        sends_done((name, None), (0, 1, 2))

    def grad_of(name, left, right):
        def rows(i):
            got = dot_tn(left[:, lanes_at(i * 512, 512)], right[...]).astype(bf16)
            weight[name][pl.ds(2 * i, 2)] = got.reshape((2,) + SHAPES[name][1:])

        loop(2, rows)

    grad_of("o", attended, d_res_low)
    for name in MLP:
        sum_middle((name, 1), 0)

    def head_back(grad, raw, gain):
        inverse = inverse_rms(raw)
        unit = raw * inverse
        return jnp.sum(grad * unit, axis=0, keepdims=True), norm_backward(grad, unit, inverse, gain[...])

    def attend_back(i):
        b, m = i // 4, lax.rem(i, 4)
        rows = pl.ds(pl.multiple_of(b * 128, 128), 128)
        lanes = lanes_at(m * 128, 128)
        d_att = both_heads(r.d_attn, rows, m)
        query, key = both_heads(r.q_rot, rows, m), r.k_rot[rows, lanes]
        probs = r.probs[i]
        d_probs = dot_nt(d_att, r.values[rows, lanes])
        r.d_b[rows, lanes_at(512 + m * 128, 128)] = dot_tn(probs.astype(bf16), d_att).astype(bf16)
        d_scores = (probs * (d_probs - jnp.sum(d_probs * probs, axis=-1, keepdims=True))).astype(bf16)
        d_query = dot(d_scores, key) * SCALE
        d_key = dot_tn(d_scores, query) * SCALE
        cos_part, sin_part = r.cos[rows, :], -r.sin[rows, :]
        for j in range(2):
            spots = lanes_at(m * 256 + 128 * j, 128)
            d_unit = rotate(d_query[128 * j : 128 * j + 128], cos_part, sin_part)
            total, d_raw = head_back(d_unit, r.q_raw[rows, spots], gain_query)
            r.head_sums[2:3, :] += total
            r.d_q[rows, spots] = d_raw.astype(bf16)
        total, d_raw = head_back(rotate(d_key, cos_part, sin_part), r.k_raw[rows, lanes], gain_key)
        r.head_sums[3:4, :] += total
        r.d_b[rows, lanes] = d_raw.astype(bf16)

    loop(8, attend_back)
    for name in MLP:
        sum_middle((name, 2), 0)
    sum_start(("o", None), 0)

    def in_back(i):
        y_pair = pl.ds(2 * i, 2)
        got = dot_nt(r.d_q[...], weight["q"][y_pair].reshape(512, 1024))
        got += dot_nt(r.d_b[...], weight["b"][y_pair].reshape(512, 1024))
        r.in_part[:, lanes_at(i * 512, 512)] = got

    loop(2, in_back)
    in_copy = to_sibling(IN_PAIR, r.in_part.at[other_rows], r.in_other)
    grad_of("q", normed, r.d_q)
    sum_start(("q", None), 0)
    grad_of("b", normed, r.d_b)
    sum_start(("b", None), 0)

    def gain_back(i):
        x = r.x[rows_of(i), :].astype(f32)
        unit = x * inverse_rms(x)
        r.gain_sums[0:1, :] += jnp.sum(r.in_part[rows_of(i), :] * unit, axis=0, keepdims=True)

    loop(8, gain_back)
    table = dot_tn(r.head_sums[...].astype(bf16), pick)
    for i in range(2):
        table += dot(jnp.where(owned, r.gain_sums[i : i + 1, :], 0.0).astype(bf16), r.eighths[i])
    weight["e"][...] = table.reshape(SHAPES["e"])
    sum_start(("e", None), 0)

    down_copy.wait()

    def finish_out(i):
        rows = rows_of(i)
        mine = pl.ds(pl.multiple_of(me * 128 + i * 32, 32), 32)
        down = r.down_part[mine, :] + r.down_other[rows, :]
        layer_out[rows, :] = (r.hidden[mine, :] + down).astype(bf16)

    loop(4, finish_out)
    for t in range(3):
        for name in MLP:
            sum_end((name, t), 0)
    in_copy.wait()

    def finish_in(i):
        rows = rows_of(i)
        mine = pl.ds(pl.multiple_of(me * 128 + i * 32, 32), 32)
        d_normed = r.in_part[mine, :] + r.in_other[rows, :]
        x = r.x[mine, :].astype(f32)
        inverse = inverse_rms(x)
        input_grad[rows, :] = r.d_res[mine, :] + norm_backward(d_normed, x * inverse, inverse, gain_in[...])

    loop(4, finish_in)

    for name in ATTN:
        sum_middle((name, None), 0)
    for name in MLP:
        sum_start((name, None), 1)
    sum_end(("e", None), 0)
    sum_start(("e", None), 1)
    for name in ATTN:
        sum_end((name, None), 0)
        sum_start((name, None), 1)
    for name in MLP:
        sum_middle((name, None), 1)
    sum_end(("e", None), 1)
    sum_start(("e", None), 2)
    for name in ATTN:
        sum_middle((name, None), 1)
    for name in MLP:
        sum_end((name, None), 1)
        sum_start((name, None), 2)
    for name in ATTN:
        sum_end((name, None), 1)
        sum_start((name, None), 2)
    sum_end(("e", None), 2)
    swap = to_sibling(FIN_PAIR + SPLIT.index("e"), fin["e"].at[1 - me], rx["e"])
    for name in MLP:
        sum_end((name, None), 2)
    rest = r.blocks[...]
    total = jnp.zeros((128, 384), f32)
    for _ in range(3):
        head = rest.astype(bf16)
        total += dot_nt(head, r.perm[...])
        rest = rest - head.astype(f32)
    for i, out in ((0, 6), (1, 7)):
        for b in range(8):
            out_buf[out][:, 384 * b : 384 * b + 384] = total[64 * i + 8 * b : 64 * i + 8 * b + 8, :]
    swap.wait()
    row = fin["e"][me] + rx["e"][...]
    for ref, first, count in zip(out_buf[9:], (0, 8, 16, 17), (8, 8, 1, 1)):
        ref[...] = row[0, first : first + count]
    for name in ATTN:
        sum_end((name, None), 2)
    for item, phase in SUMS:
        wait_for(1, item, phase, 0, 3)


def finish_kernel(*refs):
    n = len(OUTS)
    ins, outs, sems = refs[:n], refs[n : 2 * n], refs[-1]
    copies = [pltpu.make_async_copy(ins[i], outs[i], sems.at[i]) for i in range(n)]
    for copy in copies:
        copy.start()
    for copy in copies:
        copy.wait()


def body(*args):
    hbm = pl.BlockSpec(memory_space=pl.ANY)
    vmem = pl.BlockSpec(memory_space=pltpu.VMEM)
    parts = pl.pallas_call(
        layer_kernel,
        out_shape=[pltpu.VMEM(*entry) for entry in OUTS],
        in_specs=[hbm] * 14,
        out_specs=[vmem] * len(OUTS),
        scratch_shapes=[pltpu.VMEM(*entry) for group in GROUPS for entry in group.values()]
        + [pltpu.SMEM((size,), f32) for size in (8, 8, 1, 1)]
        + [pltpu.SemaphoreType.DMA((len(SEMS),))]
        + [pltpu.SemaphoreType.DMA((PAIRS,))] * 2
        + [pltpu.SemaphoreType.DMA((14,))],
        compiler_params=pltpu.CompilerParams(
            collective_id=1, has_side_effects=True, vmem_limit_bytes=57 << 20
        ),
        name="layer",
    )(*args)
    parts = [pltpu.with_memory_space_constraint(part, pltpu.VMEM) for part in parts]
    (
        layer_out, input_grad, grad_q, grad_k, grad_v, grad_o, grad_g, grad_u, grad_d, norm_gain, mlp_gain, query_gain, key_gain,
    ) = pl.pallas_call(
        finish_kernel,
        out_shape=[jax.ShapeDtypeStruct(*entry) for entry in OUTS],
        in_specs=[vmem] * len(OUTS),
        out_specs=[hbm] * len(OUTS),
        scratch_shapes=[pltpu.SemaphoreType.DMA((len(OUTS),))],
        name="finish",
    )(*parts)
    return (
        layer_out, input_grad, norm_gain, grad_q, grad_k, grad_v, query_gain, key_gain, grad_o, mlp_gain, grad_g, grad_u, grad_d,
    )


def solution(mesh):
    rows = P(("dp", "fsdp"), None)
    flat = P(("dp", "fsdp"))
    return jax.shard_map(
        body,
        mesh=mesh,
        in_specs=(rows, rows, flat, rows, rows, rows, flat, flat, rows, flat, rows, rows, rows, rows),
        out_specs=(rows, rows, flat, rows, rows, rows, flat, flat, rows, flat, rows, rows, rows),
        check_vma=False,
    )
```

```python
import types

import jax
import jax.numpy as jnp
from jax import lax
from jax.experimental import pallas as pl
from jax.experimental.pallas import tpu as pltpu
from jax.sharding import PartitionSpec as P

HD = 128
EPS = 1e-06
LOG_THETA = 13.815510557964274
SCALE = HD ** (-0.5)

bf16 = jnp.bfloat16
f32 = jnp.float32
MESH = pl.DeviceIdType.MESH

SHAPES = dict(
    q=(4, 2, 4, 4, 8, 1024),
    b=(4, 2, 4, 4, 8, 1024),
    o=(4, 4, 4, 2, 8, 1024),
    e=(4, 2, 4, 4, 1, 128),
    g=(3, 4, 2, 4, 4, 8, 512),
    u=(3, 4, 2, 4, 4, 8, 512),
    d=(3, 4, 4, 4, 8, 1024),
)
NAMES = tuple(SHAPES)
SPLIT = ("q", "b", "e", "g", "u")
CROSS = ("q", "b", "g", "u")
ATTN = ("q", "b", "o")
MLP = ("g", "u", "d")
ORDER = dict(q="xyz", g="xyz", b="yzx", u="yzx", o="zxy", d="zxy", e="zxy")
DTYPE = {name: f32 if name == "e" else bf16 for name in NAMES}


def coords():
    dp = lax.axis_index("dp")
    fs = lax.axis_index("fsdp")
    return dict(y=dp // 2, c=lax.rem(dp, 2), z=fs // 4, x=lax.rem(fs, 4))


def device(pos, axis=None, step=0):
    pos = dict(pos)
    if axis == "c":
        pos["c"] = 1 - pos["c"]
    elif axis is not None:
        pos[axis] = lax.rem(pos[axis] + step + 4, 4)
    return (pos["y"] * 2 + pos["c"], pos["z"] * 4 + pos["x"])


def item_shape(item):
    name, third = item
    return SHAPES[name] if third is None else SHAPES[name][1:]


def lead_of(item):
    return 1 if item[0] in MLP and item[1] is None else 0


def axis_places(item):
    lead = lead_of(item)
    if item[0] in SPLIT:
        return dict(y=lead, z=lead + 2, x=lead + 3)
    return dict(y=lead, z=lead + 1, x=lead + 2)


def block(ref, item, at, half=None):
    shape = item_shape(item)
    index = [slice(None)] * len(shape)
    for axis, place in axis_places(item).items():
        if axis in at:
            start, size = at[axis] if isinstance(at[axis], tuple) else (at[axis], 1)
            index[place] = pl.ds(start, size)
    if half is not None:
        if item[0] in SPLIT:
            index[lead_of(item) + 1] = pl.ds(half, 1)
        else:
            index[-1] = pl.ds(half * (shape[-1] // 2), shape[-1] // 2)
    return ref.at[tuple(index)]


def half_of(ref, item, half):
    return block(ref, item, {}, half)


def merged(item, fixed):
    shape = list(item_shape(item))
    for axis in fixed:
        shape[axis_places(item)[axis]] = 1
    return tuple(shape)


def halved(item, shape):
    shape = list(shape)
    shape[lead_of(item) + 1 if item[0] in SPLIT else -1] //= 2
    return tuple(shape)


def add_into(dst, sources, shape):
    lead = shape[:-3]
    count = 1
    for extent in lead:
        count *= extent

    def step(i, carry):
        index, rest = [], i
        for extent in reversed(lead):
            index.append(lax.rem(rest, extent))
            rest = rest // extent
        index = tuple(reversed(index))
        total = sources[0][index].astype(f32)
        for source in sources[1:]:
            total = total + source[index].astype(f32)
        dst[index] = total.astype(dst.dtype)
        return carry

    lax.fori_loop(0, count, step, 0)


def dot(left, right):
    return jnp.dot(left, right, preferred_element_type=f32)


def dot_nt(left, right):
    return lax.dot_general(left, right, (((1,), (1,)), ((), ())), preferred_element_type=f32)


def dot_tn(left, right):
    return lax.dot_general(left, right, (((0,), (0,)), ((), ())), preferred_element_type=f32)


def inverse_rms(vector):
    return lax.rsqrt(jnp.mean(vector * vector, axis=-1, keepdims=True) + EPS)


def norm_backward(grad_in, unit_vec, inverse, gain_vec):
    scaled = grad_in * gain_vec
    return inverse * (scaled - unit_vec * jnp.mean(scaled * unit_vec, axis=-1, keepdims=True))


def lanes_at(start, size):
    return pl.ds(pl.multiple_of(start, 128), size)


def rows_at(start, size):
    return pl.ds(pl.multiple_of(start, 8), size)


def loop(count, body):
    def step(i, carry):
        body(i)
        return carry

    lax.fori_loop(0, count, step, 0)


ALL = (("q", None), ("b", None), ("o", None), ("e", None), ("g", None), ("u", None), ("d", None))
THIRDS = tuple((name, t) for t in range(3) for name in MLP)
ITEMS = ALL + THIRDS
SUMS = tuple((item, phase) for item in ALL for phase in range(3) if item[0] not in MLP or phase > 0)
SUMS += tuple((item, 0) for item in THIRDS)


def is_direct(item, phase):
    return phase == 2 or item[0] == "e"


GATHERS = tuple((item, phase) for item in ALL for phase in range(3) if item[0] not in MLP or phase < 2)
GATHERS += tuple((item, 2) for item in THIRDS)
SEMS = {}
for _kind, _steps in enumerate((GATHERS, SUMS)):
    for _item, _phase in _steps:
        if _item[0] in ("u", "d"):
            continue
        _direct = is_direct(_item, _phase) if _kind else _phase == 0 or _item[0] == "e"
        for _use in range(2 if _direct else 3):
            SEMS[_kind, _item, _phase, _use] = len(SEMS)
W = {name: (SHAPES[name], DTYPE[name]) for name in NAMES}
ROWS = {name: halved((name, None), merged((name, None), ORDER[name])) for name in CROSS}
STAGE = {name: (ROWS[name], bf16) for name in CROSS}
RX = {name: (ROWS[name], bf16) for name in CROSS}
STAGE["e"] = RX["e"] = ((1, 128), f32)
FIN = dict(e=((2, 1, 128), f32))
FAR, NEAR = {}, {}
for _item, _phase in SUMS:
    _shape = merged(_item, ORDER[_item[0]][::-1][: _phase + 1])
    for _way in range(2):
        NEAR[_item, _phase, _way] = (_shape, DTYPE[_item[0]])
        if not is_direct(_item, _phase):
            FAR[_item, _phase, _way] = (halved(_item, _shape), DTYPE[_item[0]])
    if is_direct(_item, _phase):
        FAR[_item, _phase, 2] = (_shape, DTYPE[_item[0]])
INS = (
    ((8, 2048), f32), ((8, 1024), f32), ((8, 1024), f32), ((16, 1024), f32), ((8, 3072), f32), ((8, 3072), f32), ((24, 1024), f32),
)
OUTS = (((128, 1024), bf16), ((128, 1024), f32)) + INS + tuple(((size,), f32) for size in (8, 8, 1, 1))
IN_BUF = {i: entry for i, entry in enumerate(INS)}
FLAT = dict(
    x=((256, 1024), bf16),
    cot=((256, 1024), bf16),
    seg=((2, 8, 128), jnp.int32),
    seg_in=((1, 128), jnp.int32),
    perm=((384, 384), bf16),
    blocks=((128, 384), f32),
    eighths=((2, 1024, 128), bf16),
    gain_rows=((8, 1024), f32),
    head_gains=((8, 128), f32),
    gain_sums=((8, 1024), f32),
    head_sums=((8, 128), f32),
    mask=((2, 128, 128), f32),
    cos=((256, 128), f32),
    sin=((256, 128), f32),
    normed=((256, 1024), bf16),
    q_raw=((256, 1024), f32),
    k_raw=((256, 512), f32),
    values=((256, 512), bf16),
    q_rot=((256, 1024), bf16),
    k_rot=((256, 512), bf16),
    probs=((8, 256, 128), f32),
    attended=((256, 1024), bf16),
    out_part=((256, 1024), f32),
    out_other=((256, 1024), f32),
    hidden=((256, 1024), f32),
    mid_low=((256, 1024), bf16),
    mixed=((256, 512), bf16),
    d_gate=((256, 512), bf16),
    d_up=((256, 512), bf16),
    down_part=((256, 1024), f32),
    down_other=((128, 1024), f32),
    mid_part=((256, 1024), f32),
    mid_other=((256, 1024), f32),
    d_res=((256, 1024), f32),
    d_res_low=((256, 1024), bf16),
    d_attn=((256, 1024), bf16),
    d_q=((256, 1024), bf16),
    d_b=((256, 1024), bf16),
    in_part=((256, 1024), f32),
    in_other=((128, 1024), f32),
)
GROUPS = (W, STAGE, FIN, RX, FAR, NEAR, IN_BUF, FLAT)
X_PAIR, COT_PAIR, SEG_PAIR, OUT_PAIR, DOWN_PAIR, MID_PAIR, IN_PAIR, STAGE_PAIR = range(8)
FIN_PAIR = STAGE_PAIR + len(SPLIT)
PAIRS = FIN_PAIR + len(SPLIT)


def layer_kernel(
    tokens, segment, norm_gain, w_query, w_key, w_value, query_gain, key_gain, w_out, mlp_gain, w_gate, w_up, w_down,
    cotangent, *refs,
):
    refs = list(refs)
    out_buf = [refs.pop(0) for _ in OUTS]
    held = []
    for group in GROUPS:
        held.append({key: refs.pop(0) for key in group})
    weight, stage, fin, rx, far_of, near_of, in_buf, flat = held
    r = types.SimpleNamespace(**flat)
    gains_in, (sems, pair_send, pair_recv, local_in) = refs[:4], refs[4:]
    pos = coords()
    me = pos["c"]
    sibling = device(pos, "c")
    flipped = dict(pos, c=1 - me)
    own_rows = pl.ds(pl.multiple_of(me * 128, 128), 128)
    other_rows = pl.ds(pl.multiple_of((1 - me) * 128, 128), 128)
    layer_out, input_grad = out_buf[0], out_buf[1]

    barrier = pltpu.get_barrier_semaphore()
    others = [sibling]
    for axis in "xyz":
        others += [device(pos, axis, step) for step in (1, -1, 2)]
    for axis in "xy":
        others += [device(flipped, axis, step) for step in (1, -1, 2)]
    for other in others:
        pl.semaphore_signal(barrier, inc=1, device_id=other, device_id_type=MESH)
    fetches = []
    for i, src in enumerate((w_query, w_key, w_value, w_out, w_gate, w_up, w_down)):
        fetches.append(pltpu.make_async_copy(src, in_buf[i], local_in.at[i]))
    fetches.append(pltpu.make_async_copy(tokens, r.x.at[own_rows], local_in.at[7]))
    fetches.append(pltpu.make_async_copy(cotangent, r.cot.at[own_rows], local_in.at[8]))
    small = ((norm_gain, gains_in[0]), (mlp_gain, gains_in[1]), (query_gain, gains_in[2]), (key_gain, gains_in[3]), (segment, r.seg_in))
    for i, (src, dst) in enumerate(small):
        fetches.append(pltpu.make_async_copy(src, dst, local_in.at[9 + i]))
    for copy in fetches[9:] + fetches[:9]:
        copy.start()
    norm_gain, mlp_gain, query_gain, key_gain = gains_in

    def remote(src, dst, send_sem, recv_sem, target):
        return pltpu.make_async_remote_copy(
            src_ref=src, dst_ref=dst, send_sem=send_sem, recv_sem=recv_sem, device_id=target, device_id_type=MESH
        )

    def to_sibling(index, src, dst):
        copy = remote(src, dst, pair_send.at[index], pair_recv.at[index], sibling)
        copy.start()
        return copy

    def sem(kind, item, phase, use):
        name, third = item
        return sems.at[SEMS[kind, ("g" if name in MLP else name, third), phase, use]]

    def send(kind, item, phase, use, src, dst, target):
        remote(src, dst, sem(kind, item, phase, 0), sem(kind, item, phase, use), target).start()

    def wait_for(kind, item, phase, use, count):
        name, third = item
        if name in ("u", "d"):
            return
        order = ORDER[name] if kind == 0 else ORDER[name][::-1]
        fixed = order[phase + 1 :] if kind == 0 else order[:phase]
        at = {a: pos[a] for a in fixed}
        if name == "g" and third is None:
            at[fixed[0]] = (0, 3)
        like = block(weight[name], (name, None), {**at, order[phase]: (0, count)})
        pltpu.make_async_copy(like, like, sem(kind, item, phase, use)).wait()

    def view(item):
        name, third = item
        return weight[name] if third is None else weight[name].at[third]

    pairs = {}

    def gather_start(item, phase, keys=(0, 1, 2, 3)):
        order = ORDER[item[0]]
        axis = order[phase]
        at = {a: pos[a] for a in order[phase:]}
        if phase == 0 and item[0] in CROSS:
            mine = block(view(item), item, at, me)
            for step in (1, -1, 2):
                send(0, item, phase, 1, mine, mine, device(pos, axis, step))
                send(0, item, phase, 1, stage[item[0]], mine, device(flipped, axis, step))
            return
        if phase == 0 or item[0] == "e":
            for step in (1, -1, 2):
                src = block(view(item), item, at)
                send(0, item, phase, 1, src, src, device(pos, axis, step))
            return
        for key, half, step in ((0, 0, 1), (1, 1, -1), (2, 1, 1), (3, 0, -1)):
            if key in keys:
                src = block(view(item), item, at, half)
                send(0, item, phase, 1 if key < 2 else 2, src, src, device(pos, axis, step))

    def gather_forward(item, phase):
        order = ORDER[item[0]]
        axis = order[phase]
        at = {a: pos[a] for a in order[phase:]}
        wait_for(0, item, phase, 1, 1)
        for half, step in ((0, 1), (1, -1)):
            src = block(view(item), item, {**at, axis: lax.rem(pos[axis] + 4 - step, 4)}, half)
            send(0, item, phase, 2, src, src, device(pos, axis, step))

    def gather_finish(item, phase):
        if phase == 0 or item[0] == "e":
            wait_for(0, item, phase, 1, 3)
        else:
            wait_for(0, item, phase, 2, 2)

    def sum_start(item, phase):
        order = ORDER[item[0]][::-1]
        axis = order[phase]
        at = {a: pos[a] for a in order[:phase]}
        ahead, behind = lax.rem(pos[axis] + 1, 4), lax.rem(pos[axis] + 3, 4)
        opposite = lax.rem(pos[axis] + 2, 4)
        up, down, across = device(pos, axis, 1), device(pos, axis, -1), device(pos, axis, 2)
        cur = view(item)
        near_up, near_down = near_of[item, phase, 0], near_of[item, phase, 1]

        def part(place, half=None):
            return block(cur, item, {**at, axis: place}, half)

        if phase == 2 and item[0] in CROSS:
            ways = ((opposite, far_of[item, phase, 2], 2), (ahead, near_up, 1), (behind, near_down, -1))
            for place, dst, step in ways:
                slot = half_of(dst, item, me)
                send(1, item, phase, 1, part(place, me), slot, device(pos, axis, step))
                send(1, item, phase, 1, part(place, 1 - me), slot, device(flipped, axis, step))
            index = FIN_PAIR + SPLIT.index(item[0])
            pairs[index] = to_sibling(index, block(cur, item, pos, 1 - me), rx[item[0]])
        elif is_direct(item, phase):
            send(1, item, phase, 1, part(opposite), far_of[item, phase, 2], across)
            send(1, item, phase, 1, part(ahead), near_up, up)
            send(1, item, phase, 1, part(behind), near_down, down)
        else:
            send(1, item, phase, 1, part(opposite, 0), far_of[item, phase, 0], up)
            send(1, item, phase, 1, part(opposite, 1), far_of[item, phase, 1], down)
            send(1, item, phase, 2, part(ahead, 1), half_of(near_up, item, 1), up)
            send(1, item, phase, 2, part(behind, 0), half_of(near_down, item, 0), down)

    def sum_middle(item, phase):
        order = ORDER[item[0]][::-1]
        axis = order[phase]
        at = {a: pos[a] for a in order[:phase]}
        shape = halved(item, merged(item, order[: phase + 1]))
        wait_for(1, item, phase, 1, 1)
        for half, step in ((0, 1), (1, -1)):
            far, near = far_of[item, phase, half], near_of[item, phase, half]
            mine = block(view(item), item, {**at, axis: lax.rem(pos[axis] + 4 + step, 4)}, half)
            add_into(far, [far, mine], shape)
            send(1, item, phase, 2, far, half_of(near, item, half), device(pos, axis, step))

    def sum_end(item, phase):
        order = ORDER[item[0]][::-1]
        at = {a: pos[a] for a in order[: phase + 1]}
        sources = [block(view(item), item, at), near_of[item, phase, 0], near_of[item, phase, 1]]
        if is_direct(item, phase):
            sources.append(far_of[item, phase, 2])
            wait_for(1, item, phase, 1, 3)
        else:
            wait_for(1, item, phase, 2, 2)
        if phase < 2:
            add_into(sources[0], sources, merged(item, order[: phase + 1]))
            return

        name = item[0]

        def total(place, first=None):
            value = (sources[0] if first is None else first)[place].astype(f32)
            for source in sources[1:]:
                value = value + source[place].astype(f32)
            return value

        def both(t):
            lead = () if t is None else (t,)
            mine = total(lead + (0, me, 0, 0))
            theirs = rx[name][lead + (0, 0, 0, 0)].astype(f32)
            for source in sources[1:]:
                theirs = theirs + source[lead + (0, 1 - me, 0, 0)].astype(f32)
            return mine, theirs

        if name in CROSS:
            pairs[FIN_PAIR + SPLIT.index(name)].wait()
        if name == "d":
            for t in range(3):
                out_buf[8][8 * t : 8 * t + 8, :] = total((t, 0, 0, 0))
        elif name == "o":
            for t in range(2):
                out_buf[5][8 * t : 8 * t + 8, :] = total((0, 0, 0, t))
        elif name == "e":
            for c in range(2):
                fin["e"][c] = total((0, c, 0, 0))
        elif name in MLP:
            start = 0 if name == "g" else 64
            for t in range(3):
                columns = slice(128 * t, 128 * t + 128)
                for core, value in zip((me, 1 - me), both(t)):
                    for y in range(4):
                        r.blocks[rows_at(start + 8 * (2 * y + core), 8), columns] = value[:, 128 * y : 128 * y + 128]
        else:
            layouts = ((2, 4, 256, 0),) if name == "q" else ((3, 4, 128, 0), (4, 4, 128, 512))
            for core, value in zip((me, 1 - me), both(None)):
                for out, count, width, place in layouts:
                    for i in range(count):
                        lanes = slice(place + i * width, place + (i + 1) * width)
                        out_buf[out][:, lanes_at((2 * i + core) * width, width)] = value[:, lanes]

    spot = (pos["y"], me, pos["z"], pos["x"])

    def stage_columns(name, buf, start, count, width, place):
        for i in range(count):
            lanes = slice(place + i * width, place + (i + 1) * width)
            weight[name][spot + (slice(None), lanes)] = in_buf[buf][:, lanes_at((2 * i + me) * width, width)].astype(bf16)
            theirs = in_buf[buf][:, lanes_at((2 * i + 1 - me) * width, width)].astype(bf16)
            stage[name][0, 0, 0, 0, :, lanes] = theirs

    row_id = lax.broadcasted_iota(jnp.int32, (8, 128), 0)
    lane_id = lax.broadcasted_iota(jnp.int32, (8, 128), 1)
    lane_row = lax.broadcasted_iota(jnp.int32, (1, 128), 1)
    for copy in fetches[9:]:
        copy.wait()
    gains = jnp.zeros((1, 128), f32)
    for i in range(8):
        gains = jnp.where(lane_row == i, norm_gain[i], gains)
        gains = jnp.where(lane_row == 8 + i, mlp_gain[i], gains)
    gains = jnp.where(lane_row == 16, query_gain[0], gains)
    gains = jnp.where(lane_row == 17, key_gain[0], gains).astype(bf16).astype(f32)
    weight["e"][spot] = gains
    stage["e"][...] = gains
    r.seg[me] = jnp.broadcast_to(r.seg_in[...], (8, 128))
    for i in range(4):
        fetches[i].wait()
    stage_columns("q", 0, 0, 4, 256, 0)
    stage_columns("b", 1, 0, 4, 128, 0)
    stage_columns("b", 2, 0, 4, 128, 512)
    for t in range(2):
        weight["o"][pos["y"], pos["z"], pos["x"], t] = in_buf[3][8 * t : 8 * t + 8, :].astype(bf16)

    pl.semaphore_wait(barrier, len(others))

    def pair_start(name):
        index = STAGE_PAIR + SPLIT.index(name)
        dst = weight["e"].at[spot] if name == "e" else block(weight[name], (name, None), pos, me)
        pairs[name] = to_sibling(index, stage[name], dst)

    pair_start("e")
    for name in ATTN:
        gather_start((name, None), 0)
    for name in ("q", "b"):
        pair_start(name)

    to_lane = lax.broadcasted_iota(jnp.int32, (384, 384), 1)
    from_lane = ((to_lane >> 3) & 15) * 24 + (to_lane >> 7) * 8 + (to_lane & 7)
    r.perm[...] = jnp.where(lax.broadcasted_iota(jnp.int32, (384, 384), 0) == from_lane, 1.0, 0.0).astype(bf16)
    for i in range(4, 7):
        fetches[i].wait()
    for i, buf in ((0, 4), (1, 5)):
        for b in range(8):
            r.blocks[64 * i + 8 * b : 64 * i + 8 * b + 8, :] = in_buf[buf][:, 384 * b : 384 * b + 384]
    r.blocks[...] = dot(r.blocks[...].astype(bf16), r.perm[...])
    for i, name in ((0, "g"), (1, "u")):
        for y in range(4):
            mine = r.blocks[rows_at(64 * i + 8 * (2 * y + me), 8), :].astype(bf16)
            theirs = r.blocks[rows_at(64 * i + 8 * (2 * y + 1 - me), 8), :].astype(bf16)
            for t in range(3):
                lanes = slice(128 * y, 128 * y + 128)
                weight[name][(t,) + spot + (slice(None), lanes)] = mine[:, 128 * t : 128 * t + 128]
                stage[name][t, 0, 0, 0, 0, :, lanes] = theirs[:, 128 * t : 128 * t + 128]
    for t in range(3):
        weight["d"][t, pos["y"], pos["z"], pos["x"]] = in_buf[6][8 * t : 8 * t + 8, :].astype(bf16)
    pairs["e"].wait()
    gather_start(("e", None), 0)
    for name in MLP:
        gather_start((name, None), 0)
    for name in ("g", "u"):
        pair_start(name)
    fetches[7].wait()
    fetches[8].wait()
    pairs[X_PAIR] = to_sibling(X_PAIR, r.x.at[own_rows], r.x.at[own_rows])
    pairs[SEG_PAIR] = to_sibling(SEG_PAIR, r.seg.at[me], r.seg.at[me])
    pairs[COT_PAIR] = to_sibling(COT_PAIR, r.cot.at[own_rows], r.cot.at[own_rows])
    for name in ("e",) + ATTN:
        if name in CROSS:
            pairs[name].wait()
        gather_finish((name, None), 0)
        gather_start((name, None), 1)
    for name in MLP:
        if name in CROSS:
            pairs[name].wait()
        gather_finish((name, None), 0)
        gather_start((name, None), 1, (0, 1))

    for i in (X_PAIR, SEG_PAIR, COT_PAIR):
        pairs[i].wait()
    freq_lane = lax.rem(lax.broadcasted_iota(jnp.int32, (128, 128), 1), 64).astype(f32)
    inv_freq = jnp.exp(freq_lane * (-2.0 / HD * LOG_THETA))
    sign = jnp.where(lax.broadcasted_iota(jnp.int32, (128, 128), 1) < 64, -1.0, 1.0)
    t_id = lax.broadcasted_iota(jnp.int32, (128, 128), 0)
    u_id = lax.broadcasted_iota(jnp.int32, (128, 128), 1)

    def angles_of(b):
        ids = jnp.broadcast_to(r.seg[b, 0:1, :].astype(f32), (128, 128))
        same = ids == ids.T
        position = jnp.sum(jnp.where(same & (u_id < t_id), 1.0, 0.0), axis=1, keepdims=True)
        r.mask[b] = jnp.where(same & (u_id <= t_id), 1.0, 0.0)
        angles = position * inv_freq
        r.cos[128 * b : 128 * b + 128, :] = jnp.cos(angles)
        r.sin[128 * b : 128 * b + 128, :] = jnp.sin(angles) * sign

    angles_of(0)
    for name in ATTN:
        gather_forward((name, None), 1)
    for name in MLP:
        gather_start((name, None), 1, (2, 3))
    angles_of(1)
    gather_finish(("e", None), 1)
    gather_start(("e", None), 2)
    for name in ATTN:
        gather_finish((name, None), 1)
        gather_start((name, None), 2)
    for name in MLP:
        gather_forward((name, None), 1)

    unit_lane = lax.broadcasted_iota(jnp.int32, (1024, 128), 1)
    unit_row = lax.broadcasted_iota(jnp.int32, (1024, 128), 0) & 7
    r.eighths[0] = jnp.where(unit_lane == unit_row, 1.0, 0.0).astype(bf16)
    r.eighths[1] = jnp.where(unit_lane == unit_row + 8, 1.0, 0.0).astype(bf16)
    owner = lax.broadcasted_iota(jnp.int32, (128, 1024), 1) >> 3
    owned = owner == lax.broadcasted_iota(jnp.int32, (128, 1024), 0)
    pick = ((row_id == 2) & (lane_id == 16)) | ((row_id == 3) & (lane_id == 17))
    pick = jnp.where(pick, 1.0, 0.0).astype(bf16)
    gather_finish(("e", None), 2)
    table = weight["e"][...].reshape(128, 128).astype(bf16)
    for i in range(2):
        spread = jnp.where(owned, dot_nt(table, r.eighths[i]), 0.0)
        r.gain_rows[i : i + 1, :] = jnp.sum(spread, axis=0, keepdims=True)
    r.head_gains[...] = dot_nt(pick, table)
    gain_in, gain_mid = r.gain_rows.at[0:1], r.gain_rows.at[1:2]
    gain_query, gain_key = r.head_gains.at[2:3], r.head_gains.at[3:4]

    def rows_of(i, size=32):
        return pl.ds(pl.multiple_of(i * size, size), size)

    def norm_in(i):
        x = r.x[rows_of(i), :].astype(f32)
        r.normed[rows_of(i), :] = (x * inverse_rms(x) * gain_in[...]).astype(bf16)

    loop(8, norm_in)
    normed, cot = r.normed, r.cot
    for name in ATTN:
        gather_forward((name, None), 2)
    for name in MLP:
        gather_finish((name, None), 1)
    for name in MLP:
        gather_start((name, 0), 2)
    for name in MLP:
        gather_start((name, 1), 2, (0, 1))
    for name in ATTN:
        gather_finish((name, None), 2)

    def project_q(i):
        lanes = lanes_at(i * 512, 512)
        r.q_raw[:, lanes] = dot(normed[...], weight["q"][..., lanes].reshape(1024, 512))

    loop(2, project_q)
    r.k_raw[...] = dot(normed[...], weight["b"][..., :512].reshape(1024, 512))
    r.values[...] = dot(normed[...], weight["b"][..., 512:].reshape(1024, 512)).astype(bf16)

    def rotate(vector, cos_part, sin_part):
        return vector * cos_part + pltpu.roll(vector, 64, 1) * sin_part

    def turn(src, dst, gain):
        def head(h):
            lanes = lanes_at(h * 128, 128)
            raw = src[:, lanes]
            turned = rotate(raw * inverse_rms(raw) * gain[...], r.cos[...], r.sin[...])
            dst[:, lanes] = turned.astype(bf16)

        return head

    loop(8, turn(r.q_raw, r.q_rot, gain_query))
    loop(4, turn(r.k_raw, r.k_rot, gain_key))

    for name in MLP:
        gather_forward((name, 0), 2)
    for name in MLP:
        gather_start((name, 1), 2, (2, 3))
    for name in MLP:
        gather_start((name, 2), 2, (0, 1))

    def both_heads(ref, rows, m):
        first = ref[rows, lanes_at(m * 256, 128)]
        second = ref[rows, lanes_at(m * 256 + 128, 128)]
        return jnp.concatenate([first, second], axis=0)

    def attend(i):
        b, m = i // 4, lax.rem(i, 4)
        rows = pl.ds(pl.multiple_of(b * 128, 128), 128)
        lanes = lanes_at(m * 128, 128)
        scores = dot_nt(both_heads(r.q_rot, rows, m), r.k_rot[rows, lanes]) * SCALE
        mask = r.mask[b]
        masked = jnp.where(jnp.concatenate([mask, mask], axis=0) > 0.0, scores, -1e30)
        terms = jnp.exp(masked - jnp.max(masked, axis=-1, keepdims=True))
        probs = terms / jnp.sum(terms, axis=-1, keepdims=True)
        r.probs[i] = probs
        got = dot(probs.astype(bf16), r.values[rows, lanes]).astype(bf16)
        r.attended[rows, lanes_at(m * 256, 128)] = got[:128]
        r.attended[rows, lanes_at(m * 256 + 128, 128)] = got[128:]

    loop(8, attend)
    attended = r.attended

    def project_out(i):
        lanes = lanes_at(i * 512, 512)
        r.out_part[:, lanes] = dot(attended[...], weight["o"][..., lanes].reshape(1024, 512))

    loop(2, project_out)
    out_copy = to_sibling(OUT_PAIR, r.out_part, r.out_other)
    for name in MLP:
        gather_forward((name, 1), 2)
    for name in MLP:
        gather_start((name, 2), 2, (2, 3))
    out_copy.wait()

    def norm_mid(i):
        rows = rows_of(i)
        hidden = r.x[rows, :].astype(f32) + (r.out_part[rows, :] + r.out_other[rows, :])
        r.hidden[rows, :] = hidden
        r.mid_low[rows, :] = (hidden * inverse_rms(hidden) * gain_mid[...]).astype(bf16)

    loop(8, norm_mid)
    mid_low, mixed, d_gate, d_up = r.mid_low, r.mixed, r.d_gate, r.d_up

    def feed(t):
        gate = dot(mid_low[...], weight["g"][t].reshape(1024, 512))
        up = dot(mid_low[...], weight["u"][t].reshape(1024, 512))
        d_mixed = dot_nt(cot[...], weight["d"][t].reshape(512, 1024))
        sig = jax.nn.sigmoid(gate)
        act = gate * sig
        mixed[...] = (act * up).astype(bf16)
        d_gate[...] = (d_mixed * up * sig * (1.0 + gate * (1.0 - sig))).astype(bf16)
        d_up[...] = (d_mixed * act).astype(bf16)

        def mid_back(i):
            y_pair, lanes = pl.ds(2 * i, 2), lanes_at(i * 512, 512)
            got = dot_nt(d_gate[...], weight["g"][t, y_pair].reshape(512, 512))
            got += dot_nt(d_up[...], weight["u"][t, y_pair].reshape(512, 512))
            r.mid_part[:, lanes] = got if t == 0 else r.mid_part[:, lanes] + got

        def project_down(i):
            lanes = lanes_at(i * 512, 512)
            got = dot(mixed[...], weight["d"][t, ..., lanes].reshape(512, 512))
            r.down_part[:, lanes] = got if t == 0 else r.down_part[:, lanes] + got

        loop(2, mid_back)
        if t == 2:
            pairs[MID_PAIR] = to_sibling(MID_PAIR, r.mid_part, r.mid_other)
        loop(2, project_down)

    def grads(t):
        def grad_down(i):
            got = dot_tn(mixed[:, lanes_at(i * 256, 256)], cot[...]).astype(bf16)
            weight["d"][t, pl.ds(2 * i, 2)] = got.reshape(2, 4, 4, 8, 1024)

        def grad_columns(name, right):
            def rows(i):
                left = mid_low[:, lanes_at(i * 512, 512)]
                weight[name][t, pl.ds(2 * i, 2)] = dot_tn(left, right[...]).astype(bf16).reshape(2, 2, 4, 4, 8, 512)

            return rows

        loop(2, grad_down)
        sum_start(("d", t), 0)
        loop(2, grad_columns("g", d_gate))
        sum_start(("g", t), 0)
        loop(2, grad_columns("u", d_up))
        sum_start(("u", t), 0)

    def sends_done(item, phases):
        for phase in phases:
            wait_for(0, item, phase, 0, 3)

    for name in MLP:
        gather_finish((name, 0), 2)
    feed(0)
    for name in MLP:
        gather_forward((name, 2), 2)
    for name in MLP:
        sends_done((name, None), (0, 1))
        sends_done((name, 0), (2,))
    grads(0)
    for name in MLP:
        gather_finish((name, 1), 2)
    feed(1)
    for name in MLP:
        sends_done((name, 1), (2,))
    grads(1)
    for name in MLP:
        gather_finish((name, 2), 2)
    feed(2)
    for name in MLP:
        sends_done((name, 2), (2,))
    grads(2)
    down_copy = to_sibling(DOWN_PAIR, r.down_part.at[other_rows], r.down_other)
    for name in MLP:
        sum_middle((name, 0), 0)
    pairs[MID_PAIR].wait()

    r.gain_sums[...] = jnp.zeros((8, 1024), f32)
    r.head_sums[...] = jnp.zeros((8, 128), f32)

    def res_back(i):
        rows = rows_of(i)
        hidden = r.hidden[rows, :]
        inverse = inverse_rms(hidden)
        unit = hidden * inverse
        part = r.mid_part[rows, :]
        r.gain_sums[1:2, :] += jnp.sum(part * unit, axis=0, keepdims=True)
        d_mid = part + r.mid_other[rows, :]
        d_res = cot[rows, :].astype(f32) + norm_backward(d_mid, unit, inverse, gain_mid[...])
        r.d_res[rows, :] = d_res
        r.d_res_low[rows, :] = d_res.astype(bf16)

    loop(8, res_back)
    d_res_low = r.d_res_low

    def attn_back(i):
        two = weight["o"][pl.ds(2 * i, 2)].reshape(512, 1024)
        r.d_attn[:, lanes_at(i * 512, 512)] = dot_nt(d_res_low[...], two).astype(bf16)

    loop(2, attn_back)
    for name in ATTN + ("e",):
        sends_done((name, None), (0, 1, 2))

    def grad_of(name, left, right):
        def rows(i):
            got = dot_tn(left[:, lanes_at(i * 512, 512)], right[...]).astype(bf16)
            weight[name][pl.ds(2 * i, 2)] = got.reshape((2,) + SHAPES[name][1:])

        loop(2, rows)

    grad_of("o", attended, d_res_low)
    for name in MLP:
        sum_middle((name, 1), 0)

    def head_back(grad, raw, gain):
        inverse = inverse_rms(raw)
        unit = raw * inverse
        return jnp.sum(grad * unit, axis=0, keepdims=True), norm_backward(grad, unit, inverse, gain[...])

    def attend_back(i):
        b, m = i // 4, lax.rem(i, 4)
        rows = pl.ds(pl.multiple_of(b * 128, 128), 128)
        lanes = lanes_at(m * 128, 128)
        d_att = both_heads(r.d_attn, rows, m)
        query, key = both_heads(r.q_rot, rows, m), r.k_rot[rows, lanes]
        probs = r.probs[i]
        d_probs = dot_nt(d_att, r.values[rows, lanes])
        r.d_b[rows, lanes_at(512 + m * 128, 128)] = dot_tn(probs.astype(bf16), d_att).astype(bf16)
        d_scores = (probs * (d_probs - jnp.sum(d_probs * probs, axis=-1, keepdims=True))).astype(bf16)
        d_query = dot(d_scores, key) * SCALE
        d_key = dot_tn(d_scores, query) * SCALE
        cos_part, sin_part = r.cos[rows, :], -r.sin[rows, :]
        for j in range(2):
            spots = lanes_at(m * 256 + 128 * j, 128)
            d_unit = rotate(d_query[128 * j : 128 * j + 128], cos_part, sin_part)
            total, d_raw = head_back(d_unit, r.q_raw[rows, spots], gain_query)
            r.head_sums[2:3, :] += total
            r.d_q[rows, spots] = d_raw.astype(bf16)
        total, d_raw = head_back(rotate(d_key, cos_part, sin_part), r.k_raw[rows, lanes], gain_key)
        r.head_sums[3:4, :] += total
        r.d_b[rows, lanes] = d_raw.astype(bf16)

    loop(8, attend_back)
    for name in MLP:
        sum_middle((name, 2), 0)
    sum_start(("o", None), 0)

    def in_back(i):
        y_pair = pl.ds(2 * i, 2)
        got = dot_nt(r.d_q[...], weight["q"][y_pair].reshape(512, 1024))
        got += dot_nt(r.d_b[...], weight["b"][y_pair].reshape(512, 1024))
        r.in_part[:, lanes_at(i * 512, 512)] = got

    loop(2, in_back)
    in_copy = to_sibling(IN_PAIR, r.in_part.at[other_rows], r.in_other)
    grad_of("q", normed, r.d_q)
    sum_start(("q", None), 0)
    grad_of("b", normed, r.d_b)
    sum_start(("b", None), 0)

    def gain_back(i):
        x = r.x[rows_of(i), :].astype(f32)
        unit = x * inverse_rms(x)
        r.gain_sums[0:1, :] += jnp.sum(r.in_part[rows_of(i), :] * unit, axis=0, keepdims=True)

    loop(8, gain_back)
    table = dot_tn(r.head_sums[...].astype(bf16), pick)
    for i in range(2):
        table += dot(jnp.where(owned, r.gain_sums[i : i + 1, :], 0.0).astype(bf16), r.eighths[i])
    weight["e"][...] = table.reshape(SHAPES["e"])
    sum_start(("e", None), 0)

    down_copy.wait()

    def finish_out(i):
        rows = rows_of(i)
        mine = pl.ds(pl.multiple_of(me * 128 + i * 32, 32), 32)
        down = r.down_part[mine, :] + r.down_other[rows, :]
        layer_out[rows, :] = (r.hidden[mine, :] + down).astype(bf16)

    loop(4, finish_out)
    for t in range(3):
        for name in MLP:
            sum_end((name, t), 0)
    in_copy.wait()

    def finish_in(i):
        rows = rows_of(i)
        mine = pl.ds(pl.multiple_of(me * 128 + i * 32, 32), 32)
        d_normed = r.in_part[mine, :] + r.in_other[rows, :]
        x = r.x[mine, :].astype(f32)
        inverse = inverse_rms(x)
        input_grad[rows, :] = r.d_res[mine, :] + norm_backward(d_normed, x * inverse, inverse, gain_in[...])

    loop(4, finish_in)

    for name in ATTN:
        sum_middle((name, None), 0)
    for name in MLP:
        sum_start((name, None), 1)
    sum_end(("e", None), 0)
    sum_start(("e", None), 1)
    for name in ATTN:
        sum_end((name, None), 0)
        sum_start((name, None), 1)
    for name in MLP:
        sum_middle((name, None), 1)
    sum_end(("e", None), 1)
    sum_start(("e", None), 2)
    for name in ATTN:
        sum_middle((name, None), 1)
    for name in MLP:
        sum_end((name, None), 1)
        sum_start((name, None), 2)
    for name in ATTN:
        sum_end((name, None), 1)
        sum_start((name, None), 2)
    sum_end(("e", None), 2)
    swap = to_sibling(FIN_PAIR + SPLIT.index("e"), fin["e"].at[1 - me], rx["e"])
    for name in MLP:
        sum_end((name, None), 2)
    rest = r.blocks[...]
    total = jnp.zeros((128, 384), f32)
    for _ in range(3):
        head = rest.astype(bf16)
        total += dot_nt(head, r.perm[...])
        rest = rest - head.astype(f32)
    for i, out in ((0, 6), (1, 7)):
        for b in range(8):
            out_buf[out][:, 384 * b : 384 * b + 384] = total[64 * i + 8 * b : 64 * i + 8 * b + 8, :]
    swap.wait()
    row = fin["e"][me] + rx["e"][...]
    for ref, first, count in zip(out_buf[9:], (0, 8, 16, 17), (8, 8, 1, 1)):
        ref[...] = row[0, first : first + count]
    for name in ATTN:
        sum_end((name, None), 2)
    for item, phase in SUMS:
        wait_for(1, item, phase, 0, 3)


def finish_kernel(*refs):
    n = len(OUTS)
    ins, outs, sems = refs[:n], refs[n : 2 * n], refs[-1]
    copies = [pltpu.make_async_copy(ins[i], outs[i], sems.at[i]) for i in range(n)]
    for copy in copies:
        copy.start()
    for copy in copies:
        copy.wait()


def body(*args):
    hbm = pl.BlockSpec(memory_space=pl.ANY)
    vmem = pl.BlockSpec(memory_space=pltpu.VMEM)
    parts = pl.pallas_call(
        layer_kernel,
        out_shape=[pltpu.VMEM(*entry) for entry in OUTS],
        in_specs=[hbm] * 14,
        out_specs=[vmem] * len(OUTS),
        scratch_shapes=[pltpu.VMEM(*entry) for group in GROUPS for entry in group.values()]
        + [pltpu.SMEM((size,), f32) for size in (8, 8, 1, 1)]
        + [pltpu.SemaphoreType.DMA((len(SEMS),))]
        + [pltpu.SemaphoreType.DMA((PAIRS,))] * 2
        + [pltpu.SemaphoreType.DMA((14,))],
        compiler_params=pltpu.CompilerParams(
            collective_id=1, has_side_effects=True, vmem_limit_bytes=57 << 20
        ),
        name="layer",
    )(*args)
    parts = [pltpu.with_memory_space_constraint(part, pltpu.VMEM) for part in parts]
    (
        layer_out, input_grad, grad_q, grad_k, grad_v, grad_o, grad_g, grad_u, grad_d, norm_gain, mlp_gain, query_gain, key_gain,
    ) = pl.pallas_call(
        finish_kernel,
        out_shape=[jax.ShapeDtypeStruct(*entry) for entry in OUTS],
        in_specs=[vmem] * len(OUTS),
        out_specs=[hbm] * len(OUTS),
        scratch_shapes=[pltpu.SemaphoreType.DMA((len(OUTS),))],
        name="finish",
    )(*parts)
    return (
        layer_out, input_grad, norm_gain, grad_q, grad_k, grad_v, query_gain, key_gain, grad_o, mlp_gain, grad_g, grad_u, grad_d,
    )


def solution(mesh):
    rows = P(("dp", "fsdp"), None)
    flat = P(("dp", "fsdp"))
    return jax.shard_map(
        body,
        mesh=mesh,
        in_specs=(rows, rows, flat, rows, rows, rows, flat, flat, rows, flat, rows, rows, rows, rows),
        out_specs=(rows, rows, flat, rows, rows, rows, flat, flat, rows, flat, rows, rows, rows),
        check_vma=False,
    )
```
